512 devices in a mesh: dp: 64 (over x, z_hi, y, core), expert: 8 (over z_lo).
Axes of the slice: x: 4, y: 4, z: 16 (z_hi: 2, z_lo: 8; z = z_hi * 8 + z_lo), core: 2. Of those that a mesh axis runs over, the one named last changes fastest.
Arguments:
- tokens_in: bfloat16 [131072, 2560], P(('dp', 'expert')), may hold values from -6 to 6
- cotangent: bfloat16 [131072, 2560], P(('dp', 'expert')), may hold values from -0.29882812 to 0.29882812
- routes: int32 [131072, 6], P(('dp', 'expert')), may hold values from 0 to 159, as said below
- gate_weights: bfloat16 [131072, 6], P(('dp', 'expert')), may hold values from 0.5 to 8
- gate_proj: bfloat16 [8, 2560, 768], P('expert', 'dp'), may hold values from -0.125 to 0.125
- up_proj: bfloat16 [8, 2560, 768], P('expert', 'dp'), may hold values from -0.125 to 0.125
- down_proj: bfloat16 [8, 2560, 768], P('expert', 'dp'), may hold values from -0.21875 to 0.21875
Outputs:
- grad_tokens: bfloat16 [131072, 2560], P(('dp', 'expert'))
- grad_gates: bfloat16 [131072, 6], P(('dp', 'expert'))
The draws below stay inside these ranges and needn't reach their ends.
Inputs may be any that keep to these rules, and one draw needn't show every extreme that they name: `routes`: each row holds 6 different expert numbers, at most one of them below 8. Within the 256 rows of one device no number below 8 is named by more than 32 rows, and in every draw, for each group of devices along expert, some number below 8 is named by exactly 32 rows on every device of that group.
All inputs are finite; a program needn't handle non-finite values.
Results may differ from the reference program's by a relative error of at most 0.024.
Values may be sent and summed in bfloat16 or wider, within the bound.
No kernel may reach another device: no remote copies, remote signals or barrier semaphores. Data moves between devices by JAX's collectives and lax.ppermute only.
A program may use at most 64 MiB of HBM per device.

```python
import math
import jax
import jax.numpy as jnp
from jax import lax

D = 2560
H = 768
ALL_EXPERTS = 160
TOP = 6
TOK_DEV = 256
CAP = 32
EXPERTS = 8
TOKENS = 131072


def draw_routes(key, part):
    key = jax.random.fold_in(key, 7)
    keys = jax.random.split(key, 5)
    block_count = TOKENS // TOK_DEV
    counts = jax.random.randint(keys[0], (block_count, EXPERTS), 1, CAP + 1)
    hottest = jax.random.randint(keys[1], (block_count // EXPERTS,), 0, EXPERTS)
    hot_block = jnp.repeat(hottest, EXPERTS)
    column = jnp.arange(EXPERTS)[None, :]
    counts = jnp.where(column == hot_block[:, None], CAP, counts)
    ends = jnp.cumsum(counts, axis=1)
    position = jax.vmap(lambda sub: jax.random.permutation(sub, TOK_DEV))(jax.random.split(keys[2], block_count))
    inside = position < ends[:, -1:]
    owner_id = jnp.sum((position[:, :, None] >= ends[:, None, :]).astype(jnp.int32), axis=2)
    others = ALL_EXPERTS - EXPERTS
    base = jax.random.randint(keys[3], (block_count, TOK_DEV, 1), 0, others)
    chosen = EXPERTS + (base + jnp.arange(TOP)[None, None, :]) % others
    place = jax.random.randint(keys[4], (block_count, TOK_DEV, 1), 0, TOP)
    picked = inside[:, :, None] & (jnp.arange(TOP)[None, None, :] == place)
    numbers = jnp.where(picked, owner_id[:, :, None], chosen)
    return numbers.reshape(TOKENS, TOP).astype(jnp.int32)


def block_scale(stream_key, shape, shards, least, top_value):
    def one(axis_at, blocks):
        draws = jax.random.uniform(jax.random.fold_in(jax.random.fold_in(stream_key, 6), axis_at), (blocks,), jnp.float32, least / len(shards), top_value / len(shards))
        return jnp.repeat(jnp.exp(draws), shape[axis_at] // blocks).reshape((-1,) + (1,) * (len(shape) - axis_at - 1))

    gain = one(*shards[0])
    for cut in shards[1:]:
        gain = gain * one(*cut)
    return gain


def normal_values(stream_key, shape, scale, bound, pieces=(), kind=jnp.bfloat16):
    loudness = block_scale(stream_key, shape, pieces, -0.22, 0.18) if pieces else 1.0
    result = jax.random.normal(stream_key, shape, jnp.float32) * scale * loudness
    return jnp.minimum(jnp.maximum(result, -bound), bound).astype(kind)


def setup_inputs(seed: int = 0) -> dict:
    splits = jax.random.split(jax.random.key(seed), 8)
    tokens_in = normal_values(splits[0], (TOKENS, D), 1.0, 6.0, ((0, 512),))
    cotangent = normal_values(splits[1], (TOKENS, D), 0.05, 0.29882812, ((0, 512),))
    routes = draw_routes(jax.random.fold_in(splits[7], 71), 0)
    gate_weights = jnp.clip(jnp.exp(math.log(8.0) - 2.7725887 * jax.random.uniform(splits[3], (TOKENS, TOP), jnp.float32) ** block_scale(splits[3], (TOKENS, TOP), ((0, 512),), -0.2, 0.2)), 0.5, 8.0).astype(jnp.bfloat16)
    gate_proj = normal_values(splits[4], (EXPERTS, D, H), D ** -0.5, 0.125, ((0, 8), (1, 64)))
    up_proj = normal_values(splits[5], (EXPERTS, D, H), D ** -0.5, 0.125, ((0, 8), (1, 64)))
    down_proj = normal_values(splits[6], (EXPERTS, D, H), H ** -0.5, 0.21875, ((0, 8), (1, 64)))
    return dict(tokens_in=tokens_in, cotangent=cotangent, routes=routes, gate_weights=gate_weights, gate_proj=gate_proj, up_proj=up_proj, down_proj=down_proj)


def expert_rows(row_block, cotangent_rows, gate_column, gate_full, up_full, down_full):
    pre_gate = jnp.dot(row_block, gate_full, preferred_element_type=jnp.float32)
    pre_up = jnp.dot(row_block, up_full, preferred_element_type=jnp.float32)
    sigmoid_gate = jax.nn.sigmoid(pre_gate)
    activation = pre_gate * sigmoid_gate
    hidden = (activation * pre_up).astype(jnp.bfloat16)
    expert_out = jnp.dot(hidden, down_full.T, preferred_element_type=jnp.float32)
    score_rows = jnp.sum(cotangent_rows.astype(jnp.float32) * expert_out, axis=1).astype(jnp.bfloat16)
    back_hidden = jnp.dot(cotangent_rows, down_full, preferred_element_type=jnp.float32)
    scaled = gate_column.astype(jnp.float32)[:, None] * back_hidden
    silu_slope = sigmoid_gate * (1.0 + pre_gate * (1.0 - sigmoid_gate))
    grad_gate_pre = (scaled * pre_up * silu_slope).astype(jnp.bfloat16)
    grad_up_pre = (scaled * activation).astype(jnp.bfloat16)
    grad_rows = jnp.dot(grad_gate_pre, gate_full.T, preferred_element_type=jnp.float32)
    grad_rows = grad_rows + jnp.dot(grad_up_pre, up_full.T, preferred_element_type=jnp.float32)
    return grad_rows.astype(jnp.bfloat16), score_rows


def reference(tokens_in, cotangent, routes, gate_weights, gate_proj, up_proj, down_proj):
    experts = gate_proj.shape[0]
    total_rows = tokens_in.shape[0]
    width = tokens_in.shape[1]
    block_count = total_rows // TOK_DEV
    window = routes < experts
    owner_id = jnp.sum(jnp.where(window, routes, 0), axis=1).astype(jnp.int32)
    routed = jnp.any(window, axis=1)
    onehot = ((owner_id[:, None] == jnp.arange(experts, dtype=jnp.int32)[None, :]) & routed[:, None]).astype(jnp.int32)
    slot_rank = jnp.cumsum(onehot.reshape(block_count, TOK_DEV, experts), axis=1).reshape(total_rows, experts) - 1
    token_slot = jnp.sum(slot_rank * onehot, axis=1).astype(jnp.int32)
    block_id = (jnp.arange(total_rows, dtype=jnp.int32) // TOK_DEV).astype(jnp.int32)
    place_rows = (block_id * CAP + token_slot).astype(jnp.int32)
    token_gate = jnp.sum(jnp.where(window, gate_weights.astype(jnp.float32), 0.0), axis=1).astype(jnp.bfloat16)
    slot_total = block_count * CAP

    def one_expert(inputs):
        number, gate_full, up_full, down_full = inputs
        target = jnp.where(routed & (owner_id == number), place_rows, slot_total).astype(jnp.int32)
        row_block = jnp.zeros((slot_total, width), jnp.bfloat16).at[target].set(tokens_in, mode="drop")
        cotangent_rows = jnp.zeros((slot_total, width), jnp.bfloat16).at[target].set(cotangent, mode="drop")
        gate_column = jnp.zeros((slot_total,), jnp.bfloat16).at[target].set(token_gate, mode="drop")
        return expert_rows(row_block, cotangent_rows, gate_column, gate_full, up_full, down_full)

    grad_all, score_all = lax.map(one_expert, (jnp.arange(experts, dtype=jnp.int32), gate_proj, up_proj, down_proj))
    flat_index = jnp.where(routed, owner_id * slot_total + place_rows, 0).astype(jnp.int32)
    grad_tokens = jnp.where(routed[:, None], grad_all.reshape(experts * slot_total, width)[flat_index], jnp.zeros((), jnp.bfloat16))
    token_score = score_all.reshape(experts * slot_total)[flat_index]
    grad_gates = jnp.where(window, token_score[:, None], jnp.zeros((), jnp.bfloat16)).astype(jnp.bfloat16)
    return grad_tokens.astype(jnp.bfloat16), grad_gates
```

```python
import jax
import jax.numpy as jnp
from jax import lax
from jax.experimental import pallas as pl
from jax.experimental.pallas import tpu as pltpu
from jax.sharding import Mesh, PartitionSpec as P

BF = jnp.bfloat16
F32 = jnp.float32
AXES = ("x", "zh", "y", "c", "zq", "zr")
SPLIT = 128
PAD = 128


def route_place(routes, slots):
    tokens = routes.shape[0]
    window = routes < 8
    owner = jnp.sum(jnp.where(window, routes, 0), axis=1, keepdims=True)
    routed = jnp.sum(jnp.where(window, 1, 0), axis=1, keepdims=True) > 0
    lane = lax.broadcasted_iota(jnp.int32, (tokens, 128), 1)
    onehot = jnp.where((lane == owner) & routed, 1.0, 0.0)
    row = lax.broadcasted_iota(jnp.int32, (tokens, tokens), 0)
    col = lax.broadcasted_iota(jnp.int32, (tokens, tokens), 1)
    lower = jnp.where(col <= row, 1.0, 0.0).astype(BF)
    rank = jnp.dot(lower, onehot.astype(BF), preferred_element_type=F32)
    slot = jnp.sum(rank * onehot, axis=1, keepdims=True).astype(jnp.int32) - 1
    return jnp.where(routed, owner * slots + slot, -1)


def dispatch_kernel(routes_ref, tok_ref, cot_ref, out_ref, sel_ref):
    tokens, width = tok_ref.shape
    place = route_place(routes_ref[...], 32)
    lane = lax.broadcasted_iota(jnp.int32, (tokens, 256), 1)
    sel = jnp.where(lane == place, 1.0, 0.0).astype(BF)
    sel_ref[...] = sel
    step = 512

    @pl.loop(0, width // step)
    def _(i):
        cols = pl.ds(pl.multiple_of(i * step, step), step)
        for source, first in ((tok_ref, 0), (cot_ref, 32)):
            rows = lax.dot_general(
                sel, source[:, cols], (((0,), (0,)), ((), ())), preferred_element_type=F32
            ).astype(BF)
            out_ref[:, first : first + 32, cols] = rows.reshape(8, 32, step)


def combine_kernel(routes_ref, gates_ref, sel_ref, back_ref, grad_ref, score_ref):
    width = grad_ref.shape[1]
    window = routes_ref[...] < 8
    gate = jnp.sum(jnp.where(window, gates_ref[...].astype(F32), 0.0), axis=1, keepdims=True)
    sel = sel_ref[...]
    step = 512

    @pl.loop(0, width // step)
    def _(i):
        cols = pl.ds(pl.multiple_of(i * step, step), step)
        rows = back_ref[:, :, cols].reshape(256, step)
        grad_ref[:, cols] = (jnp.dot(sel, rows, preferred_element_type=F32) * gate).astype(BF)

    tail = back_ref[:, :, width : width + PAD].reshape(256, PAD)
    score = jnp.dot(sel, tail, preferred_element_type=F32)[:, 0:1]
    score_ref[...] = jnp.where(window, score, 0.0).astype(BF)


def expert_kernel(where_ref, rows_ref, *refs):
    pieces = refs[:10]
    out_ref = refs[10]
    gate_w, up_w, down_w, grad_a, grad_b, pre_g, pre_u, sems = refs[11:]
    weights = (gate_w, up_w, down_w)
    my_x, my_y = where_ref[0], where_ref[1]

    copies = ([], [], [])

    def place(src, src_row, block, half, xx, yy):
        target = ((xx * 2 + block) * 4 + yy) * 80
        for m in range(3):
            lo, hi = max(80 * m, half[0]), min(80 * m + 80, half[1])
            if lo < hi:
                copies[m].append(
                    pltpu.make_async_copy(
                        src.at[pl.ds(src_row + lo - half[0], hi - lo), :],
                        weights[m].at[pl.ds(pl.multiple_of(target + lo - 80 * m, 16), hi - lo), :],
                        sems.at[m],
                    )
                )

    whole = (0, 240)
    offs = (0, 3, 1, 2)
    for block in range(2):
        own, low, high, opp0, opp1 = pieces[5 * block : 5 * block + 5]
        for outer, (src, first, inner) in enumerate(
            ((own, 0, (0, 1, 2, 3)), (low, 0, (0, 1, 2, 3)), (high, 0, (0, 1, 2, 3)),
             (opp0, 0, (0, 1)), (opp1, 2, (2, 3)))
        ):
            far = offs[min(outer, 3)]
            for k in inner:
                near = offs[k]
                if block == 0:
                    xx, yy = lax.rem(my_x + far, 4), lax.rem(my_y + near, 4)
                else:
                    xx, yy = lax.rem(my_x + near, 4), lax.rem(my_y + far, 4)
                place(src, (k - first) * 240, block, whole, xx, yy)
    for m in range(3):
        for copy in copies[m]:
            copy.start()

    width = gate_w.shape[0]
    hidden_width = gate_w.shape[1]
    cstep = 256

    for copy in copies[0]:
        copy.wait()

    tok = rows_ref[:, 0:32, :].reshape(256, width)

    @pl.loop(0, hidden_width // cstep)
    def _(i):
        cols = pl.ds(pl.multiple_of(i * cstep, cstep), cstep)
        pre_g[:, cols] = jnp.dot(tok, gate_w[:, cols], preferred_element_type=F32)

    for copy in copies[1]:
        copy.wait()

    @pl.loop(0, hidden_width // cstep)
    def _(i):
        cols = pl.ds(pl.multiple_of(i * cstep, cstep), cstep)
        pre_u[:, cols] = jnp.dot(tok, up_w[:, cols], preferred_element_type=F32)

    for copy in copies[2]:
        copy.wait()

    cot = rows_ref[:, 32:64, :].reshape(256, width)

    def back(i, score):
        cols = pl.ds(pl.multiple_of(i * cstep, cstep), cstep)
        back_hidden = jnp.dot(cot, down_w[:, cols], preferred_element_type=F32)
        gate, up = pre_g[:, cols], pre_u[:, cols]
        sig = jax.nn.sigmoid(gate)
        act = gate * sig
        hidden = (act * up).astype(BF).astype(F32)
        grad_a[:, cols] = (back_hidden * up * (sig * (1.0 + gate * (1.0 - sig)))).astype(BF)
        grad_b[:, cols] = (back_hidden * act).astype(BF)
        return score + jnp.sum(hidden * back_hidden, axis=1, keepdims=True)

    score = lax.fori_loop(0, hidden_width // cstep, back, jnp.zeros((256, 1), F32))
    out_ref[:, :, width : width + PAD] = (
        jnp.broadcast_to(score, (256, PAD)).astype(BF).reshape(8, 32, PAD)
    )

    a, b = grad_a[...], grad_b[...]
    dims = (((1,), (1,)), ((), ()))
    dstep = 256

    @pl.loop(0, width // dstep)
    def _(i):
        part = pl.ds(pl.multiple_of(i * dstep, dstep), dstep)
        rows = lax.dot_general(a, gate_w[part, :], dims, preferred_element_type=F32)
        rows = rows + lax.dot_general(b, up_w[part, :], dims, preferred_element_type=F32)
        out_ref[:, :, part] = rows.astype(BF).reshape(8, 32, dstep)


def params():
    return pltpu.CompilerParams(vmem_limit_bytes=48 * 1024 * 1024)


def cost(flops, moved):
    return pl.CostEstimate(flops=flops, bytes_accessed=moved, transcendentals=0)


VM = pl.BlockSpec(memory_space=pltpu.VMEM)
ANY = pl.BlockSpec(memory_space=pl.ANY)


def shift(v, axis, by):
    return lax.ppermute(v, axis, [(i, (i + by) % 4) for i in range(4)])


def ring_first(v, axis):
    return shift(v, axis, 1), shift(v, axis, -1)


def ring_second(low, high, axis, cut):
    return shift(low[:cut], axis, 1), shift(high[cut:], axis, -1)


def on_device(tokens_in, cotangent, routes, gate_weights, gate_proj, up_proj, down_proj):
    width = tokens_in.shape[1]
    hidden_width = gate_proj.shape[2]
    ix, iy, ic = lax.axis_index("x"), lax.axis_index("y"), lax.axis_index("c")
    zh, zq = lax.axis_index("zh"), lax.axis_index("zq")
    ring = zh * 2 + zq

    shard = jnp.concatenate([gate_proj, up_proj, down_proj], axis=0)
    other = lax.ppermute(shard, ("c", "zq"), [(2, 0), (1, 3)])
    pair = jnp.stack([jnp.where(ic == 0, shard, other), jnp.where(ic == 0, other, shard)], axis=1)
    pair = pair.reshape(240, hidden_width)

    def at(c, p):
        return (p // 2 * 2 + c) * 2 + p % 2

    def zmove(v, source, by):
        pairs = [(at(c, p), at(c, (p + by) % 4)) for c in range(2) for p in range(4) if (p % 2 == c) == source]
        return lax.ppermute(v, ("zh", "c", "zq"), pairs)

    low, high = zmove(pair, True, 1), zmove(pair, True, -1)
    far0, far1 = zmove(low[:SPLIT], False, 1), zmove(high[SPLIT:], False, -1)
    far = jnp.concatenate([far0, far1], axis=0)
    source = ic == zq
    swapped = (ring == 0) | (ring == 3)
    block_a = jnp.where(source, jnp.where(zh == 0, pair, far), jnp.where(swapped, high, low))
    block_b = jnp.where(source, jnp.where(zh == 0, far, pair), jnp.where(swapped, low, high))

    payload, sel = pl.pallas_call(
        dispatch_kernel,
        out_shape=(
            jax.ShapeDtypeStruct((8, 64, width), BF),
            jax.ShapeDtypeStruct((256, 256), BF),
        ),
        in_specs=[VM] * 3,
        out_specs=(VM, VM),
        compiler_params=params(),
        cost_estimate=cost(2 * 256 * 512 * width, 8 * 256 * width),
    )(routes, tokens_in, cotangent)

    payload, block_a, block_b = lax.optimization_barrier((payload, block_a, block_b))
    rows = lax.all_to_all(payload, ("c", "zr"), split_axis=0, concat_axis=0, tiled=True)

    a_low, a_high = ring_first(block_a, "y")
    b_low, b_high = ring_first(block_b, "x")
    a_far = ring_second(a_low, a_high, "y", SPLIT)
    b_far = ring_second(b_low, b_high, "x", SPLIT)
    line_a = jnp.concatenate([block_a, a_low, a_high, *a_far], axis=0)
    line_b = jnp.concatenate([block_b, b_low, b_high, *b_far], axis=0)
    al, ah = ring_first(line_a, "x")
    bl, bh = ring_first(line_b, "y")
    af = ring_second(al, ah, "x", 480)
    bf = ring_second(bl, bh, "y", 480)

    back = pl.pallas_call(
        expert_kernel,
        out_shape=jax.ShapeDtypeStruct((8, 32, width + PAD), BF),
        in_specs=[pl.BlockSpec(memory_space=pltpu.SMEM), VM] + [ANY] * 10,
        out_specs=VM,
        scratch_shapes=[pltpu.VMEM((width, hidden_width), BF)] * 3
        + [pltpu.VMEM((256, hidden_width), BF)] * 2
        + [pltpu.VMEM((256, hidden_width), F32)] * 2
        + [pltpu.SemaphoreType.DMA((3,))],
        compiler_params=params(),
        cost_estimate=cost(10 * 256 * width * hidden_width, 6 * width * hidden_width),
    )(jnp.stack([ix, iy]).astype(jnp.int32), rows, line_a, al, ah, *af, line_b, bl, bh, *bf)

    home = lax.all_to_all(back, ("c", "zr"), split_axis=0, concat_axis=0, tiled=True)

    return pl.pallas_call(
        combine_kernel,
        out_shape=(
            jax.ShapeDtypeStruct(tokens_in.shape, BF),
            jax.ShapeDtypeStruct(gate_weights.shape, BF),
        ),
        in_specs=[VM] * 4,
        out_specs=(VM, VM),
        compiler_params=params(),
        cost_estimate=cost(2 * 256 * 256 * width, 4 * 256 * width),
    )(routes, gate_weights, sel, home)


def solution(mesh):
    fine = Mesh(mesh.devices.reshape(4, 2, 4, 2, 2, 4), AXES)
    rows = P(AXES, None)
    proj = P(("zq", "zr"), ("x", "zh", "y", "c"), None)
    return jax.shard_map(
        on_device,
        mesh=fine,
        in_specs=(rows, rows, rows, rows, proj, proj, proj),
        out_specs=(rows, rows),
        check_vma=False,
    )
```

```python
import functools

import jax
import jax.numpy as jnp
from jax import lax
from jax.experimental import pallas as pl
from jax.experimental.pallas import tpu as pltpu
from jax.sharding import Mesh, PartitionSpec as P

BF = jnp.bfloat16
F32 = jnp.float32
AXES = ("x", "zh", "y", "c", "zq", "zr")
SPLIT = 128
PAD = 128


def route_place(routes, slots):
    tokens = routes.shape[0]
    window = routes < 8
    owner = jnp.sum(jnp.where(window, routes, 0), axis=1, keepdims=True)
    routed = jnp.sum(jnp.where(window, 1, 0), axis=1, keepdims=True) > 0
    lane = lax.broadcasted_iota(jnp.int32, (tokens, 128), 1)
    onehot = jnp.where((lane == owner) & routed, 1.0, 0.0)
    row = lax.broadcasted_iota(jnp.int32, (tokens, tokens), 0)
    col = lax.broadcasted_iota(jnp.int32, (tokens, tokens), 1)
    lower = jnp.where(col <= row, 1.0, 0.0).astype(BF)
    rank = jnp.dot(lower, onehot.astype(BF), preferred_element_type=F32)
    slot = jnp.sum(rank * onehot, axis=1, keepdims=True).astype(jnp.int32) - 1
    return jnp.where(routed, owner * slots + slot, -1)


def dispatch_kernel(routes_ref, tok_ref, cot_ref, out_ref, sel_ref):
    tokens, width = tok_ref.shape
    place = route_place(routes_ref[...], 32)
    lane = lax.broadcasted_iota(jnp.int32, (tokens, 256), 1)
    sel = jnp.where(lane == place, 1.0, 0.0).astype(BF)
    sel_ref[...] = sel
    step = 512

    @pl.loop(0, width // step)
    def _(i):
        cols = pl.ds(pl.multiple_of(i * step, step), step)
        for source, first in ((tok_ref, 0), (cot_ref, 32)):
            rows = lax.dot_general(
                sel, source[:, cols], (((0,), (0,)), ((), ())), preferred_element_type=F32
            ).astype(BF)
            out_ref[:, first : first + 32, cols] = rows.reshape(8, 32, step)


def combine_kernel(routes_ref, gates_ref, sel_ref, back_ref, grad_ref, score_ref):
    width = grad_ref.shape[1]
    window = routes_ref[...] < 8
    gate = jnp.sum(jnp.where(window, gates_ref[...].astype(F32), 0.0), axis=1, keepdims=True)
    sel = sel_ref[...]
    step = 512

    @pl.loop(0, width // step)
    def _(i):
        cols = pl.ds(pl.multiple_of(i * step, step), step)
        rows = back_ref[:, :, cols].reshape(256, step)
        grad_ref[:, cols] = (jnp.dot(sel, rows, preferred_element_type=F32) * gate).astype(BF)

    tail = back_ref[:, :, width : width + PAD].reshape(256, PAD)
    score = jnp.dot(sel, tail, preferred_element_type=F32)[:, 0:1]
    score_ref[...] = jnp.where(window, score, 0.0).astype(BF)


def stack_kernel(gate_ref, up_ref, down_ref, out_ref):
    for m, ref in enumerate((gate_ref, up_ref, down_ref)):
        out_ref[m] = ref[0]


def expert_kernel(pieces, where_ref, rows_ref, *refs):
    sources = refs[: len(refs) - 9]
    out_ref = refs[-9]
    gate_w, up_w, down_w, grad_a, grad_b, pre_g, pre_u, sems = refs[-8:]
    weights = (gate_w, up_w, down_w)
    my_x, my_y = where_ref[0], where_ref[1]

    copies = ([], [], [])
    for number, row, block, dx, dy in pieces:
        xx, yy = lax.rem(my_x + dx, 4), lax.rem(my_y + dy, 4)
        target = pl.multiple_of(((xx * 2 + block) * 4 + yy) * 80, 16)
        for m in range(3):
            copies[m].append(
                pltpu.make_async_copy(
                    sources[number].at[pl.ds(row + 80 * m, 80), :],
                    weights[m].at[pl.ds(target, 80), :],
                    sems.at[m],
                )
            )
    for m in range(3):
        for copy in copies[m]:
            copy.start()

    width = gate_w.shape[0]
    hidden_width = gate_w.shape[1]
    cstep = 256

    for copy in copies[0]:
        copy.wait()

    tok = rows_ref[:, 0:32, :].reshape(256, width)

    @pl.loop(0, hidden_width // cstep)
    def _(i):
        cols = pl.ds(pl.multiple_of(i * cstep, cstep), cstep)
        pre_g[:, cols] = jnp.dot(tok, gate_w[:, cols], preferred_element_type=F32)

    for copy in copies[1]:
        copy.wait()

    @pl.loop(0, hidden_width // cstep)
    def _(i):
        cols = pl.ds(pl.multiple_of(i * cstep, cstep), cstep)
        pre_u[:, cols] = jnp.dot(tok, up_w[:, cols], preferred_element_type=F32)

    for copy in copies[2]:
        copy.wait()

    cot = rows_ref[:, 32:64, :].reshape(256, width)

    def back(i, score):
        cols = pl.ds(pl.multiple_of(i * cstep, cstep), cstep)
        back_hidden = jnp.dot(cot, down_w[:, cols], preferred_element_type=F32)
        gate, up = pre_g[:, cols], pre_u[:, cols]
        sig = jax.nn.sigmoid(gate)
        act = gate * sig
        hidden = (act * up).astype(BF).astype(F32)
        grad_a[:, cols] = (back_hidden * up * (sig * (1.0 + gate * (1.0 - sig)))).astype(BF)
        grad_b[:, cols] = (back_hidden * act).astype(BF)
        return score + jnp.sum(hidden * back_hidden, axis=1, keepdims=True)

    score = lax.fori_loop(0, hidden_width // cstep, back, jnp.zeros((256, 1), F32))
    out_ref[:, :, width : width + PAD] = (
        jnp.broadcast_to(score, (256, PAD)).astype(BF).reshape(8, 32, PAD)
    )

    a, b = grad_a[...], grad_b[...]
    dims = (((1,), (1,)), ((), ()))
    dstep = 256

    @pl.loop(0, width // dstep)
    def _(i):
        part = pl.ds(pl.multiple_of(i * dstep, dstep), dstep)
        rows = lax.dot_general(a, gate_w[part, :], dims, preferred_element_type=F32)
        rows = rows + lax.dot_general(b, up_w[part, :], dims, preferred_element_type=F32)
        out_ref[:, :, part] = rows.astype(BF).reshape(8, 32, dstep)


def params(mib=16):
    return pltpu.CompilerParams(vmem_limit_bytes=mib * 1024 * 1024)


def cost(flops, moved):
    return pl.CostEstimate(flops=flops, bytes_accessed=moved, transcendentals=0)


VM = pl.BlockSpec(memory_space=pltpu.VMEM)
ANY = pl.BlockSpec(memory_space=pl.ANY)


def shift(v, axis, by):
    return lax.ppermute(v, axis, [(i, (i + by) % 4) for i in range(4)])


def diagonal(v, by):
    pairs = [(i * 4 + j, (i + by) % 4 * 4 + (j + by) % 4) for i in range(4) for j in range(4)]
    return lax.ppermute(v, ("x", "y"), pairs)


def join_kernel(plan, inputs, *refs):
    sources, targets, sem = refs[:inputs], refs[inputs:-1], refs[-1]
    copies = [
        pltpu.make_async_copy(
            sources[i].at[pl.ds(row, count), :], targets[o].at[pl.ds(at, count), :], sem
        )
        for i, row, count, o, at in plan
    ]
    for copy in copies:
        copy.start()
    for copy in copies:
        copy.wait()


def join(rows, plan, *arrays):
    width = arrays[0].shape[1]
    moved = 4 * sum(rows) * width
    return pl.pallas_call(
        functools.partial(join_kernel, plan, len(arrays)),
        out_shape=[jax.ShapeDtypeStruct((r, width), BF) for r in rows],
        in_specs=[ANY] * len(arrays),
        out_specs=[ANY] * len(rows),
        scratch_shapes=[pltpu.SemaphoreType.DMA],
        compiler_params=params(),
        cost_estimate=cost(0, moved),
    )(*arrays)


def torus_gather(own):
    full = own.shape[0]
    half = full // 2
    y0, y1 = shift(own, "y", 1), shift(own, "y", -1)
    x0, x1 = shift(own, "x", 1), shift(own, "x", -1)
    ya, yb, xa, xb = join(
        [full + half] * 4,
        (
            (2, 0, full, 0, 0), (0, 0, half, 0, full),
            (3, 0, full, 1, 0), (1, half, half, 1, full),
            (1, 0, full, 2, 0), (2, 0, half, 2, full),
            (0, 0, full, 3, 0), (3, half, half, 3, full),
        ),
        y0, y1, x0, x1,
    )
    ya, yb = shift(ya, "y", 1), shift(yb, "y", -1)
    xa, xb = shift(xa, "x", 1), shift(xb, "x", -1)
    y_far, x_far, c0, c1 = join(
        [full, full, half, half],
        (
            (0, full, half, 0, 0), (1, full, half, 0, half),
            (2, full, half, 1, 0), (3, full, half, 1, half),
            (0, 0, half, 2, 0), (1, half, half, 3, 0),
        ),
        ya, yb, xa, xb,
    )
    yc, yd = shift(x_far, "y", 1), shift(x_far, "y", -1)
    xc, xd = shift(y_far, "x", 1), shift(y_far, "x", -1)
    c0, c1 = diagonal(c0, 1), diagonal(c1, -1)
    arrays = (own, y0, y1, x0, x1, ya, yb, xa, xb, yc, yd, xc, xd, c0, c1)
    places = (
        (0, 0), (0, 3), (0, 1), (3, 0), (1, 0), (3, 3), (1, 1), (3, 1), (1, 3),
        (2, 3), (2, 1), (3, 2), (1, 2),
    )
    pieces = [(n, h * half, h, dx, dy) for n, (dx, dy) in enumerate(places) for h in range(2)]
    pieces += [(5, full, 0, 0, 2), (6, full, 1, 0, 2)]
    pieces += [(7, full, 0, 2, 0), (8, full, 1, 2, 0)]
    pieces += [(13, 0, 0, 2, 2), (14, 0, 1, 2, 2)]
    return arrays, pieces


def on_device(tokens_in, cotangent, routes, gate_weights, gate_proj, up_proj, down_proj):
    width = tokens_in.shape[1]
    hidden_width = gate_proj.shape[2]
    ix, iy, ic = lax.axis_index("x"), lax.axis_index("y"), lax.axis_index("c")
    zh, zq = lax.axis_index("zh"), lax.axis_index("zq")
    ring = zh * 2 + zq

    shard = pl.pallas_call(
        stack_kernel,
        out_shape=jax.ShapeDtypeStruct((3, *gate_proj.shape[1:]), BF),
        in_specs=[VM] * 3,
        out_specs=VM,
    )(gate_proj, up_proj, down_proj)
    other = lax.ppermute(shard, ("c", "zq"), [(2, 0), (1, 3)])
    pair = jnp.stack([jnp.where(ic == 0, shard, other), jnp.where(ic == 0, other, shard)], axis=1)
    pair = pair.reshape(240, hidden_width)
    top, bottom = pair[:SPLIT], pair[SPLIT:]

    def at(c, p):
        return (p // 2 * 2 + c) * 2 + p % 2

    def zmove(v, source, by):
        pairs = [(at(c, p), at(c, (p + by) % 4)) for c in range(2) for p in range(4) if (p % 2 == c) == source]
        return lax.ppermute(v, ("zh", "c", "zq"), pairs)

    low0, high1 = zmove(top, True, 1), zmove(bottom, True, -1)
    low1, high0 = zmove(bottom, True, 1), zmove(top, True, -1)
    far0, far1 = zmove(low0, False, 1), zmove(high1, False, -1)
    source = ic == zq
    swapped = (ring == 0) | (ring == 3)

    def pick(mine, far, low, high):
        return (
            jnp.where(source, jnp.where(zh == 0, mine, far), jnp.where(swapped, high, low)),
            jnp.where(source, jnp.where(zh == 0, far, mine), jnp.where(swapped, low, high)),
        )

    (a0, b0), (a1, b1) = pick(top, far0, low0, high0), pick(bottom, far1, low1, high1)
    block = jnp.concatenate([a0, a1, b0, b1], axis=0)

    payload, sel = pl.pallas_call(
        dispatch_kernel,
        out_shape=(
            jax.ShapeDtypeStruct((8, 64, width), BF),
            jax.ShapeDtypeStruct((256, 256), BF),
        ),
        in_specs=[VM] * 3,
        out_specs=(VM, VM),
        compiler_params=params(),
        cost_estimate=cost(2 * 256 * 512 * width, 8 * 256 * width),
    )(routes, tokens_in, cotangent)

    payload, block = lax.optimization_barrier((payload, block))
    arrays, pieces = torus_gather(block)
    rows = lax.all_to_all(payload, ("c", "zr"), split_axis=0, concat_axis=0, tiled=True)

    back = pl.pallas_call(
        functools.partial(expert_kernel, pieces),
        out_shape=jax.ShapeDtypeStruct((8, 32, width + PAD), BF),
        in_specs=[pl.BlockSpec(memory_space=pltpu.SMEM), VM] + [ANY] * len(arrays),
        out_specs=VM,
        scratch_shapes=[pltpu.VMEM((width, hidden_width), BF)] * 3
        + [pltpu.VMEM((256, hidden_width), BF)] * 2
        + [pltpu.VMEM((256, hidden_width), F32)] * 2
        + [pltpu.SemaphoreType.DMA((3,))],
        compiler_params=params(56),
        cost_estimate=cost(10 * 256 * width * hidden_width, 6 * width * hidden_width),
    )(jnp.stack([ix, iy]).astype(jnp.int32), rows, *arrays)

    home = lax.all_to_all(back, ("c", "zr"), split_axis=0, concat_axis=0, tiled=True)

    return pl.pallas_call(
        combine_kernel,
        out_shape=(
            jax.ShapeDtypeStruct(tokens_in.shape, BF),
            jax.ShapeDtypeStruct(gate_weights.shape, BF),
        ),
        in_specs=[VM] * 4,
        out_specs=(VM, VM),
        compiler_params=params(),
        cost_estimate=cost(2 * 256 * 256 * width, 4 * 256 * width),
    )(routes, gate_weights, sel, home)


def solution(mesh):
    fine = Mesh(mesh.devices.reshape(4, 2, 4, 2, 2, 4), AXES)
    rows = P(AXES, None)
    proj = P(("zq", "zr"), ("x", "zh", "y", "c"), None)
    return jax.shard_map(
        on_device,
        mesh=fine,
        in_specs=(rows, rows, rows, rows, proj, proj, proj),
        out_specs=(rows, rows),
        check_vma=False,
    )
```

```python
import functools

import jax
import jax.numpy as jnp
from jax import lax
from jax.experimental import pallas as pl
from jax.experimental.pallas import tpu as pltpu
from jax.sharding import Mesh, PartitionSpec as P

BF = jnp.bfloat16
F32 = jnp.float32
AXES = ("x", "zh", "y", "c", "zq", "zr")
SPLIT = 128
PAD = 128


def route_place(routes, slots):
    tokens = routes.shape[0]
    window = routes < 8
    owner = jnp.sum(jnp.where(window, routes, 0), axis=1, keepdims=True)
    routed = jnp.sum(jnp.where(window, 1, 0), axis=1, keepdims=True) > 0
    lane = lax.broadcasted_iota(jnp.int32, (tokens, 128), 1)
    onehot = jnp.where((lane == owner) & routed, 1.0, 0.0)
    row = lax.broadcasted_iota(jnp.int32, (tokens, tokens), 0)
    col = lax.broadcasted_iota(jnp.int32, (tokens, tokens), 1)
    lower = jnp.where(col <= row, 1.0, 0.0).astype(BF)
    rank = jnp.dot(lower, onehot.astype(BF), preferred_element_type=F32)
    slot = jnp.sum(rank * onehot, axis=1, keepdims=True).astype(jnp.int32) - 1
    return jnp.where(routed, owner * slots + slot, -1)


def dispatch_kernel(routes_ref, tok_ref, cot_ref, out_ref, sel_ref):
    tokens, width = tok_ref.shape
    place = route_place(routes_ref[...], 32)
    lane = lax.broadcasted_iota(jnp.int32, (tokens, 256), 1)
    sel = jnp.where(lane == place, 1.0, 0.0).astype(BF)
    sel_ref[...] = sel
    step = 512

    @pl.loop(0, width // step)
    def _(i):
        cols = pl.ds(pl.multiple_of(i * step, step), step)
        for source, first in ((tok_ref, 0), (cot_ref, 32)):
            rows = lax.dot_general(
                sel, source[:, cols], (((0,), (0,)), ((), ())), preferred_element_type=F32
            ).astype(BF)
            out_ref[:, first : first + 32, cols] = rows.reshape(8, 32, step)


def combine_kernel(routes_ref, gates_ref, sel_ref, back_ref, grad_ref, score_ref):
    width = grad_ref.shape[1]
    window = routes_ref[...] < 8
    gate = jnp.sum(jnp.where(window, gates_ref[...].astype(F32), 0.0), axis=1, keepdims=True)
    sel = sel_ref[...]
    step = 512

    @pl.loop(0, width // step)
    def _(i):
        cols = pl.ds(pl.multiple_of(i * step, step), step)
        rows = back_ref[:, :, cols].reshape(256, step)
        grad_ref[:, cols] = (jnp.dot(sel, rows, preferred_element_type=F32) * gate).astype(BF)

    tail = back_ref[:, :, width : width + PAD].reshape(256, PAD)
    score = jnp.dot(sel, tail, preferred_element_type=F32)[:, 0:1]
    score_ref[...] = jnp.where(window, score, 0.0).astype(BF)


def stack_kernel(gate_ref, up_ref, down_ref, out_ref):
    for m, ref in enumerate((gate_ref, up_ref, down_ref)):
        out_ref[m] = ref[0]


def pair_kernel(first_ref, shard_ref, other_ref, top_ref, bottom_ref):
    swap = first_ref[0] == 0
    for m in range(3):
        mine, theirs = shard_ref[m], other_ref[m]
        for k in range(2):
            part = jnp.where(swap == (k == 0), mine, theirs)
            row = 80 * m + 40 * k
            cut = min(max(SPLIT - row, 0), 40)
            if cut:
                top_ref[row : row + cut] = part[:cut]
            if cut < 40:
                bottom_ref[row + cut - SPLIT : row + 40 - SPLIT] = part[cut:]


def block_kernel(state_ref, top, bottom, low0, low1, high0, high1, far0, far1, out_ref):
    source, order = state_ref[0] == 1, state_ref[1] == 0
    row = 0
    for z in range(2):
        for mine, low, high, far in ((top, low0, high0, far0), (bottom, low1, high1, far1)):
            count = mine.shape[0]
            first = jnp.where(source, mine[...], low[...])
            second = jnp.where(source, far[...], high[...])
            pick = order if z == 0 else jnp.logical_not(order)
            out_ref[row : row + count] = jnp.where(pick, first, second)
            row += count


def expert_kernel(pieces, where_ref, rows_ref, *refs):
    sources = refs[: len(refs) - 9]
    out_ref = refs[-9]
    gate_w, up_w, down_w, grad_a, grad_b, pre_g, pre_u, sems = refs[-8:]
    weights = (gate_w, up_w, down_w)
    my_x, my_y, core = where_ref[0], where_ref[1], where_ref[2]

    copies = ([], [], [])
    for number, row, block, far, near in pieces:
        xx = lax.rem(my_x + jnp.where(core == 0, far, near), 4)
        yy = lax.rem(my_y + jnp.where(core == 0, near, far), 4)
        target = pl.multiple_of(((xx * 2 + block) * 4 + yy) * 80, 16)
        for m in range(3):
            copies[m].append(
                pltpu.make_async_copy(
                    sources[number].at[pl.ds(row + 80 * m, 80), :],
                    weights[m].at[pl.ds(target, 80), :],
                    sems.at[m],
                )
            )
    for m in range(3):
        for copy in copies[m]:
            copy.start()

    width = gate_w.shape[0]
    hidden_width = gate_w.shape[1]
    cstep = 256

    for copy in copies[0]:
        copy.wait()

    tok = rows_ref[:, 0:32, :].reshape(256, width)

    @pl.loop(0, hidden_width // cstep)
    def _(i):
        cols = pl.ds(pl.multiple_of(i * cstep, cstep), cstep)
        pre_g[:, cols] = jnp.dot(tok, gate_w[:, cols], preferred_element_type=F32)

    for copy in copies[1]:
        copy.wait()

    @pl.loop(0, hidden_width // cstep)
    def _(i):
        cols = pl.ds(pl.multiple_of(i * cstep, cstep), cstep)
        pre_u[:, cols] = jnp.dot(tok, up_w[:, cols], preferred_element_type=F32)

    for copy in copies[2]:
        copy.wait()

    cot = rows_ref[:, 32:64, :].reshape(256, width)

    def back(i, score):
        cols = pl.ds(pl.multiple_of(i * cstep, cstep), cstep)
        back_hidden = jnp.dot(cot, down_w[:, cols], preferred_element_type=F32)
        gate, up = pre_g[:, cols], pre_u[:, cols]
        sig = jax.nn.sigmoid(gate)
        act = gate * sig
        hidden = (act * up).astype(BF).astype(F32)
        grad_a[:, cols] = (back_hidden * up * (sig * (1.0 + gate * (1.0 - sig)))).astype(BF)
        grad_b[:, cols] = (back_hidden * act).astype(BF)
        return score + jnp.sum(hidden * back_hidden, axis=1, keepdims=True)

    score = lax.fori_loop(0, hidden_width // cstep, back, jnp.zeros((256, 1), F32))
    out_ref[:, :, width : width + PAD] = (
        jnp.broadcast_to(score, (256, PAD)).astype(BF).reshape(8, 32, PAD)
    )

    a, b = grad_a[...], grad_b[...]
    dims = (((1,), (1,)), ((), ()))
    dstep = 256

    @pl.loop(0, width // dstep)
    def _(i):
        part = pl.ds(pl.multiple_of(i * dstep, dstep), dstep)
        rows = lax.dot_general(a, gate_w[part, :], dims, preferred_element_type=F32)
        rows = rows + lax.dot_general(b, up_w[part, :], dims, preferred_element_type=F32)
        out_ref[:, :, part] = rows.astype(BF).reshape(8, 32, dstep)


def params(mib=16):
    return pltpu.CompilerParams(vmem_limit_bytes=mib * 1024 * 1024)


def cost(flops, moved):
    return pl.CostEstimate(flops=flops, bytes_accessed=moved, transcendentals=0)


VM = pl.BlockSpec(memory_space=pltpu.VMEM)
ANY = pl.BlockSpec(memory_space=pl.ANY)


def join_kernel(plan, inputs, *refs):
    sources, targets, sem = refs[:inputs], refs[inputs:-1], refs[-1]
    copies = [
        pltpu.make_async_copy(
            sources[i].at[pl.ds(row, count), :], targets[o].at[pl.ds(at, count), :], sem
        )
        for i, row, count, o, at in plan
    ]
    for copy in copies:
        copy.start()
    for copy in copies:
        copy.wait()


def join(rows, plan, *arrays):
    width = arrays[0].shape[1]
    moved = 4 * sum(rows) * width
    return pl.pallas_call(
        functools.partial(join_kernel, plan, len(arrays)),
        out_shape=[jax.ShapeDtypeStruct((r, width), BF) for r in rows],
        in_specs=[ANY] * len(arrays),
        out_specs=[ANY] * len(rows),
        scratch_shapes=[pltpu.SemaphoreType.DMA],
        compiler_params=params(),
        cost_estimate=cost(0, moved),
    )(*arrays)


def shift(v, far, by):
    pairs = []
    for x in range(4):
        for y in range(4):
            for c in range(2):
                along_x = (c == 0) == far
                tx, ty = ((x + by) % 4, y) if along_x else (x, (y + by) % 4)
                pairs.append(((x * 4 + y) * 2 + c, (tx * 4 + ty) * 2 + c))
    return lax.ppermute(v, ("x", "y", "c"), pairs)


def torus_gather(own):
    full = own.shape[0]
    half = full // 2
    pair = ((0, 0, full, 0, 0), (1, 0, full, 0, full))
    low, high = shift(own, False, 1), shift(own, False, -1)
    opposite = shift(low, False, 1)
    (early,) = join([2 * full], pair, own, low)
    early_low, early_high = shift(early, True, 1), shift(early, True, -1)
    (late,) = join([2 * full], pair, high, opposite)
    late_low, late_high = shift(late, True, 1), shift(late, True, -1)
    early_far, late_far = shift(early_low, True, 1), shift(late_high, True, -1)
    arrays = (early, late, early_low, late_low, early_high, late_high, early_far, late_far)
    fars = (0, 0, 3, 3, 1, 1, 2, 2)
    pieces = [
        (n, i * full + h * half, h, fars[n], (0, 3, 1, 2)[n % 2 * 2 + i])
        for n in range(8)
        for i in range(2)
        for h in range(2)
    ]
    return arrays, pieces


def on_device(tokens_in, cotangent, routes, gate_weights, gate_proj, up_proj, down_proj):
    width = tokens_in.shape[1]
    hidden_width = gate_proj.shape[2]
    ix, iy, ic = lax.axis_index("x"), lax.axis_index("y"), lax.axis_index("c")
    zh, zq = lax.axis_index("zh"), lax.axis_index("zq")
    ring = zh * 2 + zq

    shard = pl.pallas_call(
        stack_kernel,
        out_shape=jax.ShapeDtypeStruct((3, *gate_proj.shape[1:]), BF),
        in_specs=[VM] * 3,
        out_specs=VM,
        compiler_params=params(4),
    )(gate_proj, up_proj, down_proj)
    other = lax.ppermute(shard, ("c", "zq"), [(2, 0), (1, 3)])
    smem = pl.BlockSpec(memory_space=pltpu.SMEM)
    top, bottom = pl.pallas_call(
        pair_kernel,
        out_shape=(
            jax.ShapeDtypeStruct((SPLIT, hidden_width), BF),
            jax.ShapeDtypeStruct((240 - SPLIT, hidden_width), BF),
        ),
        in_specs=[smem, VM, VM],
        out_specs=(VM, VM),
        compiler_params=params(4),
    )(ic.astype(jnp.int32)[None], shard, other)

    def at(c, p):
        return (p // 2 * 2 + c) * 2 + p % 2

    def zmove(v, source, by):
        pairs = [(at(c, p), at(c, (p + by) % 4)) for c in range(2) for p in range(4) if (p % 2 == c) == source]
        return lax.ppermute(v, ("zh", "c", "zq"), pairs)

    low0, high1 = zmove(top, True, 1), zmove(bottom, True, -1)
    low1, high0 = zmove(bottom, True, 1), zmove(top, True, -1)
    far0, far1 = zmove(low0, False, 1), zmove(high1, False, -1)
    source = ic == zq
    ordered = jnp.where(source, zh == 0, (ring == 1) | (ring == 2))
    block = pl.pallas_call(
        block_kernel,
        out_shape=jax.ShapeDtypeStruct((480, hidden_width), BF),
        in_specs=[smem] + [VM] * 8,
        out_specs=VM,
        compiler_params=params(8),
    )(jnp.stack([source, jnp.logical_not(ordered)]).astype(jnp.int32), top, bottom, low0, low1, high0, high1, far0, far1)

    (routes_later, _, _) = lax.optimization_barrier((routes, low0, high1))
    payload, sel = pl.pallas_call(
        dispatch_kernel,
        out_shape=(
            jax.ShapeDtypeStruct((8, 64, width), BF),
            jax.ShapeDtypeStruct((256, 256), BF),
        ),
        in_specs=[VM] * 3,
        out_specs=(VM, VM),
        compiler_params=params(),
        cost_estimate=cost(2 * 256 * 512 * width, 8 * 256 * width),
    )(routes_later, tokens_in, cotangent)

    payload, block = lax.optimization_barrier((payload, block))
    arrays, pieces = torus_gather(block)
    rows = lax.all_to_all(payload, ("c", "zr"), split_axis=0, concat_axis=0, tiled=True)

    back = pl.pallas_call(
        functools.partial(expert_kernel, pieces),
        out_shape=jax.ShapeDtypeStruct((8, 32, width + PAD), BF),
        in_specs=[smem, VM] + [ANY] * len(arrays),
        out_specs=VM,
        scratch_shapes=[pltpu.VMEM((width, hidden_width), BF)] * 3
        + [pltpu.VMEM((256, hidden_width), BF)] * 2
        + [pltpu.VMEM((256, hidden_width), F32)] * 2
        + [pltpu.SemaphoreType.DMA((3,))],
        compiler_params=params(56),
        cost_estimate=cost(10 * 256 * width * hidden_width, 6 * width * hidden_width),
    )(jnp.stack([ix, iy, ic]).astype(jnp.int32), rows, *arrays)

    home = lax.all_to_all(back, ("c", "zr"), split_axis=0, concat_axis=0, tiled=True)

    return pl.pallas_call(
        combine_kernel,
        out_shape=(
            jax.ShapeDtypeStruct(tokens_in.shape, BF),
            jax.ShapeDtypeStruct(gate_weights.shape, BF),
        ),
        in_specs=[VM] * 4,
        out_specs=(VM, VM),
        compiler_params=params(),
        cost_estimate=cost(2 * 256 * 256 * width, 4 * 256 * width),
    )(routes, gate_weights, sel, home)


def solution(mesh):
    fine = Mesh(mesh.devices.reshape(4, 2, 4, 2, 2, 4), AXES)
    rows = P(AXES, None)
    proj = P(("zq", "zr"), ("x", "zh", "y", "c"), None)
    return jax.shard_map(
        on_device,
        mesh=fine,
        in_specs=(rows, rows, rows, rows, proj, proj, proj),
        out_specs=(rows, rows),
        check_vma=False,
    )
```

```python
import functools

import jax
import jax.numpy as jnp
from jax import lax
from jax.experimental import pallas as pl
from jax.experimental.pallas import tpu as pltpu
from jax.sharding import Mesh, PartitionSpec as P

BF = jnp.bfloat16
F32 = jnp.float32
AXES = ("x", "zh", "y", "c", "zq", "zr")
SPLIT = 128
PAD = 128


def route_place(routes, slots):
    tokens = routes.shape[0]
    window = routes < 8
    owner = jnp.sum(jnp.where(window, routes, 0), axis=1, keepdims=True)
    routed = jnp.sum(jnp.where(window, 1, 0), axis=1, keepdims=True) > 0
    lane = lax.broadcasted_iota(jnp.int32, (tokens, 128), 1)
    onehot = jnp.where((lane == owner) & routed, 1.0, 0.0)
    row = lax.broadcasted_iota(jnp.int32, (tokens, tokens), 0)
    col = lax.broadcasted_iota(jnp.int32, (tokens, tokens), 1)
    lower = jnp.where(col <= row, 1.0, 0.0).astype(BF)
    rank = jnp.dot(lower, onehot.astype(BF), preferred_element_type=F32)
    slot = jnp.sum(rank * onehot, axis=1, keepdims=True).astype(jnp.int32) - 1
    return jnp.where(routed, owner * slots + slot, -1)


def dispatch_kernel(routes_ref, tok_ref, cot_ref, out_ref, sel_ref):
    tokens, step = tok_ref.shape

    @pl.when(pl.program_id(0) == 0)
    def _():
        place = route_place(routes_ref[...], 32)
        lane = lax.broadcasted_iota(jnp.int32, (tokens, 256), 1)
        sel_ref[...] = jnp.where(lane == place, 1.0, 0.0).astype(BF)

    sel = sel_ref[...]
    for source, first in ((tok_ref, 0), (cot_ref, 32)):
        rows = lax.dot_general(
            sel, source[...], (((0,), (0,)), ((), ())), preferred_element_type=F32
        ).astype(BF)
        out_ref[:, first : first + 32, :] = rows.reshape(8, 32, step)


def combine_kernel(routes_ref, gates_ref, sel_ref, back_ref, grad_ref, score_ref):
    width = grad_ref.shape[1]
    window = routes_ref[...] < 8
    gate = jnp.sum(jnp.where(window, gates_ref[...].astype(F32), 0.0), axis=1, keepdims=True)
    sel = sel_ref[...]
    step = 512

    @pl.loop(0, width // step)
    def _(i):
        cols = pl.ds(pl.multiple_of(i * step, step), step)
        rows = back_ref[:, :, cols].reshape(256, step)
        grad_ref[:, cols] = (jnp.dot(sel, rows, preferred_element_type=F32) * gate).astype(BF)

    tail = back_ref[:, :, width : width + PAD].reshape(256, PAD)
    score = jnp.dot(sel, tail, preferred_element_type=F32)[:, 0:1]
    score_ref[...] = jnp.where(window, score, 0.0).astype(BF)


def stack_kernel(gate_ref, up_ref, down_ref, out_ref, sems):
    copies = [
        pltpu.make_async_copy(ref.at[0], out_ref.at[m], sems.at[m])
        for m, ref in enumerate((gate_ref, up_ref, down_ref))
    ]
    for copy in copies:
        copy.start()
    for copy in copies:
        copy.wait()


def pair_kernel(first_ref, shard_ref, other_ref, top_ref, bottom_ref):
    swap = first_ref[0] == 0
    for m in range(3):
        mine, theirs = shard_ref[m], other_ref[m]
        for k in range(2):
            part = jnp.where(swap == (k == 0), mine, theirs)
            row = 80 * m + 40 * k
            cut = min(max(SPLIT - row, 0), 40)
            if cut:
                top_ref[row : row + cut] = part[:cut]
            if cut < 40:
                bottom_ref[row + cut - SPLIT : row + 40 - SPLIT] = part[cut:]


def block_kernel(state_ref, top, bottom, low0, low1, high0, high1, far0, far1, gu_ref, down_ref):
    source, order = state_ref[0] == 1, state_ref[1] == 0
    cut = 160 - SPLIT
    for z in range(2):
        pick = order if z == 0 else jnp.logical_not(order)
        parts = []
        for mine, low, high, far in ((top, low0, high0, far0), (bottom, low1, high1, far1)):
            first = jnp.where(source, mine[...], low[...])
            second = jnp.where(source, far[...], high[...])
            parts.append(jnp.where(pick, first, second))
        gu_ref[160 * z : 160 * z + SPLIT] = parts[0]
        gu_ref[160 * z + SPLIT : 160 * z + 160] = parts[1][:cut]
        down_ref[80 * z : 80 * z + 80] = parts[1][cut:]


def expert_kernel(pieces, where_ref, rows_ref, all_down_ref, *refs):
    sources = refs[: len(pieces) // 4]
    out_ref = refs[len(sources)]
    gate_w, up_w, down_w, tok_v, cot_v, result, grad_a, grad_b, pre_g, pre_u, pre_b, sems, out_sems = refs[
        len(sources) + 1 :
    ]
    my_x, my_y, core = where_ref[0], where_ref[1], where_ref[2]
    width, hidden_width = gate_w.shape

    down_copies, gate_copies, up_copies = [], [], []
    for x in range(4):
        for y in range(4):
            for z in range(2):
                down_copies.append(
                    pltpu.make_async_copy(
                        all_down_ref.at[pl.ds(((x * 4 + y) * 2 + z) * 80, 80), :],
                        down_w.at[pl.ds(((x * 2 + z) * 4 + y) * 80, 80), :],
                        sems.at[0],
                    )
                )
    down_copies.append(pltpu.make_async_copy(rows_ref.at[:, pl.ds(32, 32), :], cot_v, sems.at[1]))
    gate_copies.append(pltpu.make_async_copy(rows_ref.at[:, pl.ds(0, 32), :], tok_v, sems.at[2]))
    for number, row, block, far, near in pieces:
        xx = lax.rem(my_x + jnp.where(core == 0, far, near), 4)
        yy = lax.rem(my_y + jnp.where(core == 0, near, far), 4)
        target = pl.multiple_of(((xx * 2 + block) * 4 + yy) * 80, 16)
        for m, (weights, copies) in enumerate(((gate_w, gate_copies), (up_w, up_copies))):
            copies.append(
                pltpu.make_async_copy(
                    sources[number].at[pl.ds(row + 80 * m, 80), :],
                    weights.at[pl.ds(target, 80), :],
                    sems.at[3 + m],
                )
            )
    for copies in (down_copies, gate_copies, up_copies):
        for copy in copies:
            copy.start()

    for copy in down_copies:
        copy.wait()
    cot = cot_v[...].reshape(256, width)
    pre_b[...] = jnp.dot(cot, down_w[...], preferred_element_type=F32)
    for copy in gate_copies:
        copy.wait()
    tok = tok_v[...].reshape(256, width)
    pre_g[...] = jnp.dot(tok, gate_w[...], preferred_element_type=F32)
    for copy in up_copies:
        copy.wait()
    pre_u[...] = jnp.dot(tok, up_w[...], preferred_element_type=F32)

    cstep = 256

    def middle(i, score):
        cols = pl.ds(pl.multiple_of(i * cstep, cstep), cstep)
        gate, up, back_hidden = pre_g[:, cols], pre_u[:, cols], pre_b[:, cols]
        sig = jax.nn.sigmoid(gate)
        act = gate * sig
        hidden = (act * up).astype(BF).astype(F32)
        grad_a[:, cols] = (back_hidden * up * (sig * (1.0 + gate * (1.0 - sig)))).astype(BF)
        grad_b[:, cols] = (back_hidden * act).astype(BF)
        return score + jnp.sum(hidden * back_hidden, axis=1, keepdims=True)

    score = lax.fori_loop(0, hidden_width // cstep, middle, jnp.zeros((256, 1), F32))
    result[:, :, width : width + PAD] = (
        jnp.broadcast_to(score, (256, PAD)).astype(BF).reshape(8, 32, PAD)
    )

    a, b = grad_a[...], grad_b[...]
    dims = (((1,), (1,)), ((), ()))
    dstep = width // 2
    outs = []
    for i in range(2):
        rows = lax.dot_general(a, gate_w[i * dstep : (i + 1) * dstep, :], dims, preferred_element_type=F32)
        rows = rows + lax.dot_general(b, up_w[i * dstep : (i + 1) * dstep, :], dims, preferred_element_type=F32)
        result[:, :, i * dstep : (i + 1) * dstep] = rows.astype(BF).reshape(8, 32, dstep)
        part = pl.ds(i * dstep, dstep if i == 0 else dstep + PAD)
        outs.append(pltpu.make_async_copy(result.at[:, :, part], out_ref.at[:, :, part], out_sems.at[i]))
        outs[i].start()
    for copy in outs:
        copy.wait()


def params(mib=16):
    return pltpu.CompilerParams(vmem_limit_bytes=mib * 1024 * 1024)


def cost(flops, moved):
    return pl.CostEstimate(flops=flops, bytes_accessed=moved, transcendentals=0)


VM = pl.BlockSpec(memory_space=pltpu.VMEM)
ANY = pl.BlockSpec(memory_space=pl.ANY)


def join_kernel(plan, inputs, *refs):
    sources, targets, sem = refs[:inputs], refs[inputs:-1], refs[-1]
    copies = [
        pltpu.make_async_copy(
            sources[i].at[pl.ds(row, count), :], targets[o].at[pl.ds(at, count), :], sem
        )
        for i, row, count, o, at in plan
    ]
    for copy in copies:
        copy.start()
    for copy in copies:
        copy.wait()


def join(rows, plan, *arrays):
    width = arrays[0].shape[1]
    moved = 4 * sum(rows) * width
    return pl.pallas_call(
        functools.partial(join_kernel, plan, len(arrays)),
        out_shape=[jax.ShapeDtypeStruct((r, width), BF) for r in rows],
        in_specs=[ANY] * len(arrays),
        out_specs=[ANY] * len(rows),
        scratch_shapes=[pltpu.SemaphoreType.DMA],
        compiler_params=params(),
        cost_estimate=cost(0, moved),
    )(*arrays)


def shift(v, far, by):
    pairs = []
    for x in range(4):
        for y in range(4):
            for c in range(2):
                along_x = (c == 0) == far
                tx, ty = ((x + by) % 4, y) if along_x else (x, (y + by) % 4)
                pairs.append(((x * 4 + y) * 2 + c, (tx * 4 + ty) * 2 + c))
    return lax.ppermute(v, ("x", "y", "c"), pairs)


def torus_gather(own):
    full = own.shape[0]
    half = full // 2
    pair = ((0, 0, full, 0, 0), (1, 0, full, 0, full))
    low, high = shift(own, False, 1), shift(own, False, -1)
    opposite = shift(low, False, 1)
    (early,) = join([2 * full], pair, own, low)
    early_low, early_high = shift(early, True, 1), shift(early, True, -1)
    opposite, early_high = lax.optimization_barrier((opposite, early_high))
    (late,) = join([2 * full], pair, high, opposite)
    late_low, late_high = shift(late, True, 1), shift(late, True, -1)
    early_far, late_far = shift(early_low, True, 1), shift(late_high, True, -1)
    arrays = (early, late, early_low, late_low, early_high, late_high, early_far, late_far)
    fars = (0, 0, 3, 3, 1, 1, 2, 2)
    pieces = [
        (n, i * full + h * half, h, fars[n], (0, 3, 1, 2)[n % 2 * 2 + i])
        for n in range(8)
        for i in range(2)
        for h in range(2)
    ]
    return arrays, pieces


def on_device(tokens_in, cotangent, routes, gate_weights, gate_proj, up_proj, down_proj):
    width = tokens_in.shape[1]
    hidden_width = gate_proj.shape[2]
    ix, iy, ic = lax.axis_index("x"), lax.axis_index("y"), lax.axis_index("c")
    zh, zq = lax.axis_index("zh"), lax.axis_index("zq")
    ring = zh * 2 + zq

    shard = pl.pallas_call(
        stack_kernel,
        out_shape=jax.ShapeDtypeStruct((3, *gate_proj.shape[1:]), BF),
        in_specs=[ANY] * 3,
        out_specs=ANY,
        scratch_shapes=[pltpu.SemaphoreType.DMA((3,))],
        compiler_params=params(56),
    )(gate_proj, up_proj, down_proj)
    other = lax.ppermute(shard, ("c", "zq"), [(2, 0), (1, 3)])
    smem = pl.BlockSpec(memory_space=pltpu.SMEM)
    top, bottom = pl.pallas_call(
        pair_kernel,
        out_shape=(
            jax.ShapeDtypeStruct((SPLIT, hidden_width), BF),
            jax.ShapeDtypeStruct((240 - SPLIT, hidden_width), BF),
        ),
        in_specs=[smem, VM, VM],
        out_specs=(VM, VM),
        compiler_params=params(4),
    )(ic.astype(jnp.int32)[None], shard, other)

    def at(c, p):
        return (p // 2 * 2 + c) * 2 + p % 2

    def zmove(v, source, by):
        pairs = [(at(c, p), at(c, (p + by) % 4)) for c in range(2) for p in range(4) if (p % 2 == c) == source]
        return lax.ppermute(v, ("zh", "c", "zq"), pairs)

    low0, high1 = zmove(top, True, 1), zmove(bottom, True, -1)
    low1, high0 = zmove(bottom, True, 1), zmove(top, True, -1)
    far0, far1 = zmove(low0, False, 1), zmove(high1, False, -1)
    source = ic == zq
    ordered = jnp.where(source, zh == 0, (ring == 1) | (ring == 2))
    block, down_block = pl.pallas_call(
        block_kernel,
        out_shape=(
            jax.ShapeDtypeStruct((320, hidden_width), BF),
            jax.ShapeDtypeStruct((160, hidden_width), BF),
        ),
        in_specs=[smem] + [VM] * 8,
        out_specs=(VM, VM),
        compiler_params=params(8),
    )(jnp.stack([source, jnp.logical_not(ordered)]).astype(jnp.int32), top, bottom, low0, low1, high0, high1, far0, far1)

    (routes_later, _, _) = lax.optimization_barrier((routes, low1, high0))
    step = 512
    columns = pl.BlockSpec((256, step), lambda i: (0, i))
    payload, sel = pl.pallas_call(
        dispatch_kernel,
        grid=(width // step,),
        out_shape=(
            jax.ShapeDtypeStruct((8, 64, width), BF),
            jax.ShapeDtypeStruct((256, 256), BF),
        ),
        in_specs=[pl.BlockSpec(routes.shape, lambda i: (0, 0)), columns, columns],
        out_specs=(
            pl.BlockSpec((8, 64, step), lambda i: (0, 0, i)),
            pl.BlockSpec((256, 256), lambda i: (0, 0)),
        ),
        compiler_params=params(56),
        cost_estimate=cost(2 * 256 * 512 * width, 8 * 256 * width),
    )(routes_later, tokens_in, cotangent)

    payload, block = lax.optimization_barrier((payload, block))
    all_down = lax.all_gather(down_block, ("x", "y"), axis=0, tiled=True)
    arrays, pieces = torus_gather(block)
    rows = lax.all_to_all(payload, ("c", "zr"), split_axis=0, concat_axis=0, tiled=True)

    back = pl.pallas_call(
        functools.partial(expert_kernel, pieces),
        out_shape=jax.ShapeDtypeStruct((8, 32, width + PAD), BF),
        in_specs=[smem] + [ANY] * (2 + len(arrays)),
        out_specs=ANY,
        scratch_shapes=[pltpu.VMEM((width, hidden_width), BF)] * 3
        + [pltpu.VMEM((8, 32, width), BF)] * 2
        + [pltpu.VMEM((8, 32, width + PAD), BF)]
        + [pltpu.VMEM((256, hidden_width), BF)] * 2
        + [pltpu.VMEM((256, hidden_width), F32)] * 3
        + [pltpu.SemaphoreType.DMA((5,)), pltpu.SemaphoreType.DMA((2,))],
        compiler_params=params(56),
        cost_estimate=cost(10 * 256 * width * hidden_width, 6 * width * hidden_width),
    )(jnp.stack([ix, iy, ic]).astype(jnp.int32), rows, all_down, *arrays)

    home = lax.all_to_all(back, ("c", "zr"), split_axis=0, concat_axis=0, tiled=True)

    return pl.pallas_call(
        combine_kernel,
        out_shape=(
            jax.ShapeDtypeStruct(tokens_in.shape, BF),
            jax.ShapeDtypeStruct(gate_weights.shape, BF),
        ),
        in_specs=[VM] * 4,
        out_specs=(VM, VM),
        compiler_params=params(),
        cost_estimate=cost(2 * 256 * 256 * width, 4 * 256 * width),
    )(routes, gate_weights, sel, home)


def solution(mesh):
    fine = Mesh(mesh.devices.reshape(4, 2, 4, 2, 2, 4), AXES)
    rows = P(AXES, None)
    proj = P(("zq", "zr"), ("x", "zh", "y", "c"), None)
    return jax.shard_map(
        on_device,
        mesh=fine,
        in_specs=(rows, rows, rows, rows, proj, proj, proj),
        out_specs=(rows, rows),
        check_vma=False,
    )
```

```python
import functools

import jax
import jax.numpy as jnp
from jax import lax
from jax.experimental import pallas as pl
from jax.experimental.pallas import tpu as pltpu
from jax.sharding import Mesh, PartitionSpec as P

BF = jnp.bfloat16
F32 = jnp.float32
AXES = ("x", "zh", "y", "c", "zq", "zr")
SPLIT = 128
PAD = 128


def route_place(routes, slots):
    tokens = routes.shape[0]
    window = routes < 8
    owner = jnp.sum(jnp.where(window, routes, 0), axis=1, keepdims=True)
    routed = jnp.sum(jnp.where(window, 1, 0), axis=1, keepdims=True) > 0
    lane = lax.broadcasted_iota(jnp.int32, (tokens, 128), 1)
    onehot = jnp.where((lane == owner) & routed, 1.0, 0.0)
    row = lax.broadcasted_iota(jnp.int32, (tokens, tokens), 0)
    col = lax.broadcasted_iota(jnp.int32, (tokens, tokens), 1)
    lower = jnp.where(col <= row, 1.0, 0.0).astype(BF)
    rank = jnp.dot(lower, onehot.astype(BF), preferred_element_type=F32)
    slot = jnp.sum(rank * onehot, axis=1, keepdims=True).astype(jnp.int32) - 1
    return jnp.where(routed, owner * slots + slot, -1)


def dispatch_kernel(routes_ref, tok_ref, cot_ref, out_ref, sel_ref):
    tokens, step = tok_ref.shape

    @pl.when(pl.program_id(0) == 0)
    def _():
        place = route_place(routes_ref[...], 32)
        lane = lax.broadcasted_iota(jnp.int32, (tokens, 256), 1)
        sel_ref[...] = jnp.where(lane == place, 1.0, 0.0).astype(BF)

    sel = sel_ref[...]
    for source, first in ((tok_ref, 0), (cot_ref, 32)):
        rows = lax.dot_general(
            sel, source[...], (((0,), (0,)), ((), ())), preferred_element_type=F32
        ).astype(BF)
        out_ref[:, first : first + 32, :] = rows.reshape(8, 32, step)


def combine_kernel(routes_ref, gates_ref, sel_ref, back_ref, grad_ref, score_ref):
    width = grad_ref.shape[1]
    window = routes_ref[...] < 8
    gate = jnp.sum(jnp.where(window, gates_ref[...].astype(F32), 0.0), axis=1, keepdims=True)
    sel = sel_ref[...]
    step = 512

    @pl.loop(0, width // step)
    def _(i):
        cols = pl.ds(pl.multiple_of(i * step, step), step)
        rows = back_ref[:, :, cols].reshape(256, step)
        grad_ref[:, cols] = (jnp.dot(sel, rows, preferred_element_type=F32) * gate).astype(BF)

    tail = back_ref[:, :, width : width + PAD].reshape(256, PAD)
    score = jnp.dot(sel, tail, preferred_element_type=F32)[:, 0:1]
    score_ref[...] = jnp.where(window, score, 0.0).astype(BF)


def stack_kernel(gate_ref, up_ref, down_ref, out_ref):
    for m, ref in enumerate((gate_ref, up_ref, down_ref)):
        out_ref[m] = ref[0]


def pair_kernel(first_ref, shard_ref, other_ref, out_ref):
    swap = first_ref[0] == 0
    for m in range(3):
        mine, theirs = shard_ref[m], other_ref[m]
        for k in range(2):
            row = 80 * m + 40 * k
            out_ref[row : row + 40] = jnp.where(swap == (k == 0), mine, theirs)


def near_kernel(source_ref, mine, low, out_ref):
    out_ref[...] = jnp.where(source_ref[0] == 1, mine[...], low[...])


def far_kernel(source_ref, top, bottom, high, out_ref):
    source = source_ref[0] == 1
    cut = top.shape[0]
    out_ref[:cut] = jnp.where(source, top[...], high[:cut])
    out_ref[cut:] = jnp.where(source, bottom[...], high[cut:])


def expert_kernel(pieces, where_ref, rows_ref, *refs):
    sources = refs[: pieces[-1][0] + 1]
    out_ref = refs[len(sources)]
    gate_w, up_w, down_w, tok_v, cot_v, result, grad_a, grad_b, pre_g, pre_u, pre_b, sems, out_sems = refs[
        len(sources) + 1 :
    ]
    my_x, my_y, core, first_half = where_ref[0], where_ref[1], where_ref[2], where_ref[3]
    width, hidden_width = gate_w.shape

    gate_copies, up_copies, down_copies = [], [], []
    for number, row, chain, far, near in pieces:
        xx = lax.rem(my_x + jnp.where(core == 0, far, near), 4)
        yy = lax.rem(my_y + jnp.where(core == 0, near, far), 4)
        half = first_half if chain == 0 else 1 - first_half
        target = pl.multiple_of(((xx * 2 + half) * 4 + yy) * 80, 16)
        for m, (weights, copies) in enumerate(
            ((gate_w, gate_copies), (up_w, up_copies), (down_w, down_copies))
        ):
            copies.append(
                pltpu.make_async_copy(
                    sources[number].at[pl.ds(row + 80 * m, 80), :],
                    weights.at[pl.ds(target, 80), :],
                    sems.at[m],
                )
            )
    down_copies.append(pltpu.make_async_copy(rows_ref.at[:, pl.ds(32, 32), :], cot_v, sems.at[3]))
    gate_copies.append(pltpu.make_async_copy(rows_ref.at[:, pl.ds(0, 32), :], tok_v, sems.at[4]))
    for copies in (down_copies, gate_copies, up_copies):
        for copy in copies:
            copy.start()

    for copy in down_copies:
        copy.wait()
    cot = cot_v[...].reshape(256, width)
    pre_b[...] = jnp.dot(cot, down_w[...], preferred_element_type=F32)
    for copy in gate_copies:
        copy.wait()
    tok = tok_v[...].reshape(256, width)
    pre_g[...] = jnp.dot(tok, gate_w[...], preferred_element_type=F32)
    for copy in up_copies:
        copy.wait()
    pre_u[...] = jnp.dot(tok, up_w[...], preferred_element_type=F32)

    cstep = 256

    def middle(i, score):
        cols = pl.ds(pl.multiple_of(i * cstep, cstep), cstep)
        gate, up, back_hidden = pre_g[:, cols], pre_u[:, cols], pre_b[:, cols]
        sig = jax.nn.sigmoid(gate)
        act = gate * sig
        hidden = (act * up).astype(BF).astype(F32)
        grad_a[:, cols] = (back_hidden * up * (sig * (1.0 + gate * (1.0 - sig)))).astype(BF)
        grad_b[:, cols] = (back_hidden * act).astype(BF)
        return score + jnp.sum(hidden * back_hidden, axis=1, keepdims=True)

    score = lax.fori_loop(0, hidden_width // cstep, middle, jnp.zeros((256, 1), F32))
    result[:, :, width : width + PAD] = (
        jnp.broadcast_to(score, (256, PAD)).astype(BF).reshape(8, 32, PAD)
    )

    a, b = grad_a[...], grad_b[...]
    dims = (((1,), (1,)), ((), ()))
    dstep = width // 2
    outs = []
    for i in range(2):
        rows = lax.dot_general(a, gate_w[i * dstep : (i + 1) * dstep, :], dims, preferred_element_type=F32)
        rows = rows + lax.dot_general(b, up_w[i * dstep : (i + 1) * dstep, :], dims, preferred_element_type=F32)
        result[:, :, i * dstep : (i + 1) * dstep] = rows.astype(BF).reshape(8, 32, dstep)
        part = pl.ds(i * dstep, dstep if i == 0 else dstep + PAD)
        outs.append(pltpu.make_async_copy(result.at[:, :, part], out_ref.at[:, :, part], out_sems.at[i]))
        outs[i].start()
    for copy in outs:
        copy.wait()


def params(mib=16):
    return pltpu.CompilerParams(vmem_limit_bytes=mib * 1024 * 1024)


def cost(flops, moved):
    return pl.CostEstimate(flops=flops, bytes_accessed=moved, transcendentals=0)


VM = pl.BlockSpec(memory_space=pltpu.VMEM)
ANY = pl.BlockSpec(memory_space=pl.ANY)


def join_kernel(plan, inputs, *refs):
    sources, targets, sem = refs[:inputs], refs[inputs:-1], refs[-1]
    copies = [
        pltpu.make_async_copy(
            sources[i].at[pl.ds(row, count), :], targets[o].at[pl.ds(at, count), :], sem
        )
        for i, row, count, o, at in plan
    ]
    for copy in copies:
        copy.start()
    for copy in copies:
        copy.wait()


def join(rows, plan, *arrays):
    width = arrays[0].shape[1]
    moved = 4 * sum(rows) * width
    return pl.pallas_call(
        functools.partial(join_kernel, plan, len(arrays)),
        out_shape=[jax.ShapeDtypeStruct((r, width), BF) for r in rows],
        in_specs=[ANY] * len(arrays),
        out_specs=[ANY] * len(rows),
        scratch_shapes=[pltpu.SemaphoreType.DMA],
        compiler_params=params(),
        cost_estimate=cost(0, moved),
    )(*arrays)


def shift(v, far, by):
    pairs = []
    for x in range(4):
        for y in range(4):
            for c in range(2):
                along_x = (c == 0) == far
                tx, ty = ((x + by) % 4, y) if along_x else (x, (y + by) % 4)
                pairs.append(((x * 4 + y) * 2 + c, (tx * 4 + ty) * 2 + c))
    return lax.ppermute(v, ("x", "y", "c"), pairs)


def torus_gather(own, chain, first):
    count = own.shape[0]
    low, high = shift(own, False, 1), shift(own, False, -1)
    opposite = shift(low, False, 1)
    (line,) = join(
        [4 * count], [(n, 0, count, 0, n * count) for n in range(4)], own, low, high, opposite
    )
    line_low, line_high = shift(line, True, 1), shift(line, True, -1)
    far0, far1 = join(
        [2 * count] * 2, [(0, 0, 2 * count, 0, 0), (1, 2 * count, 2 * count, 1, 0)], line_low, line_high
    )
    far0, far1 = shift(far0, True, 1), shift(far1, True, -1)
    near = (0, 3, 1, 2)
    pieces = [(first + n, k * count, chain, far, near[k]) for n, far in enumerate((0, 3, 1)) for k in range(4)]
    pieces += [(first + 3 + k // 2, k % 2 * count, chain, 2, near[k]) for k in range(4)]
    return (line, line_low, line_high, far0, far1), pieces


def on_device(tokens_in, cotangent, routes, gate_weights, gate_proj, up_proj, down_proj):
    width = tokens_in.shape[1]
    hidden_width = gate_proj.shape[2]
    ix, iy, ic = lax.axis_index("x"), lax.axis_index("y"), lax.axis_index("c")
    zh, zq = lax.axis_index("zh"), lax.axis_index("zq")
    ring = zh * 2 + zq

    shard = pl.pallas_call(
        stack_kernel,
        out_shape=jax.ShapeDtypeStruct((3, *gate_proj.shape[1:]), BF),
        in_specs=[VM] * 3,
        out_specs=VM,
    )(gate_proj, up_proj, down_proj)
    other = lax.ppermute(shard, ("c", "zq"), [(2, 0), (1, 3)])
    smem = pl.BlockSpec(memory_space=pltpu.SMEM)

    def small(kernel, flag, *arrays):
        return pl.pallas_call(
            kernel,
            out_shape=jax.ShapeDtypeStruct((240, hidden_width), BF),
            in_specs=[smem] + [VM] * len(arrays),
            out_specs=VM,
            compiler_params=params(4),
        )(flag.astype(jnp.int32)[None], *arrays)

    pair = small(pair_kernel, ic, shard, other)

    def at(c, p):
        return (p // 2 * 2 + c) * 2 + p % 2

    def zmove(v, source, by):
        pairs = [(at(c, p), at(c, (p + by) % 4)) for c in range(2) for p in range(4) if (p % 2 == c) == source]
        return lax.ppermute(v, ("zh", "c", "zq"), pairs)

    source = ic == zq
    low, high = zmove(pair, True, 1), zmove(pair, True, -1)
    first = small(near_kernel, source, pair, low)
    far0, far1 = zmove(low[:SPLIT], False, 1), zmove(high[SPLIT:], False, -1)
    second = small(far_kernel, source, far0, far1, high)
    first_half = jnp.where(source, zh, jnp.where((ring == 1) | (ring == 2), 0, 1))

    step = 512
    columns = pl.BlockSpec((256, step), lambda i: (0, i))
    payload, sel = pl.pallas_call(
        dispatch_kernel,
        grid=(width // step,),
        out_shape=(
            jax.ShapeDtypeStruct((8, 64, width), BF),
            jax.ShapeDtypeStruct((256, 256), BF),
        ),
        in_specs=[pl.BlockSpec(routes.shape, lambda i: (0, 0)), columns, columns],
        out_specs=(
            pl.BlockSpec((8, 64, step), lambda i: (0, 0, i)),
            pl.BlockSpec((256, 256), lambda i: (0, 0)),
        ),
        compiler_params=params(56),
        cost_estimate=cost(2 * 256 * 512 * width, 8 * 256 * width),
    )(routes, tokens_in, cotangent)

    payload, low, high = lax.optimization_barrier((payload, low, high))
    arrays, pieces = torus_gather(first, 0, 0)
    second, _ = lax.optimization_barrier((second, arrays[0]))
    more_arrays, more_pieces = torus_gather(second, 1, len(arrays))
    rows = lax.all_to_all(payload, ("c", "zr"), split_axis=0, concat_axis=0, tiled=True)
    arrays, pieces = arrays + more_arrays, pieces + more_pieces

    back = pl.pallas_call(
        functools.partial(expert_kernel, pieces),
        out_shape=jax.ShapeDtypeStruct((8, 32, width + PAD), BF),
        in_specs=[smem] + [ANY] * (1 + len(arrays)),
        out_specs=ANY,
        scratch_shapes=[pltpu.VMEM((width, hidden_width), BF)] * 3
        + [pltpu.VMEM((8, 32, width), BF)] * 2
        + [pltpu.VMEM((8, 32, width + PAD), BF)]
        + [pltpu.VMEM((256, hidden_width), BF)] * 2
        + [pltpu.VMEM((256, hidden_width), F32)] * 3
        + [pltpu.SemaphoreType.DMA((5,)), pltpu.SemaphoreType.DMA((2,))],
        compiler_params=params(56),
        cost_estimate=cost(10 * 256 * width * hidden_width, 6 * width * hidden_width),
    )(jnp.stack([ix, iy, ic, first_half]).astype(jnp.int32), rows, *arrays)

    home = lax.all_to_all(back, ("c", "zr"), split_axis=0, concat_axis=0, tiled=True)

    return pl.pallas_call(
        combine_kernel,
        out_shape=(
            jax.ShapeDtypeStruct(tokens_in.shape, BF),
            jax.ShapeDtypeStruct(gate_weights.shape, BF),
        ),
        in_specs=[VM] * 4,
        out_specs=(VM, VM),
        compiler_params=params(),
        cost_estimate=cost(2 * 256 * 256 * width, 4 * 256 * width),
    )(routes, gate_weights, sel, home)


def solution(mesh):
    fine = Mesh(mesh.devices.reshape(4, 2, 4, 2, 2, 4), AXES)
    rows = P(AXES, None)
    proj = P(("zq", "zr"), ("x", "zh", "y", "c"), None)
    return jax.shard_map(
        on_device,
        mesh=fine,
        in_specs=(rows, rows, rows, rows, proj, proj, proj),
        out_specs=(rows, rows),
        check_vma=False,
    )
```

```python
import functools

import jax
import jax.numpy as jnp
from jax import lax
from jax.experimental import pallas as pl
from jax.experimental.pallas import tpu as pltpu
from jax.sharding import Mesh, PartitionSpec as P

BF = jnp.bfloat16
F32 = jnp.float32
AXES = ("x", "zh", "y", "c", "zq", "zr")
SPLIT = 128
PAD = 128


def route_place(routes, slots):
    tokens = routes.shape[0]
    window = routes < 8
    owner = jnp.sum(jnp.where(window, routes, 0), axis=1, keepdims=True)
    routed = jnp.sum(jnp.where(window, 1, 0), axis=1, keepdims=True) > 0
    lane = lax.broadcasted_iota(jnp.int32, (tokens, 128), 1)
    onehot = jnp.where((lane == owner) & routed, 1.0, 0.0)
    row = lax.broadcasted_iota(jnp.int32, (tokens, tokens), 0)
    col = lax.broadcasted_iota(jnp.int32, (tokens, tokens), 1)
    lower = jnp.where(col <= row, 1.0, 0.0).astype(BF)
    rank = jnp.dot(lower, onehot.astype(BF), preferred_element_type=F32)
    slot = jnp.sum(rank * onehot, axis=1, keepdims=True).astype(jnp.int32) - 1
    return jnp.where(routed, owner * slots + slot, -1)


def dispatch_kernel(routes_ref, tok_ref, cot_ref, out_ref, sel_ref):
    tokens, step = tok_ref.shape

    @pl.when(pl.program_id(0) == 0)
    def _():
        place = route_place(routes_ref[...], 32)
        lane = lax.broadcasted_iota(jnp.int32, (tokens, 256), 1)
        sel_ref[...] = jnp.where(lane == place, 1.0, 0.0).astype(BF)

    sel = sel_ref[...]
    for source, first in ((tok_ref, 0), (cot_ref, 32)):
        rows = lax.dot_general(
            sel, source[...], (((0,), (0,)), ((), ())), preferred_element_type=F32
        ).astype(BF)
        out_ref[:, first : first + 32, :] = rows.reshape(8, 32, step)


def combine_kernel(routes_ref, gates_ref, sel_ref, back_ref, grad_ref, score_ref):
    width = grad_ref.shape[1]
    window = routes_ref[...] < 8
    gate = jnp.sum(jnp.where(window, gates_ref[...].astype(F32), 0.0), axis=1, keepdims=True)
    sel = sel_ref[...]
    step = 512

    @pl.loop(0, width // step)
    def _(i):
        cols = pl.ds(pl.multiple_of(i * step, step), step)
        rows = back_ref[:, :, cols].reshape(256, step)
        grad_ref[:, cols] = (jnp.dot(sel, rows, preferred_element_type=F32) * gate).astype(BF)

    tail = back_ref[:, :, width : width + PAD].reshape(256, PAD)
    score = jnp.dot(sel, tail, preferred_element_type=F32)[:, 0:1]
    score_ref[...] = jnp.where(window, score, 0.0).astype(BF)


def stack_kernel(gate_ref, up_ref, down_ref, out_ref):
    for m, ref in enumerate((gate_ref, up_ref, down_ref)):
        out_ref[m] = ref[0]


def pair_kernel(first_ref, shard_ref, other_ref, out_ref):
    swap = first_ref[0] == 0
    for m in range(3):
        mine, theirs = shard_ref[m], other_ref[m]
        for k in range(2):
            row = 80 * m + 40 * k
            out_ref[row : row + 40] = jnp.where(swap == (k == 0), mine, theirs)


def near_kernel(source_ref, mine, low, out_ref):
    out_ref[...] = jnp.where(source_ref[0] == 1, mine[...], low[...])


def far_kernel(source_ref, top, bottom, high, out_ref):
    source = source_ref[0] == 1
    cut = top.shape[0]
    out_ref[:cut] = jnp.where(source, top[...], high[:cut])
    out_ref[cut:] = jnp.where(source, bottom[...], high[cut:])


def expert_kernel(pieces, where_ref, rows_ref, *refs):
    sources = refs[: pieces[-1][0] + 1]
    out_ref = refs[len(sources)]
    gate_w, up_w, down_w, tok_v, cot_v, result, grad_a, grad_b, pre_g, pre_u, pre_b, sems, out_sems = refs[
        len(sources) + 1 :
    ]
    my_x, my_y, core, first_half = where_ref[0], where_ref[1], where_ref[2], where_ref[3]
    width, hidden_width = gate_w.shape

    gate_copies, up_copies, down_copies = [], [], []
    for number, row, chain, far, near in pieces:
        xx = lax.rem(my_x + jnp.where(core == 0, far, near), 4)
        yy = lax.rem(my_y + jnp.where(core == 0, near, far), 4)
        half = first_half if chain == 0 else 1 - first_half
        target = pl.multiple_of(((xx * 2 + half) * 4 + yy) * 80, 16)
        for m, (weights, copies) in enumerate(
            ((gate_w, gate_copies), (up_w, up_copies), (down_w, down_copies))
        ):
            copies.append(
                pltpu.make_async_copy(
                    sources[number].at[pl.ds(row + 80 * m, 80), :],
                    weights.at[pl.ds(target, 80), :],
                    sems.at[m],
                )
            )
    down_copies.append(pltpu.make_async_copy(rows_ref.at[:, pl.ds(32, 32), :], cot_v, sems.at[3]))
    gate_copies.append(pltpu.make_async_copy(rows_ref.at[:, pl.ds(0, 32), :], tok_v, sems.at[4]))
    for copies in (down_copies, gate_copies, up_copies):
        for copy in copies:
            copy.start()

    for copy in down_copies:
        copy.wait()
    cot = cot_v[...].reshape(256, width)
    pre_b[...] = jnp.dot(cot, down_w[...], preferred_element_type=F32)
    for copy in gate_copies:
        copy.wait()
    tok = tok_v[...].reshape(256, width)
    pre_g[...] = jnp.dot(tok, gate_w[...], preferred_element_type=F32)
    for copy in up_copies:
        copy.wait()
    pre_u[...] = jnp.dot(tok, up_w[...], preferred_element_type=F32)

    cstep = 256

    def middle(i, score):
        cols = pl.ds(pl.multiple_of(i * cstep, cstep), cstep)
        gate, up, back_hidden = pre_g[:, cols], pre_u[:, cols], pre_b[:, cols]
        sig = jax.nn.sigmoid(gate)
        act = gate * sig
        hidden = (act * up).astype(BF).astype(F32)
        grad_a[:, cols] = (back_hidden * up * (sig * (1.0 + gate * (1.0 - sig)))).astype(BF)
        grad_b[:, cols] = (back_hidden * act).astype(BF)
        return score + jnp.sum(hidden * back_hidden, axis=1, keepdims=True)

    score = lax.fori_loop(0, hidden_width // cstep, middle, jnp.zeros((256, 1), F32))
    result[:, :, width : width + PAD] = (
        jnp.broadcast_to(score, (256, PAD)).astype(BF).reshape(8, 32, PAD)
    )

    a, b = grad_a[...], grad_b[...]
    dims = (((1,), (1,)), ((), ()))
    dstep = width // 2
    outs = []
    for i in range(2):
        rows = lax.dot_general(a, gate_w[i * dstep : (i + 1) * dstep, :], dims, preferred_element_type=F32)
        rows = rows + lax.dot_general(b, up_w[i * dstep : (i + 1) * dstep, :], dims, preferred_element_type=F32)
        result[:, :, i * dstep : (i + 1) * dstep] = rows.astype(BF).reshape(8, 32, dstep)
        part = pl.ds(i * dstep, dstep if i == 0 else dstep + PAD)
        outs.append(pltpu.make_async_copy(result.at[:, :, part], out_ref.at[:, :, part], out_sems.at[i]))
        outs[i].start()
    for copy in outs:
        copy.wait()


def params(mib=16):
    return pltpu.CompilerParams(vmem_limit_bytes=mib * 1024 * 1024)


def cost(flops, moved):
    return pl.CostEstimate(flops=flops, bytes_accessed=moved, transcendentals=0)


VM = pl.BlockSpec(memory_space=pltpu.VMEM)
ANY = pl.BlockSpec(memory_space=pl.ANY)


def join_kernel(plan, inputs, *refs):
    sources, targets, sem = refs[:inputs], refs[inputs:-1], refs[-1]
    copies = [
        pltpu.make_async_copy(
            sources[i].at[pl.ds(row, count), :], targets[o].at[pl.ds(at, count), :], sem
        )
        for i, row, count, o, at in plan
    ]
    for copy in copies:
        copy.start()
    for copy in copies:
        copy.wait()


def join(rows, plan, *arrays):
    width = arrays[0].shape[1]
    moved = 4 * sum(rows) * width
    return pl.pallas_call(
        functools.partial(join_kernel, plan, len(arrays)),
        out_shape=[jax.ShapeDtypeStruct((r, width), BF) for r in rows],
        in_specs=[ANY] * len(arrays),
        out_specs=[ANY] * len(rows),
        scratch_shapes=[pltpu.SemaphoreType.DMA],
        compiler_params=params(),
        cost_estimate=cost(0, moved),
    )(*arrays)


def shift(v, far, by):
    pairs = []
    for x in range(4):
        for y in range(4):
            for c in range(2):
                along_x = (c == 0) == far
                tx, ty = ((x + by) % 4, y) if along_x else (x, (y + by) % 4)
                pairs.append(((x * 4 + y) * 2 + c, (tx * 4 + ty) * 2 + c))
    return lax.ppermute(v, ("x", "y", "c"), pairs)


def torus_gather(own, chain, first):
    count = own.shape[0]
    low, high = shift(own, False, 1), shift(own, False, -1)
    opposite = shift(low, False, 1)
    (line,) = join(
        [4 * count], [(n, 0, count, 0, n * count) for n in range(4)], own, low, high, opposite
    )
    line_low, line_high = shift(line, True, 1), shift(line, True, -1)
    far0, far1 = join(
        [2 * count] * 2, [(0, 0, 2 * count, 0, 0), (1, 2 * count, 2 * count, 1, 0)], line_low, line_high
    )
    far0, far1 = shift(far0, True, 1), shift(far1, True, -1)
    near = (0, 3, 1, 2)
    pieces = [(first + n, k * count, chain, far, near[k]) for n, far in enumerate((0, 3, 1)) for k in range(4)]
    pieces += [(first + 3 + k // 2, k % 2 * count, chain, 2, near[k]) for k in range(4)]
    return (line, line_low, line_high, far0, far1), pieces, (low, high)


def on_device(tokens_in, cotangent, routes, gate_weights, gate_proj, up_proj, down_proj):
    width = tokens_in.shape[1]
    hidden_width = gate_proj.shape[2]
    ix, iy, ic = lax.axis_index("x"), lax.axis_index("y"), lax.axis_index("c")
    zh, zq = lax.axis_index("zh"), lax.axis_index("zq")
    ring = zh * 2 + zq

    shard = pl.pallas_call(
        stack_kernel,
        out_shape=jax.ShapeDtypeStruct((3, *gate_proj.shape[1:]), BF),
        in_specs=[VM] * 3,
        out_specs=VM,
    )(gate_proj, up_proj, down_proj)
    other = lax.ppermute(shard, ("c", "zq"), [(2, 0), (1, 3)])
    smem = pl.BlockSpec(memory_space=pltpu.SMEM)

    def small(kernel, flag, *arrays):
        return pl.pallas_call(
            kernel,
            out_shape=jax.ShapeDtypeStruct((240, hidden_width), BF),
            in_specs=[smem] + [VM] * len(arrays),
            out_specs=VM,
            compiler_params=params(4),
        )(flag.astype(jnp.int32)[None], *arrays)

    pair = small(pair_kernel, ic, shard, other)

    def at(c, p):
        return (p // 2 * 2 + c) * 2 + p % 2

    def zmove(v, source, by):
        pairs = [(at(c, p), at(c, (p + by) % 4)) for c in range(2) for p in range(4) if (p % 2 == c) == source]
        return lax.ppermute(v, ("zh", "c", "zq"), pairs)

    source = ic == zq
    low, high = zmove(pair, True, 1), zmove(pair, True, -1)
    first = small(near_kernel, source, pair, low)
    far0, far1 = zmove(low[:SPLIT], False, 1), zmove(high[SPLIT:], False, -1)
    second = small(far_kernel, source, far0, far1, high)
    first_half = jnp.where(source, zh, jnp.where((ring == 1) | (ring == 2), 0, 1))

    step = 512
    columns = pl.BlockSpec((256, step), lambda i: (0, i))
    payload, sel = pl.pallas_call(
        dispatch_kernel,
        grid=(width // step,),
        out_shape=(
            jax.ShapeDtypeStruct((8, 64, width), BF),
            jax.ShapeDtypeStruct((256, 256), BF),
        ),
        in_specs=[pl.BlockSpec(routes.shape, lambda i: (0, 0)), columns, columns],
        out_specs=(
            pl.BlockSpec((8, 64, step), lambda i: (0, 0, i)),
            pl.BlockSpec((256, 256), lambda i: (0, 0)),
        ),
        compiler_params=params(56),
        cost_estimate=cost(2 * 256 * 512 * width, 8 * 256 * width),
    )(routes, tokens_in, cotangent)

    arrays, pieces, near = torus_gather(first, 0, 0)
    payload, *_ = lax.optimization_barrier((payload, far0, far1, *near))
    rows = lax.all_to_all(payload, ("c", "zr"), split_axis=0, concat_axis=0, tiled=True)
    second, *_ = lax.optimization_barrier((second, *near))
    more_arrays, more_pieces, _ = torus_gather(second, 1, len(arrays))
    arrays, pieces = arrays + more_arrays, pieces + more_pieces

    back = pl.pallas_call(
        functools.partial(expert_kernel, pieces),
        out_shape=jax.ShapeDtypeStruct((8, 32, width + PAD), BF),
        in_specs=[smem] + [ANY] * (1 + len(arrays)),
        out_specs=ANY,
        scratch_shapes=[pltpu.VMEM((width, hidden_width), BF)] * 3
        + [pltpu.VMEM((8, 32, width), BF)] * 2
        + [pltpu.VMEM((8, 32, width + PAD), BF)]
        + [pltpu.VMEM((256, hidden_width), BF)] * 2
        + [pltpu.VMEM((256, hidden_width), F32)] * 3
        + [pltpu.SemaphoreType.DMA((5,)), pltpu.SemaphoreType.DMA((2,))],
        compiler_params=params(56),
        cost_estimate=cost(10 * 256 * width * hidden_width, 6 * width * hidden_width),
    )(jnp.stack([ix, iy, ic, first_half]).astype(jnp.int32), rows, *arrays)

    home = lax.all_to_all(back, ("c", "zr"), split_axis=0, concat_axis=0, tiled=True)

    return pl.pallas_call(
        combine_kernel,
        out_shape=(
            jax.ShapeDtypeStruct(tokens_in.shape, BF),
            jax.ShapeDtypeStruct(gate_weights.shape, BF),
        ),
        in_specs=[VM] * 4,
        out_specs=(VM, VM),
        compiler_params=params(),
        cost_estimate=cost(2 * 256 * 256 * width, 4 * 256 * width),
    )(routes, gate_weights, sel, home)


def solution(mesh):
    fine = Mesh(mesh.devices.reshape(4, 2, 4, 2, 2, 4), AXES)
    rows = P(AXES, None)
    proj = P(("zq", "zr"), ("x", "zh", "y", "c"), None)
    return jax.shard_map(
        on_device,
        mesh=fine,
        in_specs=(rows, rows, rows, rows, proj, proj, proj),
        out_specs=(rows, rows),
        check_vma=False,
    )
```

```python
import functools

import jax
import jax.numpy as jnp
from jax import lax
from jax.experimental import pallas as pl
from jax.experimental.pallas import tpu as pltpu
from jax.sharding import Mesh, PartitionSpec as P

BF = jnp.bfloat16
F32 = jnp.float32
AXES = ("x", "zh", "y", "c", "zq", "zr")
SPLIT = 128
PAD = 128


def slots_of(routes):
    tokens = routes.shape[1]
    window = routes < 8
    owner = jnp.sum(jnp.where(window, routes, 0), axis=0, keepdims=True)
    routed = jnp.sum(jnp.where(window, 1, 0), axis=0, keepdims=True) > 0
    expert = lax.broadcasted_iota(jnp.int32, (16, tokens), 0)
    onehot = jnp.where((expert == owner) & routed, 1.0, 0.0)
    row = lax.broadcasted_iota(jnp.int32, (tokens, tokens), 0)
    col = lax.broadcasted_iota(jnp.int32, (tokens, tokens), 1)
    upto = jnp.where(row <= col, 1.0, 0.0).astype(BF)
    rank = jnp.dot(onehot.astype(BF), upto, preferred_element_type=F32)
    slot = jnp.sum(rank * onehot, axis=0, keepdims=True).astype(jnp.int32) - 1
    return jnp.where(routed, owner * 32 + slot, -1)


def dispatch_kernel(routes_ref, tok_ref, cot_ref, out_ref, sel_ref):
    tokens, step = tok_ref.shape

    @pl.when(pl.program_id(0) == 0)
    def _():
        slot = lax.broadcasted_iota(jnp.int32, (256, tokens), 0)
        sel_ref[...] = jnp.where(slot == slots_of(routes_ref[...]), 1.0, 0.0).astype(BF)

    sel = sel_ref[...]
    for source, first in ((tok_ref, 0), (cot_ref, 32)):
        rows = jnp.dot(sel, source[...], preferred_element_type=F32).astype(BF)
        out_ref[:, first : first + 32, :] = rows.reshape(8, 32, step)


def combine_kernel(routes_ref, gates_ref, sel_ref, back_ref, grad_ref, score_ref):
    width = grad_ref.shape[1]
    window = routes_ref[...] < 8
    gate = jnp.sum(jnp.where(window, gates_ref[...].astype(F32), 0.0), axis=0, keepdims=True)
    sel = sel_ref[...]
    scaled = (sel.astype(F32) * gate).astype(BF)
    down = (((0,), (0,)), ((), ()))
    step = 512

    @pl.loop(0, width // step)
    def _(i):
        cols = pl.ds(pl.multiple_of(i * step, step), step)
        rows = back_ref[:, :, cols].reshape(256, step)
        grad_ref[:, cols] = lax.dot_general(
            scaled, rows, down, preferred_element_type=F32
        ).astype(BF)

    tail = back_ref[:, :, width : width + PAD].reshape(256, PAD)
    score = lax.dot_general(tail, sel, down, preferred_element_type=F32)[0:1]
    score_ref[...] = jnp.where(window, score, 0.0).astype(BF)


def stack_kernel(gate_ref, up_ref, down_ref, out_ref):
    for m, ref in enumerate((gate_ref, up_ref, down_ref)):
        out_ref[m] = ref[0]


def pair_kernel(first_ref, shard_ref, other_ref, out_ref):
    swap = first_ref[0] == 0
    for m in range(3):
        mine, theirs = shard_ref[m], other_ref[m]
        for k in range(2):
            row = 80 * m + 40 * k
            out_ref[row : row + 40] = jnp.where(swap == (k == 0), mine, theirs)


def near_kernel(source_ref, mine, low, high, out_ref, top_ref, bottom_ref):
    cut = top_ref.shape[0]
    top_ref[...] = low[:cut]
    bottom_ref[...] = high[cut:]
    out_ref[...] = jnp.where(source_ref[0] == 1, mine[...], low[...])


def far_kernel(source_ref, top, bottom, high, out_ref):
    source = source_ref[0] == 1
    cut = top.shape[0]
    out_ref[:cut] = jnp.where(source, top[...], high[:cut])
    out_ref[cut:] = jnp.where(source, bottom[...], high[cut:])


def expert_kernel(pieces, where_ref, rows_ref, *refs):
    sources = refs[: pieces[-1][0] + 1]
    out_ref = refs[len(sources)]
    gate_w, up_w, down_w, tok_v, cot_v, result, grad_a, grad_b, pre_g, pre_u, pre_b, sems, out_sems = refs[
        len(sources) + 1 :
    ]
    my_x, my_y, core, first_half = where_ref[0], where_ref[1], where_ref[2], where_ref[3]
    width, hidden_width = gate_w.shape

    gate_copies, up_copies, down_copies = [], [], []
    for number, row, chain, far, near in pieces:
        xx = lax.rem(my_x + jnp.where(core == 0, far, near), 4)
        yy = lax.rem(my_y + jnp.where(core == 0, near, far), 4)
        half = first_half if chain == 0 else 1 - first_half
        target = pl.multiple_of(((xx * 2 + half) * 4 + yy) * 80, 16)
        for m, (weights, copies) in enumerate(
            ((gate_w, gate_copies), (up_w, up_copies), (down_w, down_copies))
        ):
            copies.append(
                pltpu.make_async_copy(
                    sources[number].at[pl.ds(row + 80 * m, 80), :],
                    weights.at[pl.ds(target, 80), :],
                    sems.at[m],
                )
            )
    down_copies.append(pltpu.make_async_copy(rows_ref.at[:, pl.ds(32, 32), :], cot_v, sems.at[3]))
    gate_copies.append(pltpu.make_async_copy(rows_ref.at[:, pl.ds(0, 32), :], tok_v, sems.at[4]))
    for copies in (down_copies, gate_copies, up_copies):
        for copy in copies:
            copy.start()

    for copy in down_copies:
        copy.wait()
    cot = cot_v[...].reshape(256, width)
    pre_b[...] = jnp.dot(cot, down_w[...], preferred_element_type=F32)
    for copy in gate_copies:
        copy.wait()
    tok = tok_v[...].reshape(256, width)
    pre_g[...] = jnp.dot(tok, gate_w[...], preferred_element_type=F32)
    for copy in up_copies:
        copy.wait()
    pre_u[...] = jnp.dot(tok, up_w[...], preferred_element_type=F32)

    cstep = 256

    def middle(i, score):
        cols = pl.ds(pl.multiple_of(i * cstep, cstep), cstep)
        gate, up, back_hidden = pre_g[:, cols], pre_u[:, cols], pre_b[:, cols]
        sig = jax.nn.sigmoid(gate)
        act = gate * sig
        hidden = (act * up).astype(BF).astype(F32)
        grad_a[:, cols] = (back_hidden * up * (sig * (1.0 + gate * (1.0 - sig)))).astype(BF)
        grad_b[:, cols] = (back_hidden * act).astype(BF)
        return score + jnp.sum(hidden * back_hidden, axis=1, keepdims=True)

    score = lax.fori_loop(0, hidden_width // cstep, middle, jnp.zeros((256, 1), F32))
    result[:, :, width : width + PAD] = (
        jnp.broadcast_to(score, (256, PAD)).astype(BF).reshape(8, 32, PAD)
    )

    a, b = grad_a[...], grad_b[...]
    dims = (((1,), (1,)), ((), ()))
    dstep = width // 2
    outs = []
    for i in range(2):
        rows = lax.dot_general(a, gate_w[i * dstep : (i + 1) * dstep, :], dims, preferred_element_type=F32)
        rows = rows + lax.dot_general(b, up_w[i * dstep : (i + 1) * dstep, :], dims, preferred_element_type=F32)
        result[:, :, i * dstep : (i + 1) * dstep] = rows.astype(BF).reshape(8, 32, dstep)
        part = pl.ds(i * dstep, dstep if i == 0 else dstep + PAD)
        outs.append(pltpu.make_async_copy(result.at[:, :, part], out_ref.at[:, :, part], out_sems.at[i]))
        outs[i].start()
    for copy in outs:
        copy.wait()


def params(mib=16):
    return pltpu.CompilerParams(vmem_limit_bytes=mib * 1024 * 1024)


def cost(flops, moved):
    return pl.CostEstimate(flops=flops, bytes_accessed=moved, transcendentals=0)


VM = pl.BlockSpec(memory_space=pltpu.VMEM)
ANY = pl.BlockSpec(memory_space=pl.ANY)


def join_kernel(plan, inputs, *refs):
    sources, targets, sem = refs[:inputs], refs[inputs:-1], refs[-1]
    copies = [
        pltpu.make_async_copy(
            sources[i].at[pl.ds(row, count), :], targets[o].at[pl.ds(at, count), :], sem
        )
        for i, row, count, o, at in plan
    ]
    for copy in copies:
        copy.start()
    for copy in copies:
        copy.wait()


def join(rows, plan, *arrays):
    width = arrays[0].shape[1]
    moved = 4 * sum(rows) * width
    return pl.pallas_call(
        functools.partial(join_kernel, plan, len(arrays)),
        out_shape=[jax.ShapeDtypeStruct((r, width), BF) for r in rows],
        in_specs=[ANY] * len(arrays),
        out_specs=[ANY] * len(rows),
        scratch_shapes=[pltpu.SemaphoreType.DMA],
        compiler_params=params(),
        cost_estimate=cost(0, moved),
    )(*arrays)


def shift(v, far, by):
    pairs = []
    for x in range(4):
        for y in range(4):
            for c in range(2):
                along_x = (c == 0) == far
                tx, ty = ((x + by) % 4, y) if along_x else (x, (y + by) % 4)
                pairs.append(((x * 4 + y) * 2 + c, (tx * 4 + ty) * 2 + c))
    return lax.ppermute(v, ("x", "y", "c"), pairs)


def torus_gather(own, chain, first):
    count = own.shape[0]
    low, high = shift(own, False, 1), shift(own, False, -1)
    opposite = shift(low, False, 1)
    (line,) = join(
        [4 * count], [(n, 0, count, 0, n * count) for n in range(4)], own, low, high, opposite
    )
    line_low, line_high = shift(line, True, 1), shift(line, True, -1)
    far0, far1 = join(
        [2 * count] * 2, [(0, 0, 2 * count, 0, 0), (1, 2 * count, 2 * count, 1, 0)], line_low, line_high
    )
    far0, far1 = shift(far0, True, 1), shift(far1, True, -1)
    near = (0, 3, 1, 2)
    pieces = [(first + n, k * count, chain, far, near[k]) for n, far in enumerate((0, 3, 1)) for k in range(4)]
    pieces += [(first + 3 + k // 2, k % 2 * count, chain, 2, near[k]) for k in range(4)]
    return (line, line_low, line_high, far0, far1), pieces, (low, high, opposite)


def on_device(tokens_in, cotangent, routes, gate_weights, gate_proj, up_proj, down_proj):
    width = tokens_in.shape[1]
    hidden_width = gate_proj.shape[2]
    ix, iy, ic = lax.axis_index("x"), lax.axis_index("y"), lax.axis_index("c")
    zh, zq = lax.axis_index("zh"), lax.axis_index("zq")
    ring = zh * 2 + zq

    shard = pl.pallas_call(
        stack_kernel,
        out_shape=jax.ShapeDtypeStruct((3, *gate_proj.shape[1:]), BF),
        in_specs=[VM] * 3,
        out_specs=VM,
    )(gate_proj, up_proj, down_proj)
    other = lax.ppermute(shard, ("c", "zq"), [(2, 0), (1, 3)])
    smem = pl.BlockSpec(memory_space=pltpu.SMEM)

    def small(kernel, flag, arrays, rows):
        return pl.pallas_call(
            kernel,
            out_shape=[jax.ShapeDtypeStruct((r, hidden_width), BF) for r in rows],
            in_specs=[smem] + [VM] * len(arrays),
            out_specs=[VM] * len(rows),
            compiler_params=params(4),
        )(flag.astype(jnp.int32)[None], *arrays)

    (pair,) = small(pair_kernel, ic, (shard, other), (240,))

    def at(c, p):
        return (p // 2 * 2 + c) * 2 + p % 2

    def zmove(v, source, by):
        pairs = [(at(c, p), at(c, (p + by) % 4)) for c in range(2) for p in range(4) if (p % 2 == c) == source]
        return lax.ppermute(v, ("zh", "c", "zq"), pairs)

    source = ic == zq
    low, high = zmove(pair, True, 1), zmove(pair, True, -1)
    step = 512
    columns = pl.BlockSpec((256, step), lambda i: (0, i))
    payload, sel = pl.pallas_call(
        dispatch_kernel,
        grid=(width // step,),
        out_shape=(
            jax.ShapeDtypeStruct((8, 64, width), BF),
            jax.ShapeDtypeStruct((256, 256), BF),
        ),
        in_specs=[pl.BlockSpec((6, 256), lambda i: (0, 0)), columns, columns],
        out_specs=(
            pl.BlockSpec((8, 64, step), lambda i: (0, 0, i)),
            pl.BlockSpec((256, 256), lambda i: (0, 0)),
        ),
        compiler_params=params(56),
        cost_estimate=cost(2 * 256 * 512 * width, 8 * 256 * width),
    )(routes.T, tokens_in, cotangent)

    low, high, payload = lax.optimization_barrier((low, high, payload))
    first, top, bottom = small(near_kernel, source, (pair, low, high), (240, SPLIT, 240 - SPLIT))
    far0, far1 = zmove(top, False, 1), zmove(bottom, False, -1)
    (second,) = small(far_kernel, source, (far0, far1, high), (240,))
    first_half = jnp.where(source, zh, jnp.where((ring == 1) | (ring == 2), 0, 1))

    arrays, pieces, near = torus_gather(first, 0, 0)
    second, *_ = lax.optimization_barrier((second, near[0]))
    more_arrays, more_pieces, near2 = torus_gather(second, 1, len(arrays))
    payload, *_ = lax.optimization_barrier((payload, far0, far1, near2[0], arrays[0]))
    rows = lax.all_to_all(payload, ("c", "zr"), split_axis=0, concat_axis=0, tiled=True)
    arrays, pieces = arrays + more_arrays, pieces + more_pieces

    back = pl.pallas_call(
        functools.partial(expert_kernel, pieces),
        out_shape=jax.ShapeDtypeStruct((8, 32, width + PAD), BF),
        in_specs=[smem] + [ANY] * (1 + len(arrays)),
        out_specs=ANY,
        scratch_shapes=[pltpu.VMEM((width, hidden_width), BF)] * 3
        + [pltpu.VMEM((8, 32, width), BF)] * 2
        + [pltpu.VMEM((8, 32, width + PAD), BF)]
        + [pltpu.VMEM((256, hidden_width), BF)] * 2
        + [pltpu.VMEM((256, hidden_width), F32)] * 3
        + [pltpu.SemaphoreType.DMA((5,)), pltpu.SemaphoreType.DMA((2,))],
        compiler_params=params(56),
        cost_estimate=cost(10 * 256 * width * hidden_width, 6 * width * hidden_width),
    )(jnp.stack([ix, iy, ic, first_half]).astype(jnp.int32), rows, *arrays)

    home = lax.all_to_all(back, ("c", "zr"), split_axis=0, concat_axis=0, tiled=True)

    grad_tokens, grad_gates = pl.pallas_call(
        combine_kernel,
        out_shape=(
            jax.ShapeDtypeStruct(tokens_in.shape, BF),
            jax.ShapeDtypeStruct((6, 256), BF),
        ),
        in_specs=[VM] * 4,
        out_specs=(VM, VM),
        compiler_params=params(),
        cost_estimate=cost(2 * 256 * 256 * width, 4 * 256 * width),
    )(routes.T, gate_weights.T, sel, home)
    return grad_tokens, grad_gates.T


def solution(mesh):
    fine = Mesh(mesh.devices.reshape(4, 2, 4, 2, 2, 4), AXES)
    rows = P(AXES, None)
    proj = P(("zq", "zr"), ("x", "zh", "y", "c"), None)
    return jax.shard_map(
        on_device,
        mesh=fine,
        in_specs=(rows, rows, rows, rows, proj, proj, proj),
        out_specs=(rows, rows),
        check_vma=False,
    )
```

```python
import functools

import jax
import jax.numpy as jnp
from jax import lax
from jax.experimental import pallas as pl
from jax.experimental.pallas import tpu as pltpu
from jax.sharding import Mesh, PartitionSpec as P

BF = jnp.bfloat16
F32 = jnp.float32
AXES = ("x", "zh", "y", "c", "zq", "zr")
SPLIT = 128
PAD = 128


def slots_of(routes):
    tokens = routes.shape[1]
    window = routes < 8
    owner = jnp.sum(jnp.where(window, routes, 0), axis=0, keepdims=True)
    routed = jnp.sum(jnp.where(window, 1, 0), axis=0, keepdims=True) > 0
    expert = lax.broadcasted_iota(jnp.int32, (16, tokens), 0)
    onehot = jnp.where((expert == owner) & routed, 1.0, 0.0)
    row = lax.broadcasted_iota(jnp.int32, (tokens, tokens), 0)
    col = lax.broadcasted_iota(jnp.int32, (tokens, tokens), 1)
    upto = jnp.where(row <= col, 1.0, 0.0).astype(BF)
    rank = jnp.dot(onehot.astype(BF), upto, preferred_element_type=F32)
    slot = jnp.sum(rank * onehot, axis=0, keepdims=True).astype(jnp.int32) - 1
    return jnp.where(routed, owner * 32 + slot, -1)


def dispatch_kernel(routes_ref, tok_ref, cot_ref, out_ref, sel_ref):
    tokens, step = tok_ref.shape

    @pl.when(pl.program_id(0) == 0)
    def _():
        slot = lax.broadcasted_iota(jnp.int32, (256, tokens), 0)
        sel_ref[...] = jnp.where(slot == slots_of(routes_ref[...]), 1.0, 0.0).astype(BF)

    sel = sel_ref[...]
    for source, first in ((tok_ref, 0), (cot_ref, 32)):
        rows = jnp.dot(sel, source[...], preferred_element_type=F32).astype(BF)
        out_ref[:, first : first + 32, :] = rows.reshape(8, 32, step)


def combine_kernel(where_ref, routes_ref, gates_ref, sel_ref, *refs):
    back_refs, (grad_ref, score_ref) = refs[:8], refs[8:]
    width = grad_ref.shape[1]
    window = routes_ref[...] < 8
    gate = jnp.sum(jnp.where(window, gates_ref[...].astype(F32), 0.0), axis=0, keepdims=True)
    core, place = where_ref[2], where_ref[4]
    sel = jnp.concatenate(
        [
            sel_ref[pl.ds(pl.multiple_of(partner(core, place, r) * 32, 32), 32), :]
            for r in range(8)
        ],
        axis=0,
    )
    scaled = (sel.astype(F32) * gate).astype(BF)
    down = (((0,), (0,)), ((), ()))
    step = 512

    @pl.loop(0, width // step)
    def _(i):
        cols = pl.ds(pl.multiple_of(i * step, step), step)
        rows = jnp.concatenate([ref[:, cols] for ref in back_refs], axis=0)
        grad_ref[:, cols] = lax.dot_general(
            scaled, rows, down, preferred_element_type=F32
        ).astype(BF)

    tail = jnp.concatenate([ref[:, width : width + PAD] for ref in back_refs], axis=0)
    score = lax.dot_general(tail, sel, down, preferred_element_type=F32)[0:1]
    score_ref[...] = jnp.where(window, score, 0.0).astype(BF)


def stack_kernel(gate_ref, up_ref, down_ref, out_ref):
    for m, ref in enumerate((gate_ref, up_ref, down_ref)):
        out_ref[m] = ref[0]


def pair_kernel(first_ref, shard_ref, other_ref, out_ref):
    swap = first_ref[0] == 0
    for m in range(3):
        mine, theirs = shard_ref[m], other_ref[m]
        for k in range(2):
            row = 80 * m + 40 * k
            out_ref[row : row + 40] = jnp.where(swap == (k == 0), mine, theirs)


def near_kernel(source_ref, mine, low, out_ref, top_ref):
    top_ref[...] = low[: top_ref.shape[0]]
    out_ref[...] = jnp.where(source_ref[0] == 1, mine[...], low[...])


def far_kernel(source_ref, top, bottom, high, out_ref):
    source = source_ref[0] == 1
    cut = top.shape[0]
    out_ref[:cut] = jnp.where(source, top[...], high[:cut])
    out_ref[cut:] = jnp.where(source, bottom[...], high[cut:])


def partner(core, place, r):
    return jnp.bitwise_xor(core, r // 4) * 4 + jnp.bitwise_xor(place, r % 4)


def expert_kernel(pieces, where_ref, rows_ref, *refs):
    sources = refs[: pieces[-1][0] + 1]
    out_refs = refs[len(sources) : len(sources) + 8]
    gate_w, up_w, down_w, tok_v, cot_v, result, grad_a, grad_b, pre_g, pre_u, pre_b, sems, out_sems = refs[
        len(sources) + 8 :
    ]
    my_x, my_y, core, first_half, place = (where_ref[i] for i in range(5))
    width, hidden_width = gate_w.shape

    gate_copies, up_copies, down_copies = [], [], []
    for number, row, chain, far, near in pieces:
        xx = lax.rem(my_x + jnp.where(core == 0, far, near), 4)
        yy = lax.rem(my_y + jnp.where(core == 0, near, far), 4)
        half = first_half if chain == 0 else 1 - first_half
        target = pl.multiple_of(((xx * 2 + half) * 4 + yy) * 80, 16)
        for m, (weights, copies) in enumerate(
            ((gate_w, gate_copies), (up_w, up_copies), (down_w, down_copies))
        ):
            copies.append(
                pltpu.make_async_copy(
                    sources[number].at[pl.ds(row + 80 * m, 80), :],
                    weights.at[pl.ds(target, 80), :],
                    sems.at[m],
                )
            )
    down_copies.append(pltpu.make_async_copy(rows_ref.at[:, pl.ds(32, 32), :], cot_v, sems.at[3]))
    gate_copies.append(pltpu.make_async_copy(rows_ref.at[:, pl.ds(0, 32), :], tok_v, sems.at[4]))
    for copies in (down_copies, gate_copies, up_copies):
        for copy in copies:
            copy.start()

    for copy in down_copies:
        copy.wait()
    cot = cot_v[...].reshape(256, width)
    pre_b[...] = jnp.dot(cot, down_w[...], preferred_element_type=F32)
    for copy in gate_copies:
        copy.wait()
    tok = tok_v[...].reshape(256, width)
    pre_g[...] = jnp.dot(tok, gate_w[...], preferred_element_type=F32)
    for copy in up_copies:
        copy.wait()
    pre_u[...] = jnp.dot(tok, up_w[...], preferred_element_type=F32)

    cstep = 256

    def middle(i, score):
        cols = pl.ds(pl.multiple_of(i * cstep, cstep), cstep)
        gate, up, back_hidden = pre_g[:, cols], pre_u[:, cols], pre_b[:, cols]
        sig = jax.nn.sigmoid(gate)
        act = gate * sig
        hidden = (act * up).astype(BF).astype(F32)
        grad_a[:, cols] = (back_hidden * up * (sig * (1.0 + gate * (1.0 - sig)))).astype(BF)
        grad_b[:, cols] = (back_hidden * act).astype(BF)
        return score + jnp.sum(hidden * back_hidden, axis=1, keepdims=True)

    score = lax.fori_loop(0, hidden_width // cstep, middle, jnp.zeros((256, 1), F32))
    result[:, :, width : width + PAD] = (
        jnp.broadcast_to(score, (256, PAD)).astype(BF).reshape(8, 32, PAD)
    )

    a, b = grad_a[...], grad_b[...]
    dims = (((1,), (1,)), ((), ()))
    dstep = width // 2
    outs = []
    for i in range(2):
        rows = lax.dot_general(a, gate_w[i * dstep : (i + 1) * dstep, :], dims, preferred_element_type=F32)
        rows = rows + lax.dot_general(b, up_w[i * dstep : (i + 1) * dstep, :], dims, preferred_element_type=F32)
        result[:, :, i * dstep : (i + 1) * dstep] = rows.astype(BF).reshape(8, 32, dstep)
        part = pl.ds(i * dstep, dstep if i == 0 else dstep + PAD)
        for r, out_ref in enumerate(out_refs):
            copy = pltpu.make_async_copy(
                result.at[partner(core, place, r), :, part], out_ref.at[:, part], out_sems.at[i]
            )
            copy.start()
            outs.append(copy)
    for copy in outs:
        copy.wait()


def params(mib=16):
    return pltpu.CompilerParams(vmem_limit_bytes=mib * 1024 * 1024)


def cost(flops, moved):
    return pl.CostEstimate(flops=flops, bytes_accessed=moved, transcendentals=0)


VM = pl.BlockSpec(memory_space=pltpu.VMEM)
ANY = pl.BlockSpec(memory_space=pl.ANY)


def join_kernel(plan, inputs, *refs):
    sources, targets, sem = refs[:inputs], refs[inputs:-1], refs[-1]
    copies = [
        pltpu.make_async_copy(
            sources[i].at[pl.ds(row, count), :], targets[o].at[pl.ds(at, count), :], sem
        )
        for i, row, count, o, at in plan
    ]
    for copy in copies:
        copy.start()
    for copy in copies:
        copy.wait()


def join(rows, plan, *arrays):
    width = arrays[0].shape[1]
    moved = 4 * sum(rows) * width
    return pl.pallas_call(
        functools.partial(join_kernel, plan, len(arrays)),
        out_shape=[jax.ShapeDtypeStruct((r, width), BF) for r in rows],
        in_specs=[ANY] * len(arrays),
        out_specs=[ANY] * len(rows),
        scratch_shapes=[pltpu.SemaphoreType.DMA],
        compiler_params=params(),
        cost_estimate=cost(0, moved),
    )(*arrays)


def shift(v, far, by):
    pairs = []
    for x in range(4):
        for y in range(4):
            for c in range(2):
                along_x = (c == 0) == far
                tx, ty = ((x + by) % 4, y) if along_x else (x, (y + by) % 4)
                pairs.append(((x * 4 + y) * 2 + c, (tx * 4 + ty) * 2 + c))
    return lax.ppermute(v, ("x", "y", "c"), pairs)


def torus_gather(own, chain, first):
    count = own.shape[0]
    low, high = shift(own, False, 1), shift(own, False, -1)
    opposite = shift(low, False, 1)
    (line,) = join(
        [4 * count], [(n, 0, count, 0, n * count) for n in range(4)], own, low, high, opposite
    )
    line_low, line_high = shift(line, True, 1), shift(line, True, -1)
    far0, far1 = join(
        [2 * count] * 2, [(0, 0, 2 * count, 0, 0), (1, 2 * count, 2 * count, 1, 0)], line_low, line_high
    )
    far0, far1 = shift(far0, True, 1), shift(far1, True, -1)
    near = (0, 3, 1, 2)
    pieces = [(first + n, k * count, chain, far, near[k]) for n, far in enumerate((0, 3, 1)) for k in range(4)]
    pieces += [(first + 3 + k // 2, k % 2 * count, chain, 2, near[k]) for k in range(4)]
    return (line, line_low, line_high, far0, far1), pieces, (low, high, opposite)


def on_device(tokens_in, cotangent, routes, gate_weights, gate_proj, up_proj, down_proj):
    width = tokens_in.shape[1]
    hidden_width = gate_proj.shape[2]
    ix, iy, ic = lax.axis_index("x"), lax.axis_index("y"), lax.axis_index("c")
    zh, zq = lax.axis_index("zh"), lax.axis_index("zq")
    ring = zh * 2 + zq

    shard = pl.pallas_call(
        stack_kernel,
        out_shape=jax.ShapeDtypeStruct((3, *gate_proj.shape[1:]), BF),
        in_specs=[VM] * 3,
        out_specs=VM,
    )(gate_proj, up_proj, down_proj)
    other = lax.ppermute(shard, ("c", "zq"), [(2, 0), (1, 3)])
    smem = pl.BlockSpec(memory_space=pltpu.SMEM)

    def small(kernel, flag, arrays, rows):
        return pl.pallas_call(
            kernel,
            out_shape=[jax.ShapeDtypeStruct((r, hidden_width), BF) for r in rows],
            in_specs=[smem] + [VM] * len(arrays),
            out_specs=[VM] * len(rows),
            compiler_params=params(4),
        )(flag.astype(jnp.int32)[None], *arrays)

    (pair,) = small(pair_kernel, ic, (shard, other), (240,))

    def at(c, p):
        return (p // 2 * 2 + c) * 2 + p % 2

    def zmove(v, source, by):
        pairs = [(at(c, p), at(c, (p + by) % 4)) for c in range(2) for p in range(4) if (p % 2 == c) == source]
        return lax.ppermute(v, ("zh", "c", "zq"), pairs)

    source = ic == zq
    low, high = zmove(pair, True, 1), zmove(pair, True, -1)
    first, top = small(near_kernel, source, (pair, low), (240, SPLIT))
    far0, far1 = zmove(top, False, 1), zmove(high[SPLIT:], False, -1)
    (second,) = small(far_kernel, source, (far0, far1, high), (240,))
    first_half = jnp.where(source, zh, jnp.where((ring == 1) | (ring == 2), 0, 1))

    step = 512
    columns = pl.BlockSpec((256, step), lambda i: (0, i))
    payload, sel = pl.pallas_call(
        dispatch_kernel,
        grid=(width // step,),
        out_shape=(
            jax.ShapeDtypeStruct((8, 64, width), BF),
            jax.ShapeDtypeStruct((256, 256), BF),
        ),
        in_specs=[pl.BlockSpec((6, 256), lambda i: (0, 0)), columns, columns],
        out_specs=(
            pl.BlockSpec((8, 64, step), lambda i: (0, 0, i)),
            pl.BlockSpec((256, 256), lambda i: (0, 0)),
        ),
        compiler_params=params(56),
        cost_estimate=cost(2 * 256 * 512 * width, 8 * 256 * width),
    )(routes.T, tokens_in, cotangent)

    arrays, pieces, near = torus_gather(first, 0, 0)
    payload, *_ = lax.optimization_barrier((payload, far0, far1, *near[:2]))
    rows = lax.all_to_all(payload, ("c", "zr"), split_axis=0, concat_axis=0, tiled=True)
    second, *_ = lax.optimization_barrier((second, *near[:2]))
    more_arrays, more_pieces, _ = torus_gather(second, 1, len(arrays))
    arrays, pieces = arrays + more_arrays, pieces + more_pieces

    where = jnp.stack([ix, iy, ic, first_half, lax.axis_index("zr")]).astype(jnp.int32)
    back = pl.pallas_call(
        functools.partial(expert_kernel, pieces),
        out_shape=[jax.ShapeDtypeStruct((32, width + PAD), BF)] * 8,
        in_specs=[smem] + [ANY] * (1 + len(arrays)),
        out_specs=[ANY] * 8,
        scratch_shapes=[pltpu.VMEM((width, hidden_width), BF)] * 3
        + [pltpu.VMEM((8, 32, width), BF)] * 2
        + [pltpu.VMEM((8, 32, width + PAD), BF)]
        + [pltpu.VMEM((256, hidden_width), BF)] * 2
        + [pltpu.VMEM((256, hidden_width), F32)] * 3
        + [pltpu.SemaphoreType.DMA((5,)), pltpu.SemaphoreType.DMA((2,))],
        compiler_params=params(56),
        cost_estimate=cost(10 * 256 * width * hidden_width, 6 * width * hidden_width),
    )(where, rows, *arrays)

    home = {0: back[0]}
    for r in (4, 3, 7, 2, 6, 1, 5):
        pairs = [(d, (d // 4 ^ r // 4) * 4 + (d % 4 ^ r % 4)) for d in range(8)]
        home[r] = lax.ppermute(back[r], ("c", "zr"), pairs)
    home = [home[r] for r in range(8)]

    grad_tokens, grad_gates = pl.pallas_call(
        combine_kernel,
        out_shape=(
            jax.ShapeDtypeStruct(tokens_in.shape, BF),
            jax.ShapeDtypeStruct((6, 256), BF),
        ),
        in_specs=[smem] + [VM] * 11,
        out_specs=(VM, VM),
        compiler_params=params(),
        cost_estimate=cost(2 * 256 * 256 * width, 4 * 256 * width),
    )(where, routes.T, gate_weights.T, sel, *home)
    return grad_tokens, grad_gates.T


def solution(mesh):
    fine = Mesh(mesh.devices.reshape(4, 2, 4, 2, 2, 4), AXES)
    rows = P(AXES, None)
    proj = P(("zq", "zr"), ("x", "zh", "y", "c"), None)
    return jax.shard_map(
        on_device,
        mesh=fine,
        in_specs=(rows, rows, rows, rows, proj, proj, proj),
        out_specs=(rows, rows),
        check_vma=False,
    )
```

```python
import functools

import jax
import jax.numpy as jnp
from jax import lax
from jax.experimental import pallas as pl
from jax.experimental.pallas import tpu as pltpu
from jax.sharding import Mesh, PartitionSpec as P

BF = jnp.bfloat16
F32 = jnp.float32
AXES = ("x", "zh", "y", "c", "zq", "zr")
SPLIT = 128
PAD = 128


def slots_of(routes):
    tokens = routes.shape[1]
    window = routes < 8
    owner = jnp.sum(jnp.where(window, routes, 0), axis=0, keepdims=True)
    routed = jnp.sum(jnp.where(window, 1, 0), axis=0, keepdims=True) > 0
    expert = lax.broadcasted_iota(jnp.int32, (16, tokens), 0)
    onehot = jnp.where((expert == owner) & routed, 1.0, 0.0)
    row = lax.broadcasted_iota(jnp.int32, (tokens, tokens), 0)
    col = lax.broadcasted_iota(jnp.int32, (tokens, tokens), 1)
    upto = jnp.where(row <= col, 1.0, 0.0).astype(BF)
    rank = jnp.dot(onehot.astype(BF), upto, preferred_element_type=F32)
    slot = jnp.sum(rank * onehot, axis=0, keepdims=True).astype(jnp.int32) - 1
    return jnp.where(routed, owner * 32 + slot, -1)


def dispatch_kernel(routes_ref, tok_ref, cot_ref, out_ref, sel_ref):
    tokens, step = tok_ref.shape

    @pl.when(pl.program_id(0) == 0)
    def _():
        slot = lax.broadcasted_iota(jnp.int32, (256, tokens), 0)
        sel_ref[...] = jnp.where(slot == slots_of(routes_ref[...]), 1.0, 0.0).astype(BF)

    sel = sel_ref[...]
    for source, first in ((tok_ref, 0), (cot_ref, 32)):
        rows = jnp.dot(sel, source[...], preferred_element_type=F32).astype(BF)
        out_ref[:, first : first + 32, :] = rows.reshape(8, 32, step)


def combine_kernel(where_ref, routes_ref, gates_ref, sel_ref, *refs):
    back_refs, (grad_ref, score_ref) = refs[:8], refs[8:]
    width = grad_ref.shape[1]
    window = routes_ref[...] < 8
    gate = jnp.sum(jnp.where(window, gates_ref[...].astype(F32), 0.0), axis=0, keepdims=True)
    core, place = where_ref[2], where_ref[4]
    sel = jnp.concatenate(
        [
            sel_ref[pl.ds(pl.multiple_of(partner(core, place, r) * 32, 32), 32), :]
            for r in range(8)
        ],
        axis=0,
    )
    scaled = (sel.astype(F32) * gate).astype(BF)
    down = (((0,), (0,)), ((), ()))
    step = 512

    @pl.loop(0, width // step)
    def _(i):
        cols = pl.ds(pl.multiple_of(i * step, step), step)
        rows = jnp.concatenate([ref[:, cols] for ref in back_refs], axis=0)
        grad_ref[:, cols] = lax.dot_general(
            scaled, rows, down, preferred_element_type=F32
        ).astype(BF)

    tail = jnp.concatenate([ref[:, width : width + PAD] for ref in back_refs], axis=0)
    score = lax.dot_general(tail, sel, down, preferred_element_type=F32)[0:1]
    score_ref[...] = jnp.where(window, score, 0.0).astype(BF)


def stack_kernel(gate_ref, up_ref, down_ref, out_ref):
    for m, ref in enumerate((gate_ref, up_ref, down_ref)):
        out_ref[m] = ref[0]


def pair_kernel(first_ref, shard_ref, other_ref, out_ref):
    swap = first_ref[0] == 0
    for m in range(3):
        mine, theirs = shard_ref[m], other_ref[m]
        for k in range(2):
            row = 80 * m + 40 * k
            out_ref[row : row + 40] = jnp.where(swap == (k == 0), mine, theirs)


def near_kernel(source_ref, mine, low, out_ref, top_ref):
    top_ref[...] = low[: top_ref.shape[0]]
    out_ref[...] = jnp.where(source_ref[0] == 1, mine[...], low[...])


def far_kernel(source_ref, top, bottom, high, out_ref):
    source = source_ref[0] == 1
    cut = top.shape[0]
    out_ref[:cut] = jnp.where(source, top[...], high[:cut])
    out_ref[cut:] = jnp.where(source, bottom[...], high[cut:])


def partner(core, place, r):
    return jnp.bitwise_xor(core, r // 4) * 4 + jnp.bitwise_xor(place, r % 4)


def expert_kernel(pieces, where_ref, rows_ref, *refs):
    sources = refs[: pieces[-1][0] + 1]
    out_refs = refs[len(sources) : len(sources) + 8]
    gate_w, up_w, down_w, tok_v, cot_v, result, grad_a, grad_b, pre_g, pre_u, pre_b, sems, out_sems = refs[
        len(sources) + 8 :
    ]
    my_x, my_y, core, first_half, place = (where_ref[i] for i in range(5))
    width, hidden_width = gate_w.shape

    gate_copies, up_copies, down_copies = [], [], []
    for number, row, chain, far, near in pieces:
        xx = jnp.where(core == 0, lax.rem(my_x + far, 4), jnp.bitwise_xor(my_x, near))
        yy = jnp.where(core == 0, jnp.bitwise_xor(my_y, near), lax.rem(my_y + far, 4))
        half = first_half if chain == 0 else 1 - first_half
        target = pl.multiple_of(((xx * 2 + half) * 4 + yy) * 80, 16)
        for m, (weights, copies) in enumerate(
            ((gate_w, gate_copies), (up_w, up_copies), (down_w, down_copies))
        ):
            copies.append(
                pltpu.make_async_copy(
                    sources[number].at[pl.ds(row + 80 * m, 80), :],
                    weights.at[pl.ds(target, 80), :],
                    sems.at[m],
                )
            )
    down_copies.append(pltpu.make_async_copy(rows_ref.at[:, pl.ds(32, 32), :], cot_v, sems.at[3]))
    gate_copies.append(pltpu.make_async_copy(rows_ref.at[:, pl.ds(0, 32), :], tok_v, sems.at[4]))
    for copies in (down_copies, gate_copies, up_copies):
        for copy in copies:
            copy.start()

    for copy in down_copies:
        copy.wait()
    cot = cot_v[...].reshape(256, width)
    pre_b[...] = jnp.dot(cot, down_w[...], preferred_element_type=F32)
    for copy in gate_copies:
        copy.wait()
    tok = tok_v[...].reshape(256, width)
    pre_g[...] = jnp.dot(tok, gate_w[...], preferred_element_type=F32)
    for copy in up_copies:
        copy.wait()
    pre_u[...] = jnp.dot(tok, up_w[...], preferred_element_type=F32)

    cstep = 256

    def middle(i, score):
        cols = pl.ds(pl.multiple_of(i * cstep, cstep), cstep)
        gate, up, back_hidden = pre_g[:, cols], pre_u[:, cols], pre_b[:, cols]
        sig = jax.nn.sigmoid(gate)
        act = gate * sig
        hidden = (act * up).astype(BF).astype(F32)
        grad_a[:, cols] = (back_hidden * up * (sig * (1.0 + gate * (1.0 - sig)))).astype(BF)
        grad_b[:, cols] = (back_hidden * act).astype(BF)
        return score + jnp.sum(hidden * back_hidden, axis=1, keepdims=True)

    score = lax.fori_loop(0, hidden_width // cstep, middle, jnp.zeros((256, 1), F32))
    result[:, :, width : width + PAD] = (
        jnp.broadcast_to(score, (256, PAD)).astype(BF).reshape(8, 32, PAD)
    )

    a, b = grad_a[...], grad_b[...]
    dims = (((1,), (1,)), ((), ()))
    dstep = width // 2
    outs = []
    for i in range(2):
        rows = lax.dot_general(a, gate_w[i * dstep : (i + 1) * dstep, :], dims, preferred_element_type=F32)
        rows = rows + lax.dot_general(b, up_w[i * dstep : (i + 1) * dstep, :], dims, preferred_element_type=F32)
        result[:, :, i * dstep : (i + 1) * dstep] = rows.astype(BF).reshape(8, 32, dstep)
        part = pl.ds(i * dstep, dstep if i == 0 else dstep + PAD)
        for r, out_ref in enumerate(out_refs):
            copy = pltpu.make_async_copy(
                result.at[partner(core, place, r), :, part], out_ref.at[:, part], out_sems.at[i]
            )
            copy.start()
            outs.append(copy)
    for copy in outs:
        copy.wait()


def params(mib=16):
    return pltpu.CompilerParams(vmem_limit_bytes=mib * 1024 * 1024)


def cost(flops, moved):
    return pl.CostEstimate(flops=flops, bytes_accessed=moved, transcendentals=0)


VM = pl.BlockSpec(memory_space=pltpu.VMEM)
ANY = pl.BlockSpec(memory_space=pl.ANY)


def join_kernel(plan, inputs, *refs):
    sources, targets, sem = refs[:inputs], refs[inputs:-1], refs[-1]
    copies = [
        pltpu.make_async_copy(
            sources[i].at[pl.ds(row, count), :], targets[o].at[pl.ds(at, count), :], sem
        )
        for i, row, count, o, at in plan
    ]
    for copy in copies:
        copy.start()
    for copy in copies:
        copy.wait()


def join(rows, plan, *arrays):
    width = arrays[0].shape[1]
    moved = 4 * sum(rows) * width
    return pl.pallas_call(
        functools.partial(join_kernel, plan, len(arrays)),
        out_shape=[jax.ShapeDtypeStruct((r, width), BF) for r in rows],
        in_specs=[ANY] * len(arrays),
        out_specs=[ANY] * len(rows),
        scratch_shapes=[pltpu.SemaphoreType.DMA],
        compiler_params=params(),
        cost_estimate=cost(0, moved),
    )(*arrays)


def shift(v, by):
    pairs = []
    for x in range(4):
        for y in range(4):
            pairs.append(((x * 4 + y) * 2, ((x + by) % 4 * 4 + y) * 2))
            pairs.append(((x * 4 + y) * 2 + 1, (x * 4 + (y + by) % 4) * 2 + 1))
    return lax.ppermute(v, ("x", "y", "c"), pairs)


def exchange(v, by):
    pairs = []
    for x in range(4):
        for y in range(4):
            pairs.append(((x * 4 + y) * 2, (x * 4 + (y ^ by)) * 2))
            pairs.append(((x * 4 + y) * 2 + 1, ((x ^ by) * 4 + y) * 2 + 1))
    return lax.ppermute(v, ("x", "y", "c"), pairs)


def torus_gather(own, chain, first):
    count = own.shape[0]
    beside = exchange(own, 1)
    (half,) = join([2 * count], [(n, 0, count, 0, n * count) for n in range(2)], own, beside)
    across = exchange(half, 3)
    (line,) = join([4 * count], [(n, 0, 2 * count, 0, 2 * n * count) for n in range(2)], half, across)
    line_low, line_high = shift(line, 1), shift(line, -1)
    far0, far1 = join(
        [2 * count] * 2, [(0, 0, 2 * count, 0, 0), (1, 2 * count, 2 * count, 1, 0)], line_low, line_high
    )
    far0, far1 = shift(far0, 1), shift(far1, -1)
    near = (0, 1, 3, 2)
    pieces = [(first + n, k * count, chain, far, near[k]) for n, far in enumerate((0, 3, 1)) for k in range(4)]
    pieces += [(first + 3 + k // 2, k % 2 * count, chain, 2, near[k]) for k in range(4)]
    return (line, line_low, line_high, far0, far1), pieces, beside


def on_device(tokens_in, cotangent, routes, gate_weights, gate_proj, up_proj, down_proj):
    width = tokens_in.shape[1]
    hidden_width = gate_proj.shape[2]
    ix, iy, ic = lax.axis_index("x"), lax.axis_index("y"), lax.axis_index("c")
    zh, zq = lax.axis_index("zh"), lax.axis_index("zq")
    ring = zh * 2 + zq

    shard = pl.pallas_call(
        stack_kernel,
        out_shape=jax.ShapeDtypeStruct((3, *gate_proj.shape[1:]), BF),
        in_specs=[VM] * 3,
        out_specs=VM,
    )(gate_proj, up_proj, down_proj)
    other = lax.ppermute(shard, ("c", "zq"), [(2, 0), (1, 3)])
    smem = pl.BlockSpec(memory_space=pltpu.SMEM)

    def small(kernel, flag, arrays, rows):
        return pl.pallas_call(
            kernel,
            out_shape=[jax.ShapeDtypeStruct((r, hidden_width), BF) for r in rows],
            in_specs=[smem] + [VM] * len(arrays),
            out_specs=[VM] * len(rows),
            compiler_params=params(4),
        )(flag.astype(jnp.int32)[None], *arrays)

    (pair,) = small(pair_kernel, ic, (shard, other), (240,))

    def at(c, p):
        return (p // 2 * 2 + c) * 2 + p % 2

    def zmove(v, source, by):
        pairs = [(at(c, p), at(c, (p + by) % 4)) for c in range(2) for p in range(4) if (p % 2 == c) == source]
        return lax.ppermute(v, ("zh", "c", "zq"), pairs)

    source = ic == zq
    low, high = zmove(pair, True, 1), zmove(pair, True, -1)
    step = 512
    columns = pl.BlockSpec((256, step), lambda i: (0, i))
    payload, sel = pl.pallas_call(
        dispatch_kernel,
        grid=(width // step,),
        out_shape=(
            jax.ShapeDtypeStruct((8, 64, width), BF),
            jax.ShapeDtypeStruct((256, 256), BF),
        ),
        in_specs=[pl.BlockSpec((6, 256), lambda i: (0, 0)), columns, columns],
        out_specs=(
            pl.BlockSpec((8, 64, step), lambda i: (0, 0, i)),
            pl.BlockSpec((256, 256), lambda i: (0, 0)),
        ),
        compiler_params=params(56),
        cost_estimate=cost(2 * 256 * 512 * width, 8 * 256 * width),
    )(routes.T, tokens_in, cotangent)

    low, payload = lax.optimization_barrier((low, payload))
    first, top = small(near_kernel, source, (pair, low), (240, SPLIT))
    far0, far1 = zmove(top, False, 1), zmove(high[SPLIT:], False, -1)
    (second,) = small(far_kernel, source, (far0, far1, high), (240,))
    first_half = jnp.where(source, zh, jnp.where((ring == 1) | (ring == 2), 0, 1))

    arrays, pieces, near = torus_gather(first, 0, 0)
    payload, *_ = lax.optimization_barrier((payload, far0, far1, near))
    rows = lax.all_to_all(payload, ("c", "zr"), split_axis=0, concat_axis=0, tiled=True)
    second, *_ = lax.optimization_barrier((second, near))
    more_arrays, more_pieces, _ = torus_gather(second, 1, len(arrays))
    arrays, pieces = arrays + more_arrays, pieces + more_pieces

    where = jnp.stack([ix, iy, ic, first_half, lax.axis_index("zr")]).astype(jnp.int32)
    back = pl.pallas_call(
        functools.partial(expert_kernel, pieces),
        out_shape=[jax.ShapeDtypeStruct((32, width + PAD), BF)] * 8,
        in_specs=[smem] + [ANY] * (1 + len(arrays)),
        out_specs=[ANY] * 8,
        scratch_shapes=[pltpu.VMEM((width, hidden_width), BF)] * 3
        + [pltpu.VMEM((8, 32, width), BF)] * 2
        + [pltpu.VMEM((8, 32, width + PAD), BF)]
        + [pltpu.VMEM((256, hidden_width), BF)] * 2
        + [pltpu.VMEM((256, hidden_width), F32)] * 3
        + [pltpu.SemaphoreType.DMA((5,)), pltpu.SemaphoreType.DMA((2,))],
        compiler_params=params(56),
        cost_estimate=cost(10 * 256 * width * hidden_width, 6 * width * hidden_width),
    )(where, rows, *arrays)

    home = {0: back[0]}
    for r in (4, 3, 7, 2, 6, 1, 5):
        pairs = [(d, (d // 4 ^ r // 4) * 4 + (d % 4 ^ r % 4)) for d in range(8)]
        home[r] = lax.ppermute(back[r], ("c", "zr"), pairs)
    home = [home[r] for r in range(8)]

    grad_tokens, grad_gates = pl.pallas_call(
        combine_kernel,
        out_shape=(
            jax.ShapeDtypeStruct(tokens_in.shape, BF),
            jax.ShapeDtypeStruct((6, 256), BF),
        ),
        in_specs=[smem] + [VM] * 11,
        out_specs=(VM, VM),
        compiler_params=params(),
        cost_estimate=cost(2 * 256 * 256 * width, 4 * 256 * width),
    )(where, routes.T, gate_weights.T, sel, *home)
    return grad_tokens, grad_gates.T


def solution(mesh):
    fine = Mesh(mesh.devices.reshape(4, 2, 4, 2, 2, 4), AXES)
    rows = P(AXES, None)
    proj = P(("zq", "zr"), ("x", "zh", "y", "c"), None)
    return jax.shard_map(
        on_device,
        mesh=fine,
        in_specs=(rows, rows, rows, rows, proj, proj, proj),
        out_specs=(rows, rows),
        check_vma=False,
    )
```

```python
import functools

import jax
import jax.numpy as jnp
from jax import lax
from jax.experimental import pallas as pl
from jax.experimental.pallas import tpu as pltpu
from jax.sharding import Mesh, PartitionSpec as P

BF = jnp.bfloat16
F32 = jnp.float32
AXES = ("x", "zh", "y", "c", "zq", "zr")
SPLIT = 128
PAD = 128


def slots_of(routes):
    tokens = routes.shape[1]
    window = routes < 8
    owner = jnp.sum(jnp.where(window, routes, 0), axis=0, keepdims=True)
    routed = jnp.sum(jnp.where(window, 1, 0), axis=0, keepdims=True) > 0
    expert = lax.broadcasted_iota(jnp.int32, (16, tokens), 0)
    onehot = jnp.where((expert == owner) & routed, 1.0, 0.0)
    row = lax.broadcasted_iota(jnp.int32, (tokens, tokens), 0)
    col = lax.broadcasted_iota(jnp.int32, (tokens, tokens), 1)
    upto = jnp.where(row <= col, 1.0, 0.0).astype(BF)
    rank = jnp.dot(onehot.astype(BF), upto, preferred_element_type=F32)
    slot = jnp.sum(rank * onehot, axis=0, keepdims=True).astype(jnp.int32) - 1
    return jnp.where(routed, owner * 32 + slot, -1)


def dispatch_kernel(routes_ref, tok_ref, cot_ref, out_ref, sel_ref):
    tokens, step = tok_ref.shape

    @pl.when(pl.program_id(0) == 0)
    def _():
        slot = lax.broadcasted_iota(jnp.int32, (256, tokens), 0)
        sel_ref[...] = jnp.where(slot == slots_of(routes_ref[...]), 1.0, 0.0).astype(BF)

    sel = sel_ref[...]
    for source, first in ((tok_ref, 0), (cot_ref, 32)):
        rows = jnp.dot(sel, source[...], preferred_element_type=F32).astype(BF)
        out_ref[:, first : first + 32, :] = rows.reshape(8, 32, step)


def combine_kernel(where_ref, routes_ref, gates_ref, sel_ref, *refs):
    back_refs, (grad_ref, score_ref) = refs[:8], refs[8:]
    width = grad_ref.shape[1]
    window = routes_ref[...] < 8
    gate = jnp.sum(jnp.where(window, gates_ref[...].astype(F32), 0.0), axis=0, keepdims=True)
    core, place = where_ref[2], where_ref[4]
    sel = jnp.concatenate(
        [
            sel_ref[pl.ds(pl.multiple_of(partner(core, place, r) * 32, 32), 32), :]
            for r in range(8)
        ],
        axis=0,
    )
    scaled = (sel.astype(F32) * gate).astype(BF)
    down = (((0,), (0,)), ((), ()))
    step = 512

    @pl.loop(0, width // step)
    def _(i):
        cols = pl.ds(pl.multiple_of(i * step, step), step)
        rows = jnp.concatenate([ref[:, cols] for ref in back_refs], axis=0)
        grad_ref[:, cols] = lax.dot_general(
            scaled, rows, down, preferred_element_type=F32
        ).astype(BF)

    tail = jnp.concatenate([ref[:, width : width + PAD] for ref in back_refs], axis=0)
    score = lax.dot_general(tail, sel, down, preferred_element_type=F32)[0:1]
    score_ref[...] = jnp.where(window, score, 0.0).astype(BF)


def stack_kernel(gate_ref, up_ref, down_ref, out_ref):
    for m, ref in enumerate((gate_ref, up_ref, down_ref)):
        out_ref[m] = ref[0]


def pair_kernel(first_ref, shard_ref, other_ref, out_ref):
    swap = first_ref[0] == 0
    for m in range(3):
        mine, theirs = shard_ref[m], other_ref[m]
        for k in range(2):
            row = 80 * m + 40 * k
            out_ref[row : row + 40] = jnp.where(swap == (k == 0), mine, theirs)


def near_kernel(source_ref, mine, low, out_ref, top_ref):
    top_ref[...] = low[: top_ref.shape[0]]
    out_ref[...] = jnp.where(source_ref[0] == 1, mine[...], low[...])


def far_kernel(source_ref, top, bottom, high, out_ref):
    source = source_ref[0] == 1
    cut = top.shape[0]
    out_ref[:cut] = jnp.where(source, top[...], high[:cut])
    out_ref[cut:] = jnp.where(source, bottom[...], high[cut:])


def partner(core, place, r):
    return jnp.bitwise_xor(core, r // 4) * 4 + jnp.bitwise_xor(place, r % 4)


def expert_kernel(pieces, where_ref, rows_ref, *refs):
    sources = refs[: pieces[-1][0] + 1]
    out_refs = refs[len(sources) : len(sources) + 8]
    gate_w, up_w, down_w, tok_v, cot_v, result, grad_a, grad_b, pre_g, pre_u, pre_b, sems, out_sems = refs[
        len(sources) + 8 :
    ]
    my_x, my_y, core, first_half, place = (where_ref[i] for i in range(5))
    width, hidden_width = gate_w.shape

    gate_copies, up_copies, down_copies = [], [], []
    for number, row, chain, far, near in pieces:
        xx = jnp.where(core == 0, lax.rem(my_x + far, 4), jnp.bitwise_xor(my_x, near))
        yy = jnp.where(core == 0, jnp.bitwise_xor(my_y, near), lax.rem(my_y + far, 4))
        half = first_half if chain == 0 else 1 - first_half
        target = pl.multiple_of(((xx * 2 + half) * 4 + yy) * 80, 16)
        for m, (weights, copies) in enumerate(
            ((gate_w, gate_copies), (up_w, up_copies), (down_w, down_copies))
        ):
            copies.append(
                pltpu.make_async_copy(
                    sources[number].at[pl.ds(row + 80 * m, 80), :],
                    weights.at[pl.ds(target, 80), :],
                    sems.at[m],
                )
            )
    down_copies.append(pltpu.make_async_copy(rows_ref.at[:, pl.ds(32, 32), :], cot_v, sems.at[3]))
    gate_copies.append(pltpu.make_async_copy(rows_ref.at[:, pl.ds(0, 32), :], tok_v, sems.at[4]))
    for copies in (down_copies, gate_copies, up_copies):
        for copy in copies:
            copy.start()

    for copy in down_copies:
        copy.wait()
    cot = cot_v[...].reshape(256, width)
    pre_b[...] = jnp.dot(cot, down_w[...], preferred_element_type=F32)
    for copy in gate_copies:
        copy.wait()
    tok = tok_v[...].reshape(256, width)
    pre_g[...] = jnp.dot(tok, gate_w[...], preferred_element_type=F32)
    for copy in up_copies:
        copy.wait()
    pre_u[...] = jnp.dot(tok, up_w[...], preferred_element_type=F32)

    cstep = 256

    def middle(i, score):
        cols = pl.ds(pl.multiple_of(i * cstep, cstep), cstep)
        gate, up, back_hidden = pre_g[:, cols], pre_u[:, cols], pre_b[:, cols]
        sig = jax.nn.sigmoid(gate)
        act = gate * sig
        hidden = (act * up).astype(BF).astype(F32)
        grad_a[:, cols] = (back_hidden * up * (sig * (1.0 + gate * (1.0 - sig)))).astype(BF)
        grad_b[:, cols] = (back_hidden * act).astype(BF)
        return score + jnp.sum(hidden * back_hidden, axis=1, keepdims=True)

    score = lax.fori_loop(0, hidden_width // cstep, middle, jnp.zeros((256, 1), F32))
    result[:, :, width : width + PAD] = (
        jnp.broadcast_to(score, (256, PAD)).astype(BF).reshape(8, 32, PAD)
    )

    a, b = grad_a[...], grad_b[...]
    dims = (((1,), (1,)), ((), ()))
    dstep = width // 2
    outs = []
    for i in range(2):
        rows = lax.dot_general(a, gate_w[i * dstep : (i + 1) * dstep, :], dims, preferred_element_type=F32)
        rows = rows + lax.dot_general(b, up_w[i * dstep : (i + 1) * dstep, :], dims, preferred_element_type=F32)
        result[:, :, i * dstep : (i + 1) * dstep] = rows.astype(BF).reshape(8, 32, dstep)
        part = pl.ds(i * dstep, dstep if i == 0 else dstep + PAD)
        for r, out_ref in enumerate(out_refs):
            copy = pltpu.make_async_copy(
                result.at[partner(core, place, r), :, part], out_ref.at[:, part], out_sems.at[i]
            )
            copy.start()
            outs.append(copy)
    for copy in outs:
        copy.wait()


def params(mib=16):
    return pltpu.CompilerParams(vmem_limit_bytes=mib * 1024 * 1024)


def cost(flops, moved):
    return pl.CostEstimate(flops=flops, bytes_accessed=moved, transcendentals=0)


VM = pl.BlockSpec(memory_space=pltpu.VMEM)
ANY = pl.BlockSpec(memory_space=pl.ANY)


def join_kernel(plan, inputs, *refs):
    sources, targets, sem = refs[:inputs], refs[inputs:-1], refs[-1]
    copies = [
        pltpu.make_async_copy(
            sources[i].at[pl.ds(row, count), :], targets[o].at[pl.ds(at, count), :], sem
        )
        for i, row, count, o, at in plan
    ]
    for copy in copies:
        copy.start()
    for copy in copies:
        copy.wait()


def join(rows, plan, *arrays):
    width = arrays[0].shape[1]
    moved = 4 * sum(rows) * width
    return pl.pallas_call(
        functools.partial(join_kernel, plan, len(arrays)),
        out_shape=[jax.ShapeDtypeStruct((r, width), BF) for r in rows],
        in_specs=[ANY] * len(arrays),
        out_specs=[ANY] * len(rows),
        scratch_shapes=[pltpu.SemaphoreType.DMA],
        compiler_params=params(),
        cost_estimate=cost(0, moved),
    )(*arrays)


def shift(v, by):
    pairs = []
    for x in range(4):
        for y in range(4):
            pairs.append(((x * 4 + y) * 2, ((x + by) % 4 * 4 + y) * 2))
            pairs.append(((x * 4 + y) * 2 + 1, (x * 4 + (y + by) % 4) * 2 + 1))
    return lax.ppermute(v, ("x", "y", "c"), pairs)


def exchange(v, by):
    pairs = []
    for x in range(4):
        for y in range(4):
            pairs.append(((x * 4 + y) * 2, (x * 4 + (y ^ by)) * 2))
            pairs.append(((x * 4 + y) * 2 + 1, ((x ^ by) * 4 + y) * 2 + 1))
    return lax.ppermute(v, ("x", "y", "c"), pairs)


def torus_gather(own, chain, first):
    count = own.shape[0]
    beside = exchange(own, 1)
    (half,) = join([2 * count], [(n, 0, count, 0, n * count) for n in range(2)], own, beside)
    across = exchange(half, 3)
    half_low, half_high = shift(half, 1), shift(half, -1)
    across_high, across_low = shift(across, -1), shift(across, 1)
    half_far, across_far = shift(half_low, 1), shift(across_high, -1)
    arrays = (half, across, half_low, across_low, half_high, across_high, half_far, across_far)
    fars = (0, 0, 3, 3, 1, 1, 2, 2)
    near = (0, 1, 3, 2)
    pieces = [
        (first + n, k * count, chain, fars[n], near[n % 2 * 2 + k]) for n in range(8) for k in range(2)
    ]
    return arrays, pieces, beside


def on_device(tokens_in, cotangent, routes, gate_weights, gate_proj, up_proj, down_proj):
    width = tokens_in.shape[1]
    hidden_width = gate_proj.shape[2]
    ix, iy, ic = lax.axis_index("x"), lax.axis_index("y"), lax.axis_index("c")
    zh, zq = lax.axis_index("zh"), lax.axis_index("zq")
    ring = zh * 2 + zq

    shard = pl.pallas_call(
        stack_kernel,
        out_shape=jax.ShapeDtypeStruct((3, *gate_proj.shape[1:]), BF),
        in_specs=[VM] * 3,
        out_specs=VM,
    )(gate_proj, up_proj, down_proj)
    other = lax.ppermute(shard, ("c", "zq"), [(2, 0), (1, 3)])
    smem = pl.BlockSpec(memory_space=pltpu.SMEM)

    def small(kernel, flag, arrays, rows):
        return pl.pallas_call(
            kernel,
            out_shape=[jax.ShapeDtypeStruct((r, hidden_width), BF) for r in rows],
            in_specs=[smem] + [VM] * len(arrays),
            out_specs=[VM] * len(rows),
            compiler_params=params(4),
        )(flag.astype(jnp.int32)[None], *arrays)

    (pair,) = small(pair_kernel, ic, (shard, other), (240,))

    def at(c, p):
        return (p // 2 * 2 + c) * 2 + p % 2

    def zmove(v, source, by):
        pairs = [(at(c, p), at(c, (p + by) % 4)) for c in range(2) for p in range(4) if (p % 2 == c) == source]
        return lax.ppermute(v, ("zh", "c", "zq"), pairs)

    source = ic == zq
    low, high = zmove(pair, True, 1), zmove(pair, True, -1)
    step = 512
    columns = pl.BlockSpec((256, step), lambda i: (0, i))
    payload, sel = pl.pallas_call(
        dispatch_kernel,
        grid=(width // step,),
        out_shape=(
            jax.ShapeDtypeStruct((8, 64, width), BF),
            jax.ShapeDtypeStruct((256, 256), BF),
        ),
        in_specs=[pl.BlockSpec((6, 256), lambda i: (0, 0)), columns, columns],
        out_specs=(
            pl.BlockSpec((8, 64, step), lambda i: (0, 0, i)),
            pl.BlockSpec((256, 256), lambda i: (0, 0)),
        ),
        compiler_params=params(56),
        cost_estimate=cost(2 * 256 * 512 * width, 8 * 256 * width),
    )(routes.T, tokens_in, cotangent)

    low, payload = lax.optimization_barrier((low, payload))
    first, top = small(near_kernel, source, (pair, low), (240, SPLIT))
    far0, far1 = zmove(top, False, 1), zmove(high[SPLIT:], False, -1)
    (second,) = small(far_kernel, source, (far0, far1, high), (240,))
    first_half = jnp.where(source, zh, jnp.where((ring == 1) | (ring == 2), 0, 1))

    arrays, pieces, near = torus_gather(first, 0, 0)
    payload, *_ = lax.optimization_barrier((payload, far0, far1, near))
    rows = lax.all_to_all(payload, ("c", "zr"), split_axis=0, concat_axis=0, tiled=True)
    second, *_ = lax.optimization_barrier((second, near))
    more_arrays, more_pieces, _ = torus_gather(second, 1, len(arrays))
    arrays, pieces = arrays + more_arrays, pieces + more_pieces

    where = jnp.stack([ix, iy, ic, first_half, lax.axis_index("zr")]).astype(jnp.int32)
    back = pl.pallas_call(
        functools.partial(expert_kernel, pieces),
        out_shape=[jax.ShapeDtypeStruct((32, width + PAD), BF)] * 8,
        in_specs=[smem] + [ANY] * (1 + len(arrays)),
        out_specs=[ANY] * 8,
        scratch_shapes=[pltpu.VMEM((width, hidden_width), BF)] * 3
        + [pltpu.VMEM((8, 32, width), BF)] * 2
        + [pltpu.VMEM((8, 32, width + PAD), BF)]
        + [pltpu.VMEM((256, hidden_width), BF)] * 2
        + [pltpu.VMEM((256, hidden_width), F32)] * 3
        + [pltpu.SemaphoreType.DMA((5,)), pltpu.SemaphoreType.DMA((2,))],
        compiler_params=params(56),
        cost_estimate=cost(10 * 256 * width * hidden_width, 6 * width * hidden_width),
    )(where, rows, *arrays)

    home = {0: back[0]}
    for r in (4, 3, 7, 2, 6, 1, 5):
        pairs = [(d, (d // 4 ^ r // 4) * 4 + (d % 4 ^ r % 4)) for d in range(8)]
        home[r] = lax.ppermute(back[r], ("c", "zr"), pairs)
    home = [home[r] for r in range(8)]

    grad_tokens, grad_gates = pl.pallas_call(
        combine_kernel,
        out_shape=(
            jax.ShapeDtypeStruct(tokens_in.shape, BF),
            jax.ShapeDtypeStruct((6, 256), BF),
        ),
        in_specs=[smem] + [VM] * 11,
        out_specs=(VM, VM),
        compiler_params=params(),
        cost_estimate=cost(2 * 256 * 256 * width, 4 * 256 * width),
    )(where, routes.T, gate_weights.T, sel, *home)
    return grad_tokens, grad_gates.T


def solution(mesh):
    fine = Mesh(mesh.devices.reshape(4, 2, 4, 2, 2, 4), AXES)
    rows = P(AXES, None)
    proj = P(("zq", "zr"), ("x", "zh", "y", "c"), None)
    return jax.shard_map(
        on_device,
        mesh=fine,
        in_specs=(rows, rows, rows, rows, proj, proj, proj),
        out_specs=(rows, rows),
        check_vma=False,
    )
```

```python
import functools

import jax
import jax.numpy as jnp
from jax import lax
from jax.experimental import pallas as pl
from jax.experimental.pallas import tpu as pltpu
from jax.sharding import Mesh, PartitionSpec as P

BF = jnp.bfloat16
F32 = jnp.float32
AXES = ("x", "zh", "y", "c", "zq", "zr")
SPLIT = 128
PAD = 128


def slots_of(routes):
    tokens = routes.shape[1]
    window = routes < 8
    owner = jnp.sum(jnp.where(window, routes, 0), axis=0, keepdims=True)
    routed = jnp.sum(jnp.where(window, 1, 0), axis=0, keepdims=True) > 0
    expert = lax.broadcasted_iota(jnp.int32, (16, tokens), 0)
    onehot = jnp.where((expert == owner) & routed, 1.0, 0.0)
    row = lax.broadcasted_iota(jnp.int32, (tokens, tokens), 0)
    col = lax.broadcasted_iota(jnp.int32, (tokens, tokens), 1)
    upto = jnp.where(row <= col, 1.0, 0.0).astype(BF)
    rank = jnp.dot(onehot.astype(BF), upto, preferred_element_type=F32)
    slot = jnp.sum(rank * onehot, axis=0, keepdims=True).astype(jnp.int32) - 1
    return jnp.where(routed, owner * 32 + slot, -1)


def dispatch_kernel(routes_ref, tok_ref, cot_ref, out_ref, sel_ref):
    tokens, step = tok_ref.shape

    @pl.when(pl.program_id(0) == 0)
    def _():
        slot = lax.broadcasted_iota(jnp.int32, (256, tokens), 0)
        sel_ref[...] = jnp.where(slot == slots_of(routes_ref[...]), 1.0, 0.0).astype(BF)

    sel = sel_ref[...]
    for source, first in ((tok_ref, 0), (cot_ref, 32)):
        rows = jnp.dot(sel, source[...], preferred_element_type=F32).astype(BF)
        out_ref[:, first : first + 32, :] = rows.reshape(8, 32, step)


def combine_kernel(where_ref, routes_ref, gates_ref, sel_ref, *refs):
    back_refs, (grad_ref, score_ref) = refs[:8], refs[8:]
    width = grad_ref.shape[1]
    window = routes_ref[...] < 8
    gate = jnp.sum(jnp.where(window, gates_ref[...].astype(F32), 0.0), axis=0, keepdims=True)
    core, place = where_ref[2], where_ref[4]
    sel = jnp.concatenate(
        [
            sel_ref[pl.ds(pl.multiple_of(partner(core, place, r) * 32, 32), 32), :]
            for r in range(8)
        ],
        axis=0,
    )
    scaled = (sel.astype(F32) * gate).astype(BF)
    down = (((0,), (0,)), ((), ()))
    step = 512

    @pl.loop(0, width // step)
    def _(i):
        cols = pl.ds(pl.multiple_of(i * step, step), step)
        rows = jnp.concatenate([ref[:, cols] for ref in back_refs], axis=0)
        grad_ref[:, cols] = lax.dot_general(
            scaled, rows, down, preferred_element_type=F32
        ).astype(BF)

    tail = jnp.concatenate([ref[:, width : width + PAD] for ref in back_refs], axis=0)
    score = lax.dot_general(tail, sel, down, preferred_element_type=F32)[0:1]
    score_ref[...] = jnp.where(window, score, 0.0).astype(BF)


def stack_kernel(gate_ref, up_ref, down_ref, out_ref):
    for m, ref in enumerate((gate_ref, up_ref, down_ref)):
        out_ref[m] = ref[0]


def pair_kernel(first_ref, shard_ref, other_ref, out_ref):
    swap = first_ref[0] == 0
    for m in range(3):
        mine, theirs = shard_ref[m], other_ref[m]
        for k in range(2):
            row = 80 * m + 40 * k
            out_ref[row : row + 40] = jnp.where(swap == (k == 0), mine, theirs)


def near_kernel(source_ref, mine, low, out_ref, top_ref):
    top_ref[...] = low[: top_ref.shape[0]]
    out_ref[...] = jnp.where(source_ref[0] == 1, mine[...], low[...])


def far_kernel(source_ref, top, bottom, high, out_ref):
    source = source_ref[0] == 1
    cut = top.shape[0]
    out_ref[:cut] = jnp.where(source, top[...], high[:cut])
    out_ref[cut:] = jnp.where(source, bottom[...], high[cut:])


def partner(core, place, r):
    return jnp.bitwise_xor(core, r // 4) * 4 + jnp.bitwise_xor(place, r % 4)


def expert_kernel(pieces, where_ref, rows_ref, *refs):
    sources = refs[: pieces[-1][0] + 1]
    out_refs = refs[len(sources) : len(sources) + 8]
    gate_w, up_w, down_w, tok_v, cot_v, result, grad_a, grad_b, pre_g, pre_u, pre_b, sems, out_sems = refs[
        len(sources) + 8 :
    ]
    my_x, my_y, core, first_half, place = (where_ref[i] for i in range(5))
    width, hidden_width = gate_w.shape

    gate_copies, up_copies, down_copies = [], [], []
    for number, row, chain, far, near in pieces:
        xx = lax.rem(my_x + jnp.where(core == 0, far, near), 4)
        yy = lax.rem(my_y + jnp.where(core == 0, near, far), 4)
        half = first_half if chain == 0 else 1 - first_half
        target = pl.multiple_of(((xx * 2 + half) * 4 + yy) * 80, 16)
        for m, (weights, copies) in enumerate(
            ((gate_w, gate_copies), (up_w, up_copies), (down_w, down_copies))
        ):
            copies.append(
                pltpu.make_async_copy(
                    sources[number].at[pl.ds(row + 80 * m, 80), :],
                    weights.at[pl.ds(target, 80), :],
                    sems.at[m],
                )
            )
    down_copies.append(pltpu.make_async_copy(rows_ref.at[:, pl.ds(32, 32), :], cot_v, sems.at[3]))
    gate_copies.append(pltpu.make_async_copy(rows_ref.at[:, pl.ds(0, 32), :], tok_v, sems.at[4]))
    for copies in (down_copies, gate_copies, up_copies):
        for copy in copies:
            copy.start()

    for copy in down_copies:
        copy.wait()
    cot = cot_v[...].reshape(256, width)
    pre_b[...] = jnp.dot(cot, down_w[...], preferred_element_type=F32)
    for copy in gate_copies:
        copy.wait()
    tok = tok_v[...].reshape(256, width)
    pre_g[...] = jnp.dot(tok, gate_w[...], preferred_element_type=F32)
    for copy in up_copies:
        copy.wait()
    pre_u[...] = jnp.dot(tok, up_w[...], preferred_element_type=F32)

    cstep = 256

    def middle(i, score):
        cols = pl.ds(pl.multiple_of(i * cstep, cstep), cstep)
        gate, up, back_hidden = pre_g[:, cols], pre_u[:, cols], pre_b[:, cols]
        sig = jax.nn.sigmoid(gate)
        act = gate * sig
        hidden = (act * up).astype(BF).astype(F32)
        grad_a[:, cols] = (back_hidden * up * (sig * (1.0 + gate * (1.0 - sig)))).astype(BF)
        grad_b[:, cols] = (back_hidden * act).astype(BF)
        return score + jnp.sum(hidden * back_hidden, axis=1, keepdims=True)

    score = lax.fori_loop(0, hidden_width // cstep, middle, jnp.zeros((256, 1), F32))
    result[:, :, width : width + PAD] = (
        jnp.broadcast_to(score, (256, PAD)).astype(BF).reshape(8, 32, PAD)
    )

    a, b = grad_a[...], grad_b[...]
    dims = (((1,), (1,)), ((), ()))
    dstep = width // 2
    outs = []
    for i in range(2):
        rows = lax.dot_general(a, gate_w[i * dstep : (i + 1) * dstep, :], dims, preferred_element_type=F32)
        rows = rows + lax.dot_general(b, up_w[i * dstep : (i + 1) * dstep, :], dims, preferred_element_type=F32)
        result[:, :, i * dstep : (i + 1) * dstep] = rows.astype(BF).reshape(8, 32, dstep)
        part = pl.ds(i * dstep, dstep if i == 0 else dstep + PAD)
        for r, out_ref in enumerate(out_refs):
            copy = pltpu.make_async_copy(
                result.at[partner(core, place, r), :, part], out_ref.at[:, part], out_sems.at[i]
            )
            copy.start()
            outs.append(copy)
    for copy in outs:
        copy.wait()


def params(mib=16):
    return pltpu.CompilerParams(vmem_limit_bytes=mib * 1024 * 1024)


def cost(flops, moved):
    return pl.CostEstimate(flops=flops, bytes_accessed=moved, transcendentals=0)


VM = pl.BlockSpec(memory_space=pltpu.VMEM)
ANY = pl.BlockSpec(memory_space=pl.ANY)


def join_kernel(plan, inputs, *refs):
    sources, targets, sem = refs[:inputs], refs[inputs:-1], refs[-1]
    copies = [
        pltpu.make_async_copy(
            sources[i].at[pl.ds(row, count), :], targets[o].at[pl.ds(at, count), :], sem
        )
        for i, row, count, o, at in plan
    ]
    for copy in copies:
        copy.start()
    for copy in copies:
        copy.wait()


def join(rows, plan, *arrays):
    width = arrays[0].shape[1]
    moved = 4 * sum(rows) * width
    return pl.pallas_call(
        functools.partial(join_kernel, plan, len(arrays)),
        out_shape=[jax.ShapeDtypeStruct((r, width), BF) for r in rows],
        in_specs=[ANY] * len(arrays),
        out_specs=[ANY] * len(rows),
        scratch_shapes=[pltpu.SemaphoreType.DMA],
        compiler_params=params(),
        cost_estimate=cost(0, moved),
    )(*arrays)


def shift(v, far, by):
    pairs = []
    for x in range(4):
        for y in range(4):
            for c in range(2):
                along_x = (c == 0) == far
                tx, ty = ((x + by) % 4, y) if along_x else (x, (y + by) % 4)
                pairs.append(((x * 4 + y) * 2 + c, (tx * 4 + ty) * 2 + c))
    return lax.ppermute(v, ("x", "y", "c"), pairs)


def torus_gather(own, chain, first):
    count = own.shape[0]
    low, high = shift(own, False, 1), shift(own, False, -1)
    opposite = shift(low, False, 1)
    (line,) = join(
        [4 * count], [(n, 0, count, 0, n * count) for n in range(4)], own, low, high, opposite
    )
    line_low, line_high = shift(line, True, 1), shift(line, True, -1)
    far0, far1 = join(
        [2 * count] * 2, [(0, 0, 2 * count, 0, 0), (1, 2 * count, 2 * count, 1, 0)], line_low, line_high
    )
    far0, far1 = shift(far0, True, 1), shift(far1, True, -1)
    near = (0, 3, 1, 2)
    pieces = [(first + n, k * count, chain, far, near[k]) for n, far in enumerate((0, 3, 1)) for k in range(4)]
    pieces += [(first + 3 + k // 2, k % 2 * count, chain, 2, near[k]) for k in range(4)]
    return (line, line_low, line_high, far0, far1), pieces, (low, high, opposite)


def on_device(tokens_in, cotangent, routes, gate_weights, gate_proj, up_proj, down_proj):
    width = tokens_in.shape[1]
    hidden_width = gate_proj.shape[2]
    ix, iy, ic = lax.axis_index("x"), lax.axis_index("y"), lax.axis_index("c")
    zh, zq = lax.axis_index("zh"), lax.axis_index("zq")
    ring = zh * 2 + zq

    shard = pl.pallas_call(
        stack_kernel,
        out_shape=jax.ShapeDtypeStruct((3, *gate_proj.shape[1:]), BF),
        in_specs=[VM] * 3,
        out_specs=VM,
    )(gate_proj, up_proj, down_proj)
    other = lax.ppermute(shard, ("c", "zq"), [(2, 0), (1, 3)])
    smem = pl.BlockSpec(memory_space=pltpu.SMEM)

    def small(kernel, flag, arrays, rows):
        return pl.pallas_call(
            kernel,
            out_shape=[jax.ShapeDtypeStruct((r, hidden_width), BF) for r in rows],
            in_specs=[smem] + [VM] * len(arrays),
            out_specs=[VM] * len(rows),
            compiler_params=params(4),
        )(flag.astype(jnp.int32)[None], *arrays)

    (pair,) = small(pair_kernel, ic, (shard, other), (240,))

    def at(c, p):
        return (p // 2 * 2 + c) * 2 + p % 2

    def zmove(v, source, by):
        pairs = [(at(c, p), at(c, (p + by) % 4)) for c in range(2) for p in range(4) if (p % 2 == c) == source]
        return lax.ppermute(v, ("zh", "c", "zq"), pairs)

    source = ic == zq
    low, high = zmove(pair, True, 1), zmove(pair, True, -1)
    step = 512
    columns = pl.BlockSpec((256, step), lambda i: (0, i))
    payload, sel = pl.pallas_call(
        dispatch_kernel,
        grid=(width // step,),
        out_shape=(
            jax.ShapeDtypeStruct((8, 64, width), BF),
            jax.ShapeDtypeStruct((256, 256), BF),
        ),
        in_specs=[pl.BlockSpec((6, 256), lambda i: (0, 0)), columns, columns],
        out_specs=(
            pl.BlockSpec((8, 64, step), lambda i: (0, 0, i)),
            pl.BlockSpec((256, 256), lambda i: (0, 0)),
        ),
        compiler_params=params(56),
        cost_estimate=cost(2 * 256 * 512 * width, 8 * 256 * width),
    )(routes.T, tokens_in, cotangent)

    low, payload = lax.optimization_barrier((low, payload))
    first, top = small(near_kernel, source, (pair, low), (240, SPLIT))
    far0, far1 = zmove(top, False, 1), zmove(high[SPLIT:], False, -1)
    (second,) = small(far_kernel, source, (far0, far1, high), (240,))
    first_half = jnp.where(source, zh, jnp.where((ring == 1) | (ring == 2), 0, 1))

    arrays, pieces, near = torus_gather(first, 0, 0)
    payload, *_ = lax.optimization_barrier((payload, far0, far1, *near[:2]))
    rows = lax.all_to_all(payload, ("c", "zr"), split_axis=0, concat_axis=0, tiled=True)
    second, *_ = lax.optimization_barrier((second, *near[:2]))
    more_arrays, more_pieces, _ = torus_gather(second, 1, len(arrays))
    arrays, pieces = arrays + more_arrays, pieces + more_pieces

    where = jnp.stack([ix, iy, ic, first_half, lax.axis_index("zr")]).astype(jnp.int32)
    back = pl.pallas_call(
        functools.partial(expert_kernel, pieces),
        out_shape=[jax.ShapeDtypeStruct((32, width + PAD), BF)] * 8,
        in_specs=[smem] + [ANY] * (1 + len(arrays)),
        out_specs=[ANY] * 8,
        scratch_shapes=[pltpu.VMEM((width, hidden_width), BF)] * 3
        + [pltpu.VMEM((8, 32, width), BF)] * 2
        + [pltpu.VMEM((8, 32, width + PAD), BF)]
        + [pltpu.VMEM((256, hidden_width), BF)] * 2
        + [pltpu.VMEM((256, hidden_width), F32)] * 3
        + [pltpu.SemaphoreType.DMA((5,)), pltpu.SemaphoreType.DMA((2,))],
        compiler_params=params(56),
        cost_estimate=cost(10 * 256 * width * hidden_width, 6 * width * hidden_width),
    )(where, rows, *arrays)

    home = {0: back[0]}
    for r in (4, 3, 7, 2, 6, 1, 5):
        pairs = [(d, (d // 4 ^ r // 4) * 4 + (d % 4 ^ r % 4)) for d in range(8)]
        home[r] = lax.ppermute(back[r], ("c", "zr"), pairs)
    home = [home[r] for r in range(8)]

    grad_tokens, grad_gates = pl.pallas_call(
        combine_kernel,
        out_shape=(
            jax.ShapeDtypeStruct(tokens_in.shape, BF),
            jax.ShapeDtypeStruct((6, 256), BF),
        ),
        in_specs=[smem] + [VM] * 11,
        out_specs=(VM, VM),
        compiler_params=params(),
        cost_estimate=cost(2 * 256 * 256 * width, 4 * 256 * width),
    )(where, routes.T, gate_weights.T, sel, *home)
    return grad_tokens, grad_gates.T


def solution(mesh):
    fine = Mesh(mesh.devices.reshape(4, 2, 4, 2, 2, 4), AXES)
    rows = P(AXES, None)
    proj = P(("zq", "zr"), ("x", "zh", "y", "c"), None)
    return jax.shard_map(
        on_device,
        mesh=fine,
        in_specs=(rows, rows, rows, rows, proj, proj, proj),
        out_specs=(rows, rows),
        check_vma=False,
    )
```

```python
import functools

import jax
import jax.numpy as jnp
from jax import lax
from jax.experimental import pallas as pl
from jax.experimental.pallas import tpu as pltpu
from jax.sharding import Mesh, PartitionSpec as P

BF = jnp.bfloat16
F32 = jnp.float32
AXES = ("x", "zh", "y", "c", "zq", "zr")
SPLIT = 128
PAD = 128


def slots_of(routes):
    tokens = routes.shape[1]
    window = routes < 8
    owner = jnp.sum(jnp.where(window, routes, 0), axis=0, keepdims=True)
    routed = jnp.sum(jnp.where(window, 1, 0), axis=0, keepdims=True) > 0
    expert = lax.broadcasted_iota(jnp.int32, (16, tokens), 0)
    onehot = jnp.where((expert == owner) & routed, 1.0, 0.0)
    row = lax.broadcasted_iota(jnp.int32, (tokens, tokens), 0)
    col = lax.broadcasted_iota(jnp.int32, (tokens, tokens), 1)
    upto = jnp.where(row <= col, 1.0, 0.0).astype(BF)
    rank = jnp.dot(onehot.astype(BF), upto, preferred_element_type=F32)
    slot = jnp.sum(rank * onehot, axis=0, keepdims=True).astype(jnp.int32) - 1
    return jnp.where(routed, owner * 32 + slot, -1)


def dispatch_kernel(routes_ref, tok_ref, cot_ref, out_ref, sel_ref):
    tokens, step = tok_ref.shape

    @pl.when(pl.program_id(0) == 0)
    def _():
        slot = lax.broadcasted_iota(jnp.int32, (256, tokens), 0)
        sel_ref[...] = jnp.where(slot == slots_of(routes_ref[...]), 1.0, 0.0).astype(BF)

    sel = sel_ref[...]
    for source, first in ((tok_ref, 0), (cot_ref, 32)):
        rows = jnp.dot(sel, source[...], preferred_element_type=F32).astype(BF)
        out_ref[:, first : first + 32, :] = rows.reshape(8, 32, step)


def copy_kernel(in_ref, out_ref):
    out_ref[...] = in_ref[...]


def combine_kernel(where_ref, routes_ref, gates_ref, sel_ref, *refs):
    back_refs, (grad_ref, score_ref) = refs[:8], refs[8:]
    width = grad_ref.shape[1]
    window = routes_ref[...] < 8
    gate = jnp.sum(jnp.where(window, gates_ref[...].astype(F32), 0.0), axis=0, keepdims=True)
    core, place = where_ref[2], where_ref[4]
    sel = jnp.concatenate(
        [
            sel_ref[pl.ds(pl.multiple_of(partner(core, place, r) * 32, 32), 32), :]
            for r in range(8)
        ],
        axis=0,
    )
    scaled = (sel.astype(F32) * gate).astype(BF)
    down = (((0,), (0,)), ((), ()))
    step = 512

    @pl.loop(0, width // step)
    def _(i):
        cols = pl.ds(pl.multiple_of(i * step, step), step)
        rows = jnp.concatenate([ref[:, cols] for ref in back_refs], axis=0)
        grad_ref[:, cols] = lax.dot_general(
            scaled, rows, down, preferred_element_type=F32
        ).astype(BF)

    tail = jnp.concatenate([ref[:, width : width + PAD] for ref in back_refs], axis=0)
    score = lax.dot_general(tail, sel, down, preferred_element_type=F32)[0:1]
    score_ref[...] = jnp.where(window, score, 0.0).astype(BF)


def stack_kernel(gate_ref, up_ref, down_ref, out_ref):
    for m, ref in enumerate((gate_ref, up_ref, down_ref)):
        out_ref[m] = ref[0]


def pair_kernel(first_ref, shard_ref, other_ref, out_ref):
    swap = first_ref[0] == 0
    for m in range(3):
        mine, theirs = shard_ref[m], other_ref[m]
        for k in range(2):
            row = 80 * m + 40 * k
            out_ref[row : row + 40] = jnp.where(swap == (k == 0), mine, theirs)


def near_kernel(source_ref, mine, low, out_ref, top_ref):
    top_ref[...] = low[: top_ref.shape[0]]
    out_ref[...] = jnp.where(source_ref[0] == 1, mine[...], low[...])


def far_kernel(source_ref, top, bottom, high, out_ref):
    source = source_ref[0] == 1
    cut = top.shape[0]
    out_ref[:cut] = jnp.where(source, top[...], high[:cut])
    out_ref[cut:] = jnp.where(source, bottom[...], high[cut:])


def partner(core, place, r):
    return jnp.bitwise_xor(core, r // 4) * 4 + jnp.bitwise_xor(place, r % 4)


def expert_kernel(pieces, where_ref, rows_ref, *refs):
    sources = refs[: pieces[-1][0] + 1]
    out_refs = refs[len(sources) : len(sources) + 8]
    gate_w, up_w, down_w, tok_v, cot_v, result, grad_a, grad_b, pre_g, pre_u, pre_b, slope, sems, out_sems = refs[
        len(sources) + 8 :
    ]
    my_x, my_y, core, first_half, place = (where_ref[i] for i in range(5))
    width, hidden_width = gate_w.shape

    gate_copies, up_copies, down_copies = [], [], []
    for number, row, chain, far, near in pieces:
        xx = lax.rem(my_x + jnp.where(core == 0, far, near), 4)
        yy = lax.rem(my_y + jnp.where(core == 0, near, far), 4)
        half = first_half if chain == 0 else 1 - first_half
        target = pl.multiple_of(((xx * 2 + half) * 4 + yy) * 80, 16)
        for m, (weights, copies) in enumerate(
            ((gate_w, gate_copies), (up_w, up_copies), (down_w, down_copies))
        ):
            copies.append(
                pltpu.make_async_copy(
                    sources[number].at[pl.ds(row + 80 * m, 80), :],
                    weights.at[pl.ds(target, 80), :],
                    sems.at[m],
                )
            )
    down_copies.append(pltpu.make_async_copy(rows_ref.at[:, pl.ds(32, 32), :], cot_v, sems.at[3]))
    gate_copies.append(pltpu.make_async_copy(rows_ref.at[:, pl.ds(0, 32), :], tok_v, sems.at[4]))
    for copies in (down_copies, gate_copies, up_copies):
        for copy in copies:
            copy.start()

    for copy in down_copies:
        copy.wait()
    cot = cot_v[...].reshape(256, width)
    pre_b[...] = jnp.dot(cot, down_w[...], preferred_element_type=F32)
    for copy in gate_copies:
        copy.wait()
    tok = tok_v[...].reshape(256, width)
    pre_g[...] = jnp.dot(tok, gate_w[...], preferred_element_type=F32)
    cstep = 256

    @pl.loop(0, hidden_width // cstep)
    def _(i):
        cols = pl.ds(pl.multiple_of(i * cstep, cstep), cstep)
        gate, back_hidden = pre_g[:, cols], pre_b[:, cols]
        sig = jax.nn.sigmoid(gate)
        act = gate * sig
        grad_b[:, cols] = (back_hidden * act).astype(BF)
        slope[:, cols] = sig * (1.0 + gate * (1.0 - sig))
        pre_g[:, cols] = act

    for copy in up_copies:
        copy.wait()
    pre_u[...] = jnp.dot(tok, up_w[...], preferred_element_type=F32)

    def middle(i, score):
        cols = pl.ds(pl.multiple_of(i * cstep, cstep), cstep)
        act, up, back_hidden = pre_g[:, cols], pre_u[:, cols], pre_b[:, cols]
        hidden = (act * up).astype(BF).astype(F32)
        grad_a[:, cols] = (back_hidden * up * slope[:, cols]).astype(BF)
        return score + jnp.sum(hidden * back_hidden, axis=1, keepdims=True)

    score = lax.fori_loop(0, hidden_width // cstep, middle, jnp.zeros((256, 1), F32))
    result[:, :, width : width + PAD] = (
        jnp.broadcast_to(score, (256, PAD)).astype(BF).reshape(8, 32, PAD)
    )

    a, b = grad_a[...], grad_b[...]
    dims = (((1,), (1,)), ((), ()))
    dstep = width // 2
    outs = []
    for i in range(2):
        rows = lax.dot_general(a, gate_w[i * dstep : (i + 1) * dstep, :], dims, preferred_element_type=F32)
        rows = rows + lax.dot_general(b, up_w[i * dstep : (i + 1) * dstep, :], dims, preferred_element_type=F32)
        result[:, :, i * dstep : (i + 1) * dstep] = rows.astype(BF).reshape(8, 32, dstep)
        part = pl.ds(i * dstep, dstep if i == 0 else dstep + PAD)
        for r, out_ref in enumerate(out_refs):
            copy = pltpu.make_async_copy(
                result.at[partner(core, place, r), :, part], out_ref.at[:, part], out_sems.at[i]
            )
            copy.start()
            outs.append(copy)
    for copy in outs:
        copy.wait()


def params(mib=16):
    return pltpu.CompilerParams(vmem_limit_bytes=mib * 1024 * 1024)


def cost(flops, moved):
    return pl.CostEstimate(flops=flops, bytes_accessed=moved, transcendentals=0)


VM = pl.BlockSpec(memory_space=pltpu.VMEM)
ANY = pl.BlockSpec(memory_space=pl.ANY)


def join_kernel(plan, inputs, *refs):
    sources, targets, sem = refs[:inputs], refs[inputs:-1], refs[-1]
    copies = [
        pltpu.make_async_copy(
            sources[i].at[pl.ds(row, count), :], targets[o].at[pl.ds(at, count), :], sem
        )
        for i, row, count, o, at in plan
    ]
    for copy in copies:
        copy.start()
    for copy in copies:
        copy.wait()


def join(rows, plan, *arrays):
    width = arrays[0].shape[1]
    moved = 4 * sum(rows) * width
    return pl.pallas_call(
        functools.partial(join_kernel, plan, len(arrays)),
        out_shape=[jax.ShapeDtypeStruct((r, width), BF) for r in rows],
        in_specs=[ANY] * len(arrays),
        out_specs=[ANY] * len(rows),
        scratch_shapes=[pltpu.SemaphoreType.DMA],
        compiler_params=params(),
        cost_estimate=cost(0, moved),
    )(*arrays)


def shift(v, far, by):
    pairs = []
    for x in range(4):
        for y in range(4):
            for c in range(2):
                along_x = (c == 0) == far
                tx, ty = ((x + by) % 4, y) if along_x else (x, (y + by) % 4)
                pairs.append(((x * 4 + y) * 2 + c, (tx * 4 + ty) * 2 + c))
    return lax.ppermute(v, ("x", "y", "c"), pairs)


def torus_gather(own, chain, first):
    count = own.shape[0]
    low, high = shift(own, False, 1), shift(own, False, -1)
    opposite = shift(low, False, 1)
    (line,) = join(
        [4 * count], [(n, 0, count, 0, n * count) for n in range(4)], own, low, high, opposite
    )
    line_low, line_high = shift(line, True, 1), shift(line, True, -1)
    far0, far1 = join(
        [2 * count] * 2, [(0, 0, 2 * count, 0, 0), (1, 2 * count, 2 * count, 1, 0)], line_low, line_high
    )
    far0, far1 = shift(far0, True, 1), shift(far1, True, -1)
    near = (0, 3, 1, 2)
    pieces = [(first + n, k * count, chain, far, near[k]) for n, far in enumerate((0, 3, 1)) for k in range(4)]
    pieces += [(first + 3 + k // 2, k % 2 * count, chain, 2, near[k]) for k in range(4)]
    return (line, line_low, line_high, far0, far1), pieces, (low, high, opposite)


def on_device(tokens_in, cotangent, routes, gate_weights, gate_proj, up_proj, down_proj):
    width = tokens_in.shape[1]
    hidden_width = gate_proj.shape[2]
    ix, iy, ic = lax.axis_index("x"), lax.axis_index("y"), lax.axis_index("c")
    zh, zq = lax.axis_index("zh"), lax.axis_index("zq")
    ring = zh * 2 + zq

    shard = pl.pallas_call(
        stack_kernel,
        out_shape=jax.ShapeDtypeStruct((3, *gate_proj.shape[1:]), BF),
        in_specs=[VM] * 3,
        out_specs=VM,
    )(gate_proj, up_proj, down_proj)
    other = lax.ppermute(shard, ("c", "zq"), [(2, 0), (1, 3)])
    smem = pl.BlockSpec(memory_space=pltpu.SMEM)

    def small(kernel, flag, arrays, rows):
        return pl.pallas_call(
            kernel,
            out_shape=[jax.ShapeDtypeStruct((r, hidden_width), BF) for r in rows],
            in_specs=[smem] + [VM] * len(arrays),
            out_specs=[VM] * len(rows),
            compiler_params=params(4),
        )(flag.astype(jnp.int32)[None], *arrays)

    (pair,) = small(pair_kernel, ic, (shard, other), (240,))

    def at(c, p):
        return (p // 2 * 2 + c) * 2 + p % 2

    def zmove(v, source, by):
        pairs = [(at(c, p), at(c, (p + by) % 4)) for c in range(2) for p in range(4) if (p % 2 == c) == source]
        return lax.ppermute(v, ("zh", "c", "zq"), pairs)

    source = ic == zq
    low, high = zmove(pair, True, 1), zmove(pair, True, -1)
    first, top = small(near_kernel, source, (pair, low), (240, SPLIT))
    far0, far1 = zmove(top, False, 1), zmove(high[SPLIT:], False, -1)
    (second,) = small(far_kernel, source, (far0, far1, high), (240,))
    first_half = jnp.where(source, zh, jnp.where((ring == 1) | (ring == 2), 0, 1))

    step = 512
    columns = pl.BlockSpec((256, step), lambda i: (0, i))
    payload, sel = pl.pallas_call(
        dispatch_kernel,
        grid=(width // step,),
        out_shape=(
            jax.ShapeDtypeStruct((8, 64, width), BF),
            jax.ShapeDtypeStruct((256, 256), BF),
        ),
        in_specs=[pl.BlockSpec((6, 256), lambda i: (0, 0)), columns, columns],
        out_specs=(
            pl.BlockSpec((8, 64, step), lambda i: (0, 0, i)),
            pl.BlockSpec((256, 256), lambda i: (0, 0)),
        ),
        compiler_params=params(56),
        cost_estimate=cost(2 * 256 * 512 * width, 8 * 256 * width),
    )(routes.T, tokens_in, cotangent)

    arrays, pieces, near = torus_gather(first, 0, 0)
    payload, *_ = lax.optimization_barrier((payload, far0, far1, *near[:2]))
    rows = lax.all_to_all(payload, ("c", "zr"), split_axis=0, concat_axis=0, tiled=True)
    second, *_ = lax.optimization_barrier((second, *near[:2]))
    more_arrays, more_pieces, _ = torus_gather(second, 1, len(arrays))
    arrays, pieces = arrays + more_arrays, pieces + more_pieces

    where = jnp.stack([ix, iy, ic, first_half, lax.axis_index("zr")]).astype(jnp.int32)
    back = pl.pallas_call(
        functools.partial(expert_kernel, pieces),
        out_shape=[jax.ShapeDtypeStruct((32, width + PAD), BF)] * 8,
        in_specs=[smem] + [ANY] * (1 + len(arrays)),
        out_specs=[ANY] * 8,
        scratch_shapes=[pltpu.VMEM((width, hidden_width), BF)] * 3
        + [pltpu.VMEM((8, 32, width), BF)] * 2
        + [pltpu.VMEM((8, 32, width + PAD), BF)]
        + [pltpu.VMEM((256, hidden_width), BF)] * 2
        + [pltpu.VMEM((256, hidden_width), F32)] * 4
        + [pltpu.SemaphoreType.DMA((5,)), pltpu.SemaphoreType.DMA((2,))],
        compiler_params=params(56),
        cost_estimate=cost(10 * 256 * width * hidden_width, 6 * width * hidden_width),
    )(where, rows, *arrays)

    home = {
        0: pl.pallas_call(
            copy_kernel,
            out_shape=jax.ShapeDtypeStruct((32, width + PAD), BF),
            in_specs=[VM],
            out_specs=VM,
            compiler_params=params(4),
            cost_estimate=cost(0, 4 * 32 * (width + PAD)),
        )(back[0])
    }
    for r in (4, 3, 7, 2, 6, 1, 5):
        pairs = [(d, (d // 4 ^ r // 4) * 4 + (d % 4 ^ r % 4)) for d in range(8)]
        home[r] = lax.ppermute(back[r], ("c", "zr"), pairs)
    home = [home[r] for r in range(8)]

    grad_tokens, grad_gates = pl.pallas_call(
        combine_kernel,
        out_shape=(
            jax.ShapeDtypeStruct(tokens_in.shape, BF),
            jax.ShapeDtypeStruct((6, 256), BF),
        ),
        in_specs=[smem] + [VM] * 11,
        out_specs=(VM, VM),
        compiler_params=params(),
        cost_estimate=cost(2 * 256 * 256 * width, 4 * 256 * width),
    )(where, routes.T, gate_weights.T, sel, *home)
    return grad_tokens, grad_gates.T


def solution(mesh):
    fine = Mesh(mesh.devices.reshape(4, 2, 4, 2, 2, 4), AXES)
    rows = P(AXES, None)
    proj = P(("zq", "zr"), ("x", "zh", "y", "c"), None)
    return jax.shard_map(
        on_device,
        mesh=fine,
        in_specs=(rows, rows, rows, rows, proj, proj, proj),
        out_specs=(rows, rows),
        check_vma=False,
    )
```

```python
import functools

import jax
import jax.numpy as jnp
from jax import lax
from jax.experimental import pallas as pl
from jax.experimental.pallas import tpu as pltpu
from jax.sharding import Mesh, PartitionSpec as P

BF = jnp.bfloat16
F32 = jnp.float32
AXES = ("x", "zh", "y", "c", "zq", "zr")
SPLIT = 128
PAD = 128


def slots_of(routes):
    tokens = routes.shape[1]
    window = routes < 8
    owner = jnp.sum(jnp.where(window, routes, 0), axis=0, keepdims=True)
    routed = jnp.sum(jnp.where(window, 1, 0), axis=0, keepdims=True) > 0
    expert = lax.broadcasted_iota(jnp.int32, (16, tokens), 0)
    onehot = jnp.where((expert == owner) & routed, 1.0, 0.0)
    row = lax.broadcasted_iota(jnp.int32, (tokens, tokens), 0)
    col = lax.broadcasted_iota(jnp.int32, (tokens, tokens), 1)
    upto = jnp.where(row <= col, 1.0, 0.0).astype(BF)
    rank = jnp.dot(onehot.astype(BF), upto, preferred_element_type=F32)
    slot = jnp.sum(rank * onehot, axis=0, keepdims=True).astype(jnp.int32) - 1
    return jnp.where(routed, owner * 32 + slot, -1)


def dispatch_kernel(routes_ref, tok_ref, cot_ref, out_ref, sel_ref):
    tokens, step = tok_ref.shape

    @pl.when(pl.program_id(0) == 0)
    def _():
        slot = lax.broadcasted_iota(jnp.int32, (256, tokens), 0)
        sel_ref[...] = jnp.where(slot == slots_of(routes_ref[...]), 1.0, 0.0).astype(BF)

    sel = sel_ref[...]
    for source, first in ((tok_ref, 0), (cot_ref, 32)):
        rows = jnp.dot(sel, source[...], preferred_element_type=F32).astype(BF)
        out_ref[:, first : first + 32, :] = rows.reshape(8, 32, step)


def copy_kernel(in_ref, out_ref):
    out_ref[...] = in_ref[...]


def combine_kernel(where_ref, routes_ref, gates_ref, sel_ref, *refs):
    back_refs, (grad_ref, score_ref) = refs[:8], refs[8:]
    width = grad_ref.shape[1]
    window = routes_ref[...] < 8
    gate = jnp.sum(jnp.where(window, gates_ref[...].astype(F32), 0.0), axis=0, keepdims=True)
    core, place = where_ref[2], where_ref[4]
    sel = jnp.concatenate(
        [
            sel_ref[pl.ds(pl.multiple_of(partner(core, place, r) * 32, 32), 32), :]
            for r in range(8)
        ],
        axis=0,
    )
    scaled = (sel.astype(F32) * gate).astype(BF)
    down = (((0,), (0,)), ((), ()))
    step = width // 2

    @pl.loop(0, width // step)
    def _(i):
        cols = pl.ds(pl.multiple_of(i * step, step), step)
        rows = jnp.concatenate([ref[:, cols] for ref in back_refs], axis=0)
        grad_ref[:, cols] = lax.dot_general(
            scaled, rows, down, preferred_element_type=F32
        ).astype(BF)

    tail = jnp.concatenate([ref[:, width : width + PAD] for ref in back_refs], axis=0)
    score = lax.dot_general(tail, sel, down, preferred_element_type=F32)[0:1]
    score_ref[...] = jnp.where(window, score, 0.0).astype(BF)


def stack_kernel(gate_ref, up_ref, down_ref, out_ref):
    for m, ref in enumerate((gate_ref, up_ref, down_ref)):
        out_ref[m] = ref[0]


def pair_kernel(first_ref, shard_ref, other_ref, out_ref):
    swap = first_ref[0] == 0
    for m in range(3):
        mine, theirs = shard_ref[m], other_ref[m]
        for k in range(2):
            row = 80 * m + 40 * k
            out_ref[row : row + 40] = jnp.where(swap == (k == 0), mine, theirs)


def near_kernel(source_ref, mine, low, out_ref, top_ref):
    top_ref[...] = low[: top_ref.shape[0]]
    out_ref[...] = jnp.where(source_ref[0] == 1, mine[...], low[...])


def far_kernel(source_ref, top, bottom, high, out_ref):
    source = source_ref[0] == 1
    cut = top.shape[0]
    out_ref[:cut] = jnp.where(source, top[...], high[:cut])
    out_ref[cut:] = jnp.where(source, bottom[...], high[cut:])


def partner(core, place, r):
    return jnp.bitwise_xor(core, r // 4) * 4 + jnp.bitwise_xor(place, r % 4)


def expert_kernel(pieces, where_ref, rows_ref, *refs):
    sources = refs[: pieces[-1][0] + 1]
    out_refs = refs[len(sources) : len(sources) + 8]
    gate_w, up_w, down_w, tok_v, cot_v, result, grad_a, grad_b, pre_g, pre_u, pre_b, sems, out_sems = refs[
        len(sources) + 8 :
    ]
    my_x, my_y, core, first_half, place = (where_ref[i] for i in range(5))
    width, hidden_width = gate_w.shape

    gate_copies, up_copies, down_copies = [], [], []
    for number, row, chain, far, near in pieces:
        xx = lax.rem(my_x + jnp.where(core == 0, far, near), 4)
        yy = lax.rem(my_y + jnp.where(core == 0, near, far), 4)
        half = first_half if chain == 0 else 1 - first_half
        target = pl.multiple_of(((xx * 2 + half) * 4 + yy) * 80, 16)
        for m, (weights, copies) in enumerate(
            ((gate_w, gate_copies), (up_w, up_copies), (down_w, down_copies))
        ):
            copies.append(
                pltpu.make_async_copy(
                    sources[number].at[pl.ds(row + 80 * m, 80), :],
                    weights.at[pl.ds(target, 80), :],
                    sems.at[m],
                )
            )
    down_copies.append(pltpu.make_async_copy(rows_ref.at[:, pl.ds(32, 32), :], cot_v, sems.at[3]))
    gate_copies.append(pltpu.make_async_copy(rows_ref.at[:, pl.ds(0, 32), :], tok_v, sems.at[4]))
    for copies in (down_copies, gate_copies, up_copies):
        for copy in copies:
            copy.start()

    for copy in down_copies:
        copy.wait()
    cot = cot_v[...].reshape(256, width)
    pre_b[...] = jnp.dot(cot, down_w[...], preferred_element_type=F32)
    for copy in gate_copies:
        copy.wait()
    tok = tok_v[...].reshape(256, width)
    pre_g[...] = jnp.dot(tok, gate_w[...], preferred_element_type=F32)
    for copy in up_copies:
        copy.wait()
    pre_u[...] = jnp.dot(tok, up_w[...], preferred_element_type=F32)

    cstep = 256

    def middle(i, score):
        cols = pl.ds(pl.multiple_of(i * cstep, cstep), cstep)
        gate, up, back_hidden = pre_g[:, cols], pre_u[:, cols], pre_b[:, cols]
        sig = jax.nn.sigmoid(gate)
        act = gate * sig
        hidden = (act * up).astype(BF).astype(F32)
        grad_a[:, cols] = (back_hidden * up * (sig * (1.0 + gate * (1.0 - sig)))).astype(BF)
        grad_b[:, cols] = (back_hidden * act).astype(BF)
        return score + jnp.sum(hidden * back_hidden, axis=1, keepdims=True)

    score = lax.fori_loop(0, hidden_width // cstep, middle, jnp.zeros((256, 1), F32))
    result[:, :, width : width + PAD] = (
        jnp.broadcast_to(score, (256, PAD)).astype(BF).reshape(8, 32, PAD)
    )

    a, b = grad_a[...], grad_b[...]
    dims = (((1,), (1,)), ((), ()))
    dstep = width // 2
    outs = []
    for i in range(2):
        rows = lax.dot_general(a, gate_w[i * dstep : (i + 1) * dstep, :], dims, preferred_element_type=F32)
        rows = rows + lax.dot_general(b, up_w[i * dstep : (i + 1) * dstep, :], dims, preferred_element_type=F32)
        result[:, :, i * dstep : (i + 1) * dstep] = rows.astype(BF).reshape(8, 32, dstep)
        part = pl.ds(i * dstep, dstep if i == 0 else dstep + PAD)
        for r, out_ref in enumerate(out_refs):
            copy = pltpu.make_async_copy(
                result.at[partner(core, place, r), :, part], out_ref.at[:, part], out_sems.at[i]
            )
            copy.start()
            outs.append(copy)
    for copy in outs:
        copy.wait()


def params(mib=16):
    return pltpu.CompilerParams(vmem_limit_bytes=mib * 1024 * 1024)


def cost(flops, moved):
    return pl.CostEstimate(flops=flops, bytes_accessed=moved, transcendentals=0)


VM = pl.BlockSpec(memory_space=pltpu.VMEM)
ANY = pl.BlockSpec(memory_space=pl.ANY)


def join_kernel(plan, inputs, *refs):
    sources, targets, sem = refs[:inputs], refs[inputs:-1], refs[-1]
    copies = [
        pltpu.make_async_copy(
            sources[i].at[pl.ds(row, count), :], targets[o].at[pl.ds(at, count), :], sem
        )
        for i, row, count, o, at in plan
    ]
    for copy in copies:
        copy.start()
    for copy in copies:
        copy.wait()


def join(rows, plan, *arrays):
    width = arrays[0].shape[1]
    moved = 4 * sum(rows) * width
    return pl.pallas_call(
        functools.partial(join_kernel, plan, len(arrays)),
        out_shape=[jax.ShapeDtypeStruct((r, width), BF) for r in rows],
        in_specs=[ANY] * len(arrays),
        out_specs=[ANY] * len(rows),
        scratch_shapes=[pltpu.SemaphoreType.DMA],
        compiler_params=params(),
        cost_estimate=cost(0, moved),
    )(*arrays)


def shift(v, far, by):
    pairs = []
    for x in range(4):
        for y in range(4):
            for c in range(2):
                along_x = (c == 0) == far
                tx, ty = ((x + by) % 4, y) if along_x else (x, (y + by) % 4)
                pairs.append(((x * 4 + y) * 2 + c, (tx * 4 + ty) * 2 + c))
    return lax.ppermute(v, ("x", "y", "c"), pairs)


def torus_gather(own, chain, first):
    count = own.shape[0]
    low, high = shift(own, False, 1), shift(own, False, -1)
    opposite = shift(low, False, 1)
    (line,) = join(
        [4 * count], [(n, 0, count, 0, n * count) for n in range(4)], own, low, high, opposite
    )
    line_low, line_high = shift(line, True, 1), shift(line, True, -1)
    far0, far1 = join(
        [2 * count] * 2, [(0, 0, 2 * count, 0, 0), (1, 2 * count, 2 * count, 1, 0)], line_low, line_high
    )
    far0, far1 = shift(far0, True, 1), shift(far1, True, -1)
    near = (0, 3, 1, 2)
    pieces = [(first + n, k * count, chain, far, near[k]) for n, far in enumerate((0, 3, 1)) for k in range(4)]
    pieces += [(first + 3 + k // 2, k % 2 * count, chain, 2, near[k]) for k in range(4)]
    return (line, line_low, line_high, far0, far1), pieces, (low, high, opposite)


def on_device(tokens_in, cotangent, routes, gate_weights, gate_proj, up_proj, down_proj):
    width = tokens_in.shape[1]
    hidden_width = gate_proj.shape[2]
    ix, iy, ic = lax.axis_index("x"), lax.axis_index("y"), lax.axis_index("c")
    zh, zq = lax.axis_index("zh"), lax.axis_index("zq")
    ring = zh * 2 + zq

    shard = pl.pallas_call(
        stack_kernel,
        out_shape=jax.ShapeDtypeStruct((3, *gate_proj.shape[1:]), BF),
        in_specs=[VM] * 3,
        out_specs=VM,
    )(gate_proj, up_proj, down_proj)
    other = lax.ppermute(shard, ("c", "zq"), [(2, 0), (1, 3)])
    smem = pl.BlockSpec(memory_space=pltpu.SMEM)

    def small(kernel, flag, arrays, rows):
        return pl.pallas_call(
            kernel,
            out_shape=[jax.ShapeDtypeStruct((r, hidden_width), BF) for r in rows],
            in_specs=[smem] + [VM] * len(arrays),
            out_specs=[VM] * len(rows),
            compiler_params=params(4),
        )(flag.astype(jnp.int32)[None], *arrays)

    (pair,) = small(pair_kernel, ic, (shard, other), (240,))

    def at(c, p):
        return (p // 2 * 2 + c) * 2 + p % 2

    def zmove(v, source, by):
        pairs = [(at(c, p), at(c, (p + by) % 4)) for c in range(2) for p in range(4) if (p % 2 == c) == source]
        return lax.ppermute(v, ("zh", "c", "zq"), pairs)

    source = ic == zq
    low, high = zmove(pair, True, 1), zmove(pair, True, -1)
    first, top = small(near_kernel, source, (pair, low), (240, SPLIT))
    far0, far1 = zmove(top, False, 1), zmove(high[SPLIT:], False, -1)
    (second,) = small(far_kernel, source, (far0, far1, high), (240,))
    first_half = jnp.where(source, zh, jnp.where((ring == 1) | (ring == 2), 0, 1))

    step = 512
    columns = pl.BlockSpec((256, step), lambda i: (0, i))
    payload, sel = pl.pallas_call(
        dispatch_kernel,
        grid=(width // step,),
        out_shape=(
            jax.ShapeDtypeStruct((8, 64, width), BF),
            jax.ShapeDtypeStruct((256, 256), BF),
        ),
        in_specs=[pl.BlockSpec((6, 256), lambda i: (0, 0)), columns, columns],
        out_specs=(
            pl.BlockSpec((8, 64, step), lambda i: (0, 0, i)),
            pl.BlockSpec((256, 256), lambda i: (0, 0)),
        ),
        compiler_params=params(56),
        cost_estimate=cost(2 * 256 * 512 * width, 8 * 256 * width),
    )(routes.T, tokens_in, cotangent)

    arrays, pieces, near = torus_gather(first, 0, 0)
    payload, *_ = lax.optimization_barrier((payload, far0, far1, *near[:2]))
    rows = lax.all_to_all(payload, ("c", "zr"), split_axis=0, concat_axis=0, tiled=True)
    second, *_ = lax.optimization_barrier((second, *near[:2]))
    more_arrays, more_pieces, _ = torus_gather(second, 1, len(arrays))
    arrays, pieces = arrays + more_arrays, pieces + more_pieces

    where = jnp.stack([ix, iy, ic, first_half, lax.axis_index("zr")]).astype(jnp.int32)
    back = pl.pallas_call(
        functools.partial(expert_kernel, pieces),
        out_shape=[jax.ShapeDtypeStruct((32, width + PAD), BF)] * 8,
        in_specs=[smem] + [ANY] * (1 + len(arrays)),
        out_specs=[ANY] * 8,
        scratch_shapes=[pltpu.VMEM((width, hidden_width), BF)] * 3
        + [pltpu.VMEM((8, 32, width), BF)] * 2
        + [pltpu.VMEM((8, 32, width + PAD), BF)]
        + [pltpu.VMEM((256, hidden_width), BF)] * 2
        + [pltpu.VMEM((256, hidden_width), F32)] * 3
        + [pltpu.SemaphoreType.DMA((5,)), pltpu.SemaphoreType.DMA((2,))],
        compiler_params=params(56),
        cost_estimate=cost(10 * 256 * width * hidden_width, 6 * width * hidden_width),
    )(where, rows, *arrays)

    home = {
        0: pl.pallas_call(
            copy_kernel,
            out_shape=jax.ShapeDtypeStruct((32, width + PAD), BF),
            in_specs=[VM],
            out_specs=VM,
            compiler_params=params(4),
            cost_estimate=cost(0, 4 * 32 * (width + PAD)),
        )(back[0])
    }
    for r in (4, 3, 7, 2, 6, 1, 5):
        pairs = [(d, (d // 4 ^ r // 4) * 4 + (d % 4 ^ r % 4)) for d in range(8)]
        home[r] = lax.ppermute(back[r], ("c", "zr"), pairs)
    home = [home[r] for r in range(8)]

    grad_tokens, grad_gates = pl.pallas_call(
        combine_kernel,
        out_shape=(
            jax.ShapeDtypeStruct(tokens_in.shape, BF),
            jax.ShapeDtypeStruct((6, 256), BF),
        ),
        in_specs=[smem] + [VM] * 11,
        out_specs=(VM, VM),
        compiler_params=params(),
        cost_estimate=cost(2 * 256 * 256 * width, 4 * 256 * width),
    )(where, routes.T, gate_weights.T, sel, *home)
    return grad_tokens, grad_gates.T


def solution(mesh):
    fine = Mesh(mesh.devices.reshape(4, 2, 4, 2, 2, 4), AXES)
    rows = P(AXES, None)
    proj = P(("zq", "zr"), ("x", "zh", "y", "c"), None)
    return jax.shard_map(
        on_device,
        mesh=fine,
        in_specs=(rows, rows, rows, rows, proj, proj, proj),
        out_specs=(rows, rows),
        check_vma=False,
    )
```
